32 devices in a mesh: groups: 2 (over y), blk: 4 (over x, core), ulysses: 4 (over z).
Axes of the slice: x: 2, y: 2, z: 4, core: 2. Of those that a mesh axis runs over, the one named last changes fastest.
Arguments:
- query_proj: bfloat16 [1024, 1024], P(('groups', 'blk', 'ulysses')), parts along dimension 0, may hold values from -200 to 200
- key_proj: bfloat16 [1024, 1024], P(('groups', 'blk', 'ulysses')), parts along dimension 0, may hold values from -200 to 200
- value_proj: bfloat16 [1024, 1024], P(('groups', 'blk', 'ulysses')), parts along dimension 0, may hold values from -6 to 6
- query_gain: float32 [1024], replicated, may hold values from 1.2 to 2.4
- key_gain: float32 [1024], replicated, may hold values from 1.2 to 2.4
- control: bfloat16 [1024, 384], P(('groups', 'blk', 'ulysses')), parts along dimension 0, may hold values from -6 to 6
- hint_weight: bfloat16 [384, 1024], replicated, may hold values from -0.3125 to 0.3125
- hint_gain: float32 [8, 1024], replicated, may hold values from 0.3 to 3
- owner_map: int32 [32, 4], P(('groups', 'blk', 'ulysses')), parts along dimension 0, may hold values from 0 to 3, each once within a row
- layer_index: int32 [32], P(('groups', 'blk', 'ulysses')), parts along dimension 0, may hold values from 0 to 7
Outputs:
- block_out: bfloat16 [1024, 1024], P(('groups', 'blk', 'ulysses')), parts along dimension 0
The draws below stay inside these ranges and needn't reach their ends.
There are 2 independent parts, one for each index of `groups`. The reference program is written for one: setup_inputs(seed, part) draws one part's arguments, and reference() takes and returns one part's arrays. A program takes and returns all parts, laid end to end along the dimension named above; an argument that names none is the same for every part. Nothing has to cross between parts.
Inputs may be any that keep to these rules, and one draw needn't show every extreme that they name: `owner_map`: each row is a permutation of 0 to 3.
All inputs are finite; a program needn't handle non-finite values.
Results may differ from the reference program's by a relative error of at most 0.008.
Values may be sent and summed in bfloat16 or wider, within the bound.
No kernel may reach another device: no remote copies, remote signals or barrier semaphores. Data moves between devices by JAX's collectives and lax.ppermute only.
A program may use at most 64 MiB of HBM per device.

```python
import math
import jax
import jax.numpy as jnp
from jax import lax

HEAD_DIM = 128
HEADS = 8
FEATS = 1024
CTRL_IN = 384
CTRL_LAYERS = 8
TOK_DEV = 32
SLAB = 8
TOKENS = 512
N_BLK = 4
N_ULYSSES = 4


def paired_draw(key):
    base_q = jax.random.fold_in(key, 11)
    base_k = jax.random.fold_in(key, 12)
    column_key = jax.random.fold_in(key, 13)
    columns = jnp.exp(jax.random.uniform(column_key, (FEATS,), jnp.float32, 0.0, 2.302585))
    query_rows = jax.random.truncated_normal(base_q, -4.0, 4.0, (TOKENS, FEATS), jnp.float32) * columns
    key_rows = jax.random.truncated_normal(base_k, -4.0, 4.0, (TOKENS, FEATS), jnp.float32) * columns
    query_rows = jnp.clip(query_rows, -200.0, 200.0)
    key_rows = jnp.clip(key_rows, -200.0, 200.0)
    return (query_rows, key_rows)


def draw_query_proj(key, part):
    return paired_draw(key)[0].astype(jnp.bfloat16)


def draw_key_proj(key, part):
    return paired_draw(key)[1].astype(jnp.bfloat16)


def set_ends(entries, key, smallest, high):
    shape = entries.shape
    place = [jax.random.randint(jax.random.fold_in(key, axis), (), 0, shape[axis]) for axis in range(len(shape))]
    entries = entries.at[tuple(place)].set(smallest)
    longest = shape.index(max(shape))
    place[longest] = (place[longest] + 1) % shape[longest]
    return entries.at[tuple(place)].set(high)


def block_levels(key, extent, cuts, low, top_value):
    level = 1.0
    for axis_at, blocks in cuts:
        steps = jax.random.uniform(jax.random.fold_in(jax.random.fold_in(key, 6), axis_at), (blocks,), jnp.float32, low / len(cuts), top_value / len(cuts))
        level = level * jnp.repeat(jnp.exp(steps), extent[axis_at] // blocks).reshape((-1,) + (1,) * (len(extent) - 1 - axis_at))
    return level


def normal_values(own_key, dims, deviation, most, shards=(), held_as=jnp.bfloat16):
    level = block_levels(own_key, dims, shards, -0.22, 0.18) if shards else 1.0
    values = jax.random.normal(own_key, dims, jnp.float32) * deviation * level
    return jnp.minimum(jnp.maximum(values, -most), most).astype(held_as)


def setup_inputs(seed: int = 0, part: int = 0) -> dict:
    key_list = jax.random.split(jax.random.key(seed), 11)
    own_keys = jax.random.split(jax.random.fold_in(key_list[10], part), 11)
    query_proj = draw_query_proj(jax.random.fold_in(jax.random.fold_in(key_list[10], part), 71), part)
    key_proj = draw_key_proj(jax.random.fold_in(jax.random.fold_in(key_list[10], part), 71), part)
    value_proj = normal_values(own_keys[2], (TOKENS, FEATS), 1.0, 6.0, ((0, 16),))
    query_gain = jnp.clip(jax.random.uniform(key_list[3], (FEATS,), jnp.float32, 1.2, 2.4), 1.2, 2.4)
    key_gain = jnp.clip(jax.random.uniform(key_list[4], (FEATS,), jnp.float32, 1.2, 2.4), 1.2, 2.4)
    control = normal_values(own_keys[5], (TOKENS, CTRL_IN), 1.0, 6.0, ((0, 16),))
    hint_weight = normal_values(key_list[6], (CTRL_IN, FEATS), CTRL_IN ** -0.5, 0.3125)
    hint_gain = jnp.clip(jnp.exp(jax.random.uniform(key_list[7], (CTRL_LAYERS, FEATS), jnp.float32, math.log(0.3), math.log(3.0))), 0.3, 3.0)
    owner_map = jax.vmap(lambda own: jax.random.permutation(own, N_ULYSSES))(jax.random.split(own_keys[8], (N_BLK * N_ULYSSES))).reshape((N_BLK * N_ULYSSES, N_ULYSSES)).astype(jnp.int32)
    layer_index = set_ends(jax.random.randint(own_keys[9], (N_BLK * N_ULYSSES,), 0, CTRL_LAYERS), jax.random.fold_in(own_keys[9], 1), 0, CTRL_LAYERS - 1).astype(jnp.int32)
    return dict(query_proj=query_proj, key_proj=key_proj, value_proj=value_proj, query_gain=query_gain, key_gain=key_gain, control=control, hint_weight=hint_weight, hint_gain=hint_gain, owner_map=owner_map, layer_index=layer_index)


def normalize_rows(rows, gain):
    values = rows.astype(jnp.float32)
    scale = lax.rsqrt(lax.optimization_barrier(jnp.mean(values * values, axis=-1, keepdims=True)) + 1e-06)
    return (values * scale * gain).astype(jnp.bfloat16)

def query_block_size(count):
    block = min(count, 1024)
    while count % block:
        block = block - 1
    return block

def one_head(triple):
    queries, keys, values = triple
    count = queries.shape[0]
    block = query_block_size(count)
    shaped = queries.reshape(count // block, block, HEAD_DIM)

    def per_block(query_rows):
        scores = jnp.dot(query_rows, keys.T, preferred_element_type=jnp.float32) * HEAD_DIM ** (-0.5)
        peak = lax.optimization_barrier(jnp.max(scores, axis=-1, keepdims=True))
        expo = jnp.exp(scores - peak)
        totals = lax.optimization_barrier(jnp.sum(expo, axis=-1, keepdims=True))
        probs = expo.astype(jnp.bfloat16)
        mixed = jnp.dot(probs, values, preferred_element_type=jnp.float32)
        return (mixed / totals).astype(jnp.bfloat16)
    return lax.map(per_block, shaped).reshape(count, HEAD_DIM)

def reference(query_proj, key_proj, value_proj, query_gain, key_gain, control, hint_weight, hint_gain, owner_map, layer_index):
    count = query_proj.shape[0]
    query_normed = normalize_rows(query_proj, query_gain)
    key_normed = normalize_rows(key_proj, key_gain)
    split_q = query_normed.reshape(count, HEADS, HEAD_DIM).transpose(1, 0, 2)
    split_k = key_normed.reshape(count, HEADS, HEAD_DIM).transpose(1, 0, 2)
    split_v = value_proj.reshape(count, HEADS, HEAD_DIM).transpose(1, 0, 2)
    attended = lax.map(one_head, (split_q, split_k, split_v))
    attended = attended.transpose(1, 0, 2).reshape(count, FEATS)
    control_normed = normalize_rows(control, jnp.float32(1.0))
    hint = jnp.dot(control_normed, hint_weight, preferred_element_type=jnp.float32).astype(jnp.bfloat16)
    slabs = hint.reshape(N_BLK, N_ULYSSES, N_ULYSSES, SLAB, FEATS)
    owners = owner_map.reshape(N_BLK, N_ULYSSES, N_ULYSSES)
    positions = jnp.arange(N_ULYSSES, dtype=jnp.int32)
    match = (owners[:, :, :, None] == positions[None, None, None, :]).astype(jnp.int32)
    inverse = lax.optimization_barrier(jnp.sum(positions[None, None, :, None] * match, axis=2)).astype(jnp.int32)
    picked = jnp.take_along_axis(slabs, inverse[:, :, :, None, None], axis=2)
    placed = picked.transpose(0, 2, 1, 3, 4).reshape(N_BLK * N_ULYSSES, TOK_DEV, FEATS)
    gains = jnp.take(hint_gain, layer_index.astype(jnp.int32), axis=0)
    scaled = (placed.astype(jnp.float32) * gains[:, None, :]).reshape(count, FEATS)
    return (attended.astype(jnp.float32) + scaled).astype(jnp.bfloat16)
```

```python
import functools

import jax
import jax.numpy as jnp
from jax import lax
from jax.experimental import pallas as pl
from jax.experimental.pallas import tpu as pltpu
from jax.sharding import PartitionSpec as P

HEAD_DIM = 128
EPS = 1e-06
VIDEO = ("ulysses", "blk")


def normed(rows, gain):
    values = rows.astype(jnp.float32)
    scale = lax.rsqrt(jnp.mean(values * values, axis=-1, keepdims=True) + EPS)
    return values * scale * gain


def pack_kernel(splits, q_ref, k_ref, v_ref, qg_ref, kg_ref, send_ref):
    rows, feats = q_ref.shape
    heads = feats // HEAD_DIM
    part = rows // splits
    queries = normed(q_ref[...], qg_ref[...]).astype(jnp.bfloat16)
    keys = normed(k_ref[...], kg_ref[...]).astype(jnp.bfloat16)
    values = v_ref[...]
    for head in range(heads):
        cols = slice(head * HEAD_DIM, (head + 1) * HEAD_DIM)
        for piece in range(splits):
            to = head * splits + piece
            send_ref[to, :part] = queries[piece * part : (piece + 1) * part, cols]
            send_ref[to, part : part + rows] = keys[:, cols]
            send_ref[to, part + rows :] = values[:, cols]


def slab_kernel(me_ref, owner_ref, control_ref, *out_refs):
    owners = len(out_refs)
    slab_rows = out_refs[0].shape[0]
    values = control_ref[...].astype(jnp.float32)
    slabs = [values[j * slab_rows : (j + 1) * slab_rows] for j in range(owners)]
    for shift, out_ref in enumerate(out_refs):
        owner = lax.rem(me_ref[0] + shift, owners)
        picked = slabs[0]
        for j in range(1, owners):
            picked = jnp.where(owner_ref[0, j] == owner, slabs[j], picked)
        out_ref[...] = picked.astype(jnp.bfloat16)


def attend_kernel(part, rows, got_ref, out_ref):
    count = got_ref.shape[0]
    keys = got_ref[:, part : part + rows].reshape(count * rows, HEAD_DIM)
    values = got_ref[:, part + rows :].reshape(count * rows, HEAD_DIM)
    block = max(1, min(count, 2**18 // (count * rows * part)))

    def attend(sources):
        queries = got_ref[sources, :part].reshape(block * part, HEAD_DIM)
        scores = lax.dot_general(
            queries, keys, (((1,), (1,)), ((), ())), preferred_element_type=jnp.float32
        ) * (HEAD_DIM ** (-0.5))
        peak = jnp.max(scores, axis=-1, keepdims=True)
        expo = jnp.exp(scores - peak)
        totals = jnp.sum(expo, axis=-1, keepdims=True)
        mixed = jnp.dot(expo.astype(jnp.bfloat16), values, preferred_element_type=jnp.float32)
        mixed = (mixed / totals).astype(jnp.bfloat16)
        out_ref[sources] = mixed.reshape(block, part, HEAD_DIM)

    if block == count:
        attend(slice(None))
    else:
        pl.loop(0, count // block)(lambda i: attend(pl.ds(i * block, block)))


def hint_kernel(me_ref, layer_ref, weight_ref, gain_ref, *refs):
    arrived, out_ref = refs[:-1], refs[-1]
    owners = len(arrived)
    slab_rows = arrived[0].shape[0]
    patches = jnp.concatenate([ref[...].astype(jnp.float32) for ref in arrived], axis=0)
    rows = normed(patches, 1.0).astype(jnp.bfloat16)
    hint = jnp.dot(rows, weight_ref[...], preferred_element_type=jnp.float32)
    hint = hint.astype(jnp.bfloat16).astype(jnp.float32) * gain_ref[pl.ds(layer_ref[0], 1), :]
    for shift in range(owners):
        source = lax.rem(me_ref[0] + owners - shift, owners)
        out_ref[source] = hint[shift * slab_rows : (shift + 1) * slab_rows]


def finish_kernel(splits, back_ref, hint_ref, out_ref):
    rows = out_ref.shape[0]
    part = rows // splits
    for to in range(back_ref.shape[0]):
        head, piece = divmod(to, splits)
        at = slice(piece * part, (piece + 1) * part)
        cols = slice(head * HEAD_DIM, (head + 1) * HEAD_DIM)
        out_ref[at, cols] = (back_ref[to].astype(jnp.float32) + hint_ref[at, cols]).astype(
            jnp.bfloat16
        )


VMEM = pl.BlockSpec(memory_space=pltpu.VMEM)
SMEM = pl.BlockSpec(memory_space=pltpu.SMEM)


def call(kernel, out_shape, specs, *operands, flops=0, nbytes=0):
    return pl.pallas_call(
        kernel,
        out_shape=out_shape,
        in_specs=specs,
        out_specs=jax.tree.map(lambda _: VMEM, out_shape),
        compiler_params=pltpu.CompilerParams(vmem_limit_bytes=32 * 2**20),
        cost_estimate=pl.CostEstimate(flops=flops, bytes_accessed=nbytes, transcendentals=0),
    )(*operands)


def shape(dims, dtype=jnp.bfloat16):
    return jax.ShapeDtypeStruct(dims, dtype)


def ring(owners, shift):
    return [(i, (i + shift) % owners) for i in range(owners)]


def shards(
    query_proj,
    key_proj,
    value_proj,
    query_gain,
    key_gain,
    control,
    hint_weight,
    hint_gain,
    owner_map,
    layer_index,
):
    owners = lax.axis_size("ulysses")
    count = owners * lax.axis_size("blk")
    rows, feats = query_proj.shape
    heads = feats // HEAD_DIM
    splits = count // heads
    part = rows // splits
    width = control.shape[1]
    me = lax.axis_index("ulysses").astype(jnp.int32).reshape(1)
    send = call(
        functools.partial(pack_kernel, splits),
        shape((count, part + 2 * rows, HEAD_DIM)),
        [VMEM] * 5,
        query_proj,
        key_proj,
        value_proj,
        query_gain.reshape(1, feats),
        key_gain.reshape(1, feats),
    )
    slabs = call(
        slab_kernel,
        [shape((rows // owners, width))] * owners,
        [SMEM, SMEM, VMEM],
        me,
        owner_map,
        control,
    )
    got = lax.all_to_all(send, VIDEO, split_axis=0, concat_axis=0, tiled=True)
    arrived = [slabs[0]] + [
        lax.ppermute(slabs[shift], "ulysses", ring(owners, shift)) for shift in range(1, owners)
    ]
    hint = call(
        hint_kernel,
        shape((owners, rows // owners, feats), jnp.float32),
        [SMEM, SMEM] + [VMEM] * (owners + 2),
        me,
        layer_index,
        hint_weight,
        hint_gain,
        *arrived,
        flops=2 * rows * width * feats,
        nbytes=2 * width * feats,
    )
    mixed = call(
        functools.partial(attend_kernel, part, rows),
        shape((count, part, HEAD_DIM)),
        [VMEM],
        got,
        flops=4 * count * part * count * rows * HEAD_DIM,
        nbytes=2 * got.size,
    )
    back = lax.all_to_all(mixed, VIDEO, split_axis=0, concat_axis=0, tiled=True)
    return call(
        functools.partial(finish_kernel, splits),
        shape((rows, feats)),
        [VMEM, VMEM],
        back,
        hint.reshape(rows, feats),
    )


def solution(mesh):
    split = P(("groups", "blk", "ulysses"), None)
    return jax.shard_map(
        shards,
        mesh=mesh,
        in_specs=(
            split,
            split,
            split,
            P(),
            P(),
            split,
            P(),
            P(),
            split,
            P(("groups", "blk", "ulysses")),
        ),
        out_specs=split,
        check_vma=False,
    )
```

```python
import functools

import jax
import jax.numpy as jnp
from jax import lax
from jax.experimental import pallas as pl
from jax.experimental.pallas import tpu as pltpu
from jax.sharding import PartitionSpec as P

HEAD_DIM = 128
EPS = 1e-06
VIDEO = ("ulysses", "blk")


def normed(rows, gain):
    values = rows.astype(jnp.float32)
    scale = lax.rsqrt(jnp.mean(values * values, axis=-1, keepdims=True) + EPS)
    return values * scale * gain


def pack_kernel(splits, *refs):
    sources, send_ref, held, copy_sems = refs[:5], refs[5], refs[6:11], refs[11]
    copies = [
        pltpu.make_async_copy(source, buffer, copy_sems.at[i])
        for i, (source, buffer) in enumerate(zip(sources, held))
    ]
    for copy in copies:
        copy.start()
    q_ref, k_ref, v_ref, qg_ref, kg_ref = held
    rows, feats = q_ref.shape
    part = rows // splits
    for copy in copies:
        copy.wait()
    packed = (
        normed(q_ref[...], qg_ref[...]).astype(jnp.bfloat16),
        normed(k_ref[...], kg_ref[...]).astype(jnp.bfloat16),
        v_ref[...],
    )
    for head in range(feats // HEAD_DIM):
        cols = slice(head * HEAD_DIM, (head + 1) * HEAD_DIM)
        for piece in range(splits):
            for i, array in enumerate(packed):
                send_ref[head * splits + piece, i * part : (i + 1) * part] = array[
                    piece * part : (piece + 1) * part, cols
                ]


def attend_kernel(*refs):
    got_refs, out_ref = refs[:-1], refs[-1]
    count, part, _ = out_ref.shape
    keys = [ref[:, part : 2 * part].reshape(count * part, HEAD_DIM) for ref in got_refs]
    values = [ref[:, 2 * part :].reshape(count * part, HEAD_DIM) for ref in got_refs]
    keys, values = jnp.concatenate(keys, axis=0), jnp.concatenate(values, axis=0)
    block = max(1, min(count, 2**18 // (part * keys.shape[0])))

    def attend(sources):
        queries = got_refs[0][sources, :part].reshape(block * part, HEAD_DIM)
        scores = lax.dot_general(
            queries, keys, (((1,), (1,)), ((), ())), preferred_element_type=jnp.float32
        ) * (HEAD_DIM ** (-0.5))
        peak = jnp.max(scores, axis=-1, keepdims=True)
        expo = jnp.exp(scores - peak)
        totals = jnp.sum(expo, axis=-1, keepdims=True)
        mixed = jnp.dot(expo.astype(jnp.bfloat16), values, preferred_element_type=jnp.float32)
        mixed = (mixed / totals).astype(jnp.bfloat16)
        out_ref[sources] = mixed.reshape(block, part, HEAD_DIM)

    if block == count:
        attend(slice(None))
    else:
        pl.loop(0, count // block)(lambda i: attend(pl.ds(i * block, block)))


def finish_kernel(splits, me_ref, layer_ref, owner_ref, got_ref, weight_ref, gain_ref, back_ref, out_ref):
    owners = got_ref.shape[0]
    slabs = []
    for source in range(owners):
        slab = jnp.int32(0)
        for j in range(1, owners):
            slab = jnp.where(owner_ref[source, j] == me_ref[0], j, slab)
        slabs.append(got_ref[source, slab].astype(jnp.float32))
    patches = normed(jnp.concatenate(slabs, axis=0), 1.0).astype(jnp.bfloat16)
    hint = jnp.dot(patches, weight_ref[...], preferred_element_type=jnp.float32)
    hint = hint.astype(jnp.bfloat16).astype(jnp.float32) * gain_ref[pl.ds(layer_ref[0], 1), :]
    part = out_ref.shape[0] // splits
    for to in range(back_ref.shape[0]):
        head, piece = divmod(to, splits)
        at = slice(piece * part, (piece + 1) * part)
        cols = slice(head * HEAD_DIM, (head + 1) * HEAD_DIM)
        out_ref[at, cols] = (back_ref[to].astype(jnp.float32) + hint[at, cols]).astype(
            jnp.bfloat16
        )


VMEM = pl.BlockSpec(memory_space=pltpu.VMEM)
SMEM = pl.BlockSpec(memory_space=pltpu.SMEM)
HBM = pl.BlockSpec(memory_space=pltpu.HBM)


def call(kernel, out_shape, specs, *operands, scratch=(), flops=0, nbytes=0):
    return pl.pallas_call(
        kernel,
        out_shape=out_shape,
        in_specs=specs,
        out_specs=jax.tree.map(lambda _: VMEM, out_shape),
        scratch_shapes=scratch,
        compiler_params=pltpu.CompilerParams(vmem_limit_bytes=32 * 2**20),
        cost_estimate=pl.CostEstimate(flops=flops, bytes_accessed=nbytes, transcendentals=0),
    )(*operands)


def shape(dims, dtype=jnp.bfloat16):
    return jax.ShapeDtypeStruct(dims, dtype)


def team_ring(size, splits, shift):
    return [(i, i - i % splits + (i + shift) % splits) for i in range(size)]


def shards(
    query_proj,
    key_proj,
    value_proj,
    query_gain,
    key_gain,
    control,
    hint_weight,
    hint_gain,
    owner_map,
    layer_index,
):
    owners, blocks = lax.axis_size("ulysses"), lax.axis_size("blk")
    count = owners * blocks
    rows, feats = query_proj.shape
    splits = count // (feats // HEAD_DIM)
    part = rows // splits
    width = control.shape[1]
    me = lax.axis_index("ulysses").astype(jnp.int32).reshape(1)
    arrived = lax.all_gather(control, "ulysses", axis=0)
    owner_rows = lax.all_gather(owner_map[0], "ulysses", axis=0)
    sources = (
        query_proj,
        key_proj,
        value_proj,
        query_gain.reshape(1, feats),
        key_gain.reshape(1, feats),
    )
    sources = [pltpu.with_memory_space_constraint(source, pltpu.HBM) for source in sources]
    send = call(
        functools.partial(pack_kernel, splits),
        shape((count, 3 * part, HEAD_DIM)),
        [HBM] * len(sources),
        *sources,
        scratch=[pltpu.VMEM(source.shape, source.dtype) for source in sources]
        + [pltpu.SemaphoreType.DMA((len(sources),))],
    )
    got = lax.all_to_all(send, VIDEO, split_axis=0, concat_axis=0, tiled=True)
    team = [got] + [
        lax.ppermute(got, "blk", team_ring(blocks, splits, shift)) for shift in range(1, splits)
    ]
    mixed = call(
        attend_kernel,
        shape((count, part, HEAD_DIM)),
        [VMEM] * splits,
        *team,
        flops=4 * count * part * count * rows * HEAD_DIM,
        nbytes=6 * count * rows * HEAD_DIM,
    )
    back = lax.all_to_all(mixed, VIDEO, split_axis=0, concat_axis=0, tiled=True)
    return call(
        functools.partial(finish_kernel, splits),
        shape((rows, feats)),
        [SMEM] * 3 + [VMEM] * 4,
        me,
        layer_index,
        owner_rows,
        arrived.reshape(owners, owners, rows // owners, width),
        hint_weight,
        hint_gain,
        back,
        flops=2 * rows * width * feats,
        nbytes=2 * width * feats,
    )


def solution(mesh):
    split = P(("groups", "blk", "ulysses"), None)
    return jax.shard_map(
        shards,
        mesh=mesh,
        in_specs=(
            split,
            split,
            split,
            P(),
            P(),
            split,
            P(),
            P(),
            split,
            P(("groups", "blk", "ulysses")),
        ),
        out_specs=split,
        check_vma=False,
    )
```

```python
import functools

import jax
import jax.numpy as jnp
from jax import lax
from jax.experimental import pallas as pl
from jax.experimental.pallas import tpu as pltpu
from jax.sharding import PartitionSpec as P

HEAD_DIM = 128
EPS = 1e-06
VIDEO = ("ulysses", "blk")


def normed(rows, gain):
    values = rows.astype(jnp.float32)
    scale = lax.rsqrt(jnp.mean(values * values, axis=-1, keepdims=True) + EPS)
    return values * scale * gain


def pack_kernel(splits, owners, owner_ref, *refs):
    total = (len(refs) - 2) // 2
    sources, send_ref, held, copy_sems = refs[:total], refs[total], refs[total + 1 : -1], refs[-1]
    copies = [
        pltpu.make_async_copy(source, buffer, copy_sems.at[i])
        for i, (source, buffer) in enumerate(zip(sources, held))
    ]
    for copy in copies:
        copy.start()
    q_ref, k_ref, v_ref, control_ref, qg_ref, kg_ref = held
    rows, feats = q_ref.shape
    part, slab_rows = rows // splits, rows // owners
    for copy in copies:
        copy.wait()
    packed = (
        normed(q_ref[...], qg_ref[...]).astype(jnp.bfloat16),
        normed(k_ref[...], kg_ref[...]).astype(jnp.bfloat16),
        v_ref[...],
    )
    for head in range(feats // HEAD_DIM):
        cols = slice(head * HEAD_DIM, (head + 1) * HEAD_DIM)
        for piece in range(splits):
            for i, array in enumerate(packed):
                send_ref[head * splits + piece, i * part : (i + 1) * part] = array[
                    piece * part : (piece + 1) * part, cols
                ]
    patches = control_ref[...].astype(jnp.float32)
    slabs = [patches[j * slab_rows : (j + 1) * slab_rows] for j in range(owners)]
    blocks = send_ref.shape[0] // owners
    for owner in range(owners):
        slab = slabs[0]
        for j in range(1, owners):
            slab = jnp.where(owner_ref[0, j] == owner, slabs[j], slab)
        slab = slab.astype(jnp.bfloat16)
        for tile in range(slab.shape[1] // HEAD_DIM):
            at = 3 * part + tile * slab_rows
            for block in range(blocks):
                send_ref[owner * blocks + block, at : at + slab_rows] = slab[
                    :, tile * HEAD_DIM : (tile + 1) * HEAD_DIM
                ]


def gain_kernel(layer_ref, gain_ref, out_ref):
    out_ref[...] = gain_ref[pl.ds(layer_ref[0], 1), :]


def attend_kernel(part, owners, block_ref, *refs):
    got_refs, (out_ref, patch_ref) = refs[:-2], refs[-2:]
    count = out_ref.shape[0]
    blocks = count // owners
    rows, width = patch_ref.shape
    slab_rows = rows // owners
    slabs = [
        got_refs[0][source * blocks + block_ref[0], 3 * part :].astype(jnp.float32)
        for source in range(owners)
    ]
    patches = [
        jnp.concatenate([slab[i * slab_rows : (i + 1) * slab_rows] for slab in slabs], axis=0)
        for i in range(width // HEAD_DIM)
    ]
    patch_ref[...] = normed(jnp.concatenate(patches, axis=1), 1.0).astype(jnp.bfloat16)

    keys = [ref[:, part : 2 * part].reshape(count * part, HEAD_DIM) for ref in got_refs]
    values = [ref[:, 2 * part : 3 * part].reshape(count * part, HEAD_DIM) for ref in got_refs]
    keys, values = jnp.concatenate(keys, axis=0), jnp.concatenate(values, axis=0)
    block = max(1, min(count, 2**18 // (part * keys.shape[0])))

    def attend(sources):
        queries = got_refs[0][sources, :part].reshape(block * part, HEAD_DIM)
        scores = lax.dot_general(
            queries, keys, (((1,), (1,)), ((), ())), preferred_element_type=jnp.float32
        ) * (HEAD_DIM ** (-0.5))
        peak = jnp.max(scores, axis=-1, keepdims=True)
        expo = jnp.exp(scores - peak)
        totals = jnp.sum(expo, axis=-1, keepdims=True)
        mixed = jnp.dot(expo.astype(jnp.bfloat16), values, preferred_element_type=jnp.float32)
        mixed = (mixed / totals).astype(jnp.bfloat16)
        out_ref[sources] = mixed.reshape(block, part, HEAD_DIM)

    if block == count:
        attend(slice(None))
    else:
        pl.loop(0, count // block)(lambda i: attend(pl.ds(i * block, block)))


def hint_kernel(patch_ref, weight_ref, gain_ref, out_ref):
    hint = jnp.dot(patch_ref[...], weight_ref[...], preferred_element_type=jnp.float32)
    out_ref[...] = hint.astype(jnp.bfloat16).astype(jnp.float32) * gain_ref[...]


def finish_kernel(splits, back_ref, hint_ref, out_ref):
    part = out_ref.shape[0] // splits
    for to in range(back_ref.shape[0]):
        head, piece = divmod(to, splits)
        at = slice(piece * part, (piece + 1) * part)
        cols = slice(head * HEAD_DIM, (head + 1) * HEAD_DIM)
        out_ref[at, cols] = (back_ref[to].astype(jnp.float32) + hint_ref[at, cols]).astype(
            jnp.bfloat16
        )


VMEM = pl.BlockSpec(memory_space=pltpu.VMEM)
SMEM = pl.BlockSpec(memory_space=pltpu.SMEM)
HBM = pl.BlockSpec(memory_space=pltpu.HBM)


def call(kernel, out_shape, specs, *operands, scratch=(), flops=0, nbytes=0):
    return pl.pallas_call(
        kernel,
        out_shape=out_shape,
        in_specs=specs,
        out_specs=jax.tree.map(lambda _: VMEM, out_shape),
        scratch_shapes=scratch,
        compiler_params=pltpu.CompilerParams(vmem_limit_bytes=32 * 2**20),
        cost_estimate=pl.CostEstimate(flops=flops, bytes_accessed=nbytes, transcendentals=0),
    )(*operands)


def shape(dims, dtype=jnp.bfloat16):
    return jax.ShapeDtypeStruct(dims, dtype)


def team_ring(size, splits, shift):
    return [(i, i - i % splits + (i + shift) % splits) for i in range(size)]


def shards(
    query_proj,
    key_proj,
    value_proj,
    query_gain,
    key_gain,
    control,
    hint_weight,
    hint_gain,
    owner_map,
    layer_index,
):
    owners, blocks = lax.axis_size("ulysses"), lax.axis_size("blk")
    count = owners * blocks
    rows, feats = query_proj.shape
    splits = count // (feats // HEAD_DIM)
    part = rows // splits
    width = control.shape[1]
    sources = (
        query_proj,
        key_proj,
        value_proj,
        control,
        query_gain.reshape(1, feats),
        key_gain.reshape(1, feats),
    )
    sources = [pltpu.with_memory_space_constraint(source, pltpu.HBM) for source in sources]
    send = call(
        functools.partial(pack_kernel, splits, owners),
        shape((count, 3 * part + rows // owners * (width // HEAD_DIM), HEAD_DIM)),
        [SMEM] + [HBM] * len(sources),
        owner_map,
        *sources,
        scratch=[pltpu.VMEM(source.shape, source.dtype) for source in sources]
        + [pltpu.SemaphoreType.DMA((len(sources),))],
    )
    got = lax.all_to_all(send, VIDEO, split_axis=0, concat_axis=0, tiled=True)
    gain_row = call(
        gain_kernel,
        shape((1, feats), jnp.float32),
        [SMEM, VMEM],
        layer_index,
        hint_gain,
        nbytes=hint_gain.size * 4,
    )
    got, gain_row = lax.optimization_barrier((got, gain_row))
    team = [got] + [
        lax.ppermute(got, "blk", team_ring(blocks, splits, shift)) for shift in range(1, splits)
    ]
    mixed, patches = call(
        functools.partial(attend_kernel, part, owners),
        [shape((count, part, HEAD_DIM)), shape((rows, width))],
        [SMEM] + [VMEM] * splits,
        lax.axis_index("blk").astype(jnp.int32).reshape(1),
        *team,
        flops=4 * count * part * count * rows * HEAD_DIM,
        nbytes=6 * count * rows * HEAD_DIM,
    )
    back = lax.all_to_all(mixed, VIDEO, split_axis=0, concat_axis=0, tiled=True)
    hint = call(
        hint_kernel,
        shape((rows, feats), jnp.float32),
        [VMEM] * 3,
        patches,
        hint_weight,
        gain_row,
        flops=2 * rows * width * feats,
        nbytes=2 * width * feats,
    )
    return call(
        functools.partial(finish_kernel, splits),
        shape((rows, feats)),
        [VMEM, VMEM],
        back,
        hint,
    )


def solution(mesh):
    split = P(("groups", "blk", "ulysses"), None)
    return jax.shard_map(
        shards,
        mesh=mesh,
        in_specs=(
            split,
            split,
            split,
            P(),
            P(),
            split,
            P(),
            P(),
            split,
            P(("groups", "blk", "ulysses")),
        ),
        out_specs=split,
        check_vma=False,
    )
```

```python
import functools

import jax
import jax.numpy as jnp
from jax import lax
from jax.experimental import pallas as pl
from jax.experimental.pallas import tpu as pltpu
from jax.sharding import PartitionSpec as P

HEAD_DIM = 128
EPS = 1e-06


def normed(rows, gain):
    values = rows.astype(jnp.float32)
    scale = lax.rsqrt(jnp.mean(values * values, axis=-1, keepdims=True) + EPS)
    return values * scale * gain


def partner(me, size, step):
    if size & (size - 1) == 0:
        return me ^ step
    return (step + size - me) % size


def swap(array, axis, step):
    size = lax.axis_size(axis)
    return lax.ppermute(array, axis, [(i, partner(i, size, step)) for i in range(size)])


def pack_kernel(owners, *refs):
    total = (len(refs) - owners - 2) // 2
    sources, out_refs = refs[:total], refs[total : total + owners]
    held, (norm_ref, copy_sems) = refs[total + owners : -2], refs[-2:]
    copies = [
        pltpu.make_async_copy(source, buffer, copy_sems.at[i])
        for i, (source, buffer) in enumerate(zip(sources, held))
    ]
    for copy in copies:
        copy.start()
    owner_ref, q_ref, k_ref, v_ref, control_ref, qg_ref, kg_ref = held
    rows, feats = q_ref.shape
    share = feats // owners
    slab_rows, width = rows // owners, control_ref.shape[1]
    me = lax.axis_index("ulysses")
    for copy in copies:
        copy.wait()
    norm_ref[0] = normed(k_ref[...], kg_ref[...]).astype(jnp.bfloat16)
    norm_ref[1] = v_ref[...]
    norm_ref[2] = normed(q_ref[...], qg_ref[...]).astype(jnp.bfloat16)
    patches = control_ref[...].astype(jnp.float32)
    slabs = [patches[j * slab_rows : (j + 1) * slab_rows] for j in range(owners)]
    for step, out_ref in enumerate(out_refs):
        to = partner(me, owners, step)
        at = 0
        for i in range(3):
            for head in range(share // HEAD_DIM):
                cols = pl.ds(pl.multiple_of(to * share + head * HEAD_DIM, HEAD_DIM), HEAD_DIM)
                out_ref[at : at + rows] = norm_ref[i, :, cols]
                at = at + rows
        slab = slabs[0]
        for j in range(1, owners):
            slab = jnp.where(owner_ref[0, j] == to, slabs[j], slab)
        slab = slab.astype(jnp.bfloat16)
        for tile in range(width // HEAD_DIM):
            out_ref[at : at + slab_rows] = slab[:, tile * HEAD_DIM : (tile + 1) * HEAD_DIM]
            at = at + slab_rows


def sort_kernel(rows, *refs):
    got_refs, (pair_ref, patch_ref) = refs[:-2], refs[-2:]
    owners = len(got_refs)
    slab_rows, width = rows // owners, patch_ref.shape[1]
    size = pair_ref.shape[1]
    start = 3 * size // 2
    for step, ref in enumerate(got_refs):
        pair_ref[step] = ref[:size]
    slabs = [ref[start:].astype(jnp.float32) for ref in got_refs]
    patches = [
        jnp.concatenate([slab[i * slab_rows : (i + 1) * slab_rows] for slab in slabs], axis=0)
        for i in range(width // HEAD_DIM)
    ]
    patch_ref[...] = normed(jnp.concatenate(patches, axis=1), 1.0).astype(jnp.bfloat16)


def attend_kernel(rows, owners, *refs):
    got_refs, pair_refs, out_refs = refs[:owners], refs[owners:-owners], refs[-owners:]
    heads = out_refs[0].shape[0] // rows
    count = len(pair_refs) * owners * rows
    group = max(1, min(owners, 2**17 // (rows * count)))
    for head in range(heads):
        at, past, ask = (slice((i * heads + head) * rows, (i * heads + head + 1) * rows) for i in range(3))
        keys = jnp.concatenate([ref[:, at].reshape(-1, HEAD_DIM) for ref in pair_refs], axis=0)
        values = jnp.concatenate([ref[:, past].reshape(-1, HEAD_DIM) for ref in pair_refs], axis=0)
        for first in range(0, owners, group):
            part = range(first, min(first + group, owners))
            queries = jnp.concatenate([got_refs[i][ask] for i in part], axis=0)
            scores = lax.dot_general(
                queries, keys, (((1,), (1,)), ((), ())), preferred_element_type=jnp.float32
            ) * (HEAD_DIM ** (-0.5))
            peak = jnp.max(scores, axis=-1, keepdims=True)
            expo = jnp.exp(scores - peak)
            totals = jnp.sum(expo, axis=-1, keepdims=True)
            mixed = jnp.dot(expo.astype(jnp.bfloat16), values, preferred_element_type=jnp.float32)
            mixed = (mixed / totals).astype(jnp.bfloat16)
            for j, i in enumerate(part):
                out_refs[i][at] = mixed[j * rows : (j + 1) * rows]


def hint_kernel(layer_ref, patch_ref, weight_ref, gain_ref, out_ref):
    owners, slab_rows, _ = out_ref.shape
    hint = jnp.dot(patch_ref[...], weight_ref[...], preferred_element_type=jnp.float32)
    hint = hint.astype(jnp.bfloat16).astype(jnp.float32) * gain_ref[pl.ds(layer_ref[0], 1), :]
    me = lax.axis_index("ulysses")
    for step in range(owners):
        out_ref[partner(me, owners, step)] = hint[step * slab_rows : (step + 1) * slab_rows]


def finish_kernel(owners, hint_ref, *refs):
    back_refs, out_ref = refs[:-1], refs[-1]
    rows, feats = out_ref.shape
    share = feats // owners
    me = lax.axis_index("ulysses")
    for step, ref in enumerate(back_refs):
        for head in range(share // HEAD_DIM):
            start = partner(me, owners, step) * share + head * HEAD_DIM
            cols = pl.ds(pl.multiple_of(start, HEAD_DIM), HEAD_DIM)
            attended = ref[head * rows : (head + 1) * rows].astype(jnp.float32)
            out_ref[:, cols] = (attended + hint_ref[:, cols]).astype(jnp.bfloat16)


VMEM = pl.BlockSpec(memory_space=pltpu.VMEM)
SMEM = pl.BlockSpec(memory_space=pltpu.SMEM)
HBM = pl.BlockSpec(memory_space=pltpu.HBM)


def call(kernel, out_shape, specs, *operands, scratch=(), flops=0, nbytes=0):
    return pl.pallas_call(
        kernel,
        out_shape=out_shape,
        in_specs=specs,
        out_specs=jax.tree.map(lambda _: VMEM, out_shape),
        scratch_shapes=scratch,
        compiler_params=pltpu.CompilerParams(vmem_limit_bytes=32 * 2**20),
        cost_estimate=pl.CostEstimate(flops=flops, bytes_accessed=nbytes, transcendentals=0),
    )(*operands)


def shape(dims, dtype=jnp.bfloat16):
    return jax.ShapeDtypeStruct(dims, dtype)


def gather_pairs(pairs, axis):
    size = lax.axis_size(axis)
    if size & (size - 1):
        return [swap(pairs, axis, step) for step in range(size)]
    held = [pairs]
    step = size // 2
    while step:
        held = held + [swap(array, axis, step) for array in held]
        step = step // 2
    return held


def shards(
    query_proj,
    key_proj,
    value_proj,
    query_gain,
    key_gain,
    control,
    hint_weight,
    hint_gain,
    owner_map,
    layer_index,
):
    owners = lax.axis_size("ulysses")
    rows, feats = query_proj.shape
    width = control.shape[1]
    lines = rows * (feats // owners // HEAD_DIM)
    slab_lines = rows // owners * (width // HEAD_DIM)
    sources = (
        owner_map,
        query_proj,
        key_proj,
        value_proj,
        control,
        query_gain.reshape(1, feats),
        key_gain.reshape(1, feats),
    )
    sources = [pltpu.with_memory_space_constraint(source, pltpu.HBM) for source in sources]
    sent = call(
        functools.partial(pack_kernel, owners),
        [shape((3 * lines + slab_lines, HEAD_DIM))] * owners,
        [HBM] * len(sources),
        *sources,
        scratch=[pltpu.SMEM(owner_map.shape, owner_map.dtype)]
        + [pltpu.VMEM(source.shape, source.dtype) for source in sources[1:]]
        + [
            pltpu.VMEM((3, rows, feats), jnp.bfloat16),
            pltpu.SemaphoreType.DMA((len(sources),)),
        ],
    )
    far = [swap(sent[step], "ulysses", step) for step in range(owners - 1, 0, -1)]
    got = [sent[0]] + far[::-1]
    pairs, patches = call(
        functools.partial(sort_kernel, rows),
        [shape((owners, 2 * lines, HEAD_DIM)), shape((rows, width))],
        [VMEM] * owners,
        *got,
    )
    held = gather_pairs(pairs, "blk")
    hint = call(
        hint_kernel,
        shape((owners, rows // owners, feats), jnp.float32),
        [SMEM] + [VMEM] * 3,
        layer_index,
        patches,
        hint_weight,
        hint_gain,
        flops=2 * rows * width * feats,
        nbytes=2 * width * feats,
    )
    mixed = call(
        functools.partial(attend_kernel, rows, owners),
        [shape((lines, HEAD_DIM))] * owners,
        [VMEM] * (owners + len(held)),
        *got,
        *held,
        flops=4 * lines * owners * len(held) * owners * rows * HEAD_DIM,
        nbytes=4 * len(held) * pairs.size,
    )
    far = [swap(mixed[step], "ulysses", step) for step in range(owners - 1, 0, -1)]
    return call(
        functools.partial(finish_kernel, owners),
        shape((rows, feats)),
        [VMEM] * (owners + 1),
        hint.reshape(rows, feats),
        mixed[0],
        *far[::-1],
    )


def solution(mesh):
    split = P(("groups", "blk", "ulysses"), None)
    return jax.shard_map(
        shards,
        mesh=mesh,
        in_specs=(
            split,
            split,
            split,
            P(),
            P(),
            split,
            P(),
            P(),
            split,
            P(("groups", "blk", "ulysses")),
        ),
        out_specs=split,
        check_vma=False,
    )
```

```python
import functools

import jax
import jax.numpy as jnp
from jax import lax
from jax.experimental import pallas as pl
from jax.experimental.pallas import tpu as pltpu
from jax.sharding import PartitionSpec as P

HEAD_DIM = 128
EPS = 1e-06


def normed(rows, gain):
    values = rows.astype(jnp.float32)
    scale = lax.rsqrt(jnp.mean(values * values, axis=-1, keepdims=True) + EPS)
    return values * scale * gain


def partner(me, size, step):
    if size & (size - 1) == 0:
        return me ^ step
    return (step + size - me) % size


def swap(array, axis, step):
    size = lax.axis_size(axis)
    return lax.ppermute(array, axis, [(i, partner(i, size, step)) for i in range(size)])


def pack_kernel(owners, *refs):
    total = (len(refs) - 2 * owners - 2) // 2
    sources, outs = refs[:total], refs[total : total + 2 * owners]
    held, (norm_ref, copy_sems) = refs[total + 2 * owners : -2], refs[-2:]
    copies = [
        pltpu.make_async_copy(source, buffer, copy_sems.at[i])
        for i, (source, buffer) in enumerate(zip(sources, held))
    ]
    for copy in copies:
        copy.start()
    owner_ref, q_ref, k_ref, v_ref, control_ref, qg_ref, kg_ref = held
    rows, feats = q_ref.shape
    share = feats // owners
    slab_rows, width = rows // owners, control_ref.shape[1]
    me = lax.axis_index("ulysses")
    for copy in copies:
        copy.wait()
    norm_ref[0] = normed(k_ref[...], kg_ref[...]).astype(jnp.bfloat16)
    norm_ref[1] = v_ref[...]
    norm_ref[2] = normed(q_ref[...], qg_ref[...]).astype(jnp.bfloat16)
    patches = control_ref[...].astype(jnp.float32)
    slabs = [patches[j * slab_rows : (j + 1) * slab_rows] for j in range(owners)]
    for step in range(owners):
        to = partner(me, owners, step)
        pair_ref, ask_ref = outs[step], outs[owners + step]
        for i, (out_ref, first) in enumerate(((pair_ref, 0), (pair_ref, 1), (ask_ref, 0))):
            for head in range(share // HEAD_DIM):
                cols = pl.ds(pl.multiple_of(to * share + head * HEAD_DIM, HEAD_DIM), HEAD_DIM)
                at = (first * (share // HEAD_DIM) + head) * rows
                out_ref[at : at + rows] = norm_ref[i, :, cols]
        slab = slabs[0]
        for j in range(1, owners):
            slab = jnp.where(owner_ref[0, j] == to, slabs[j], slab)
        slab = slab.astype(jnp.bfloat16)
        for tile in range(width // HEAD_DIM):
            at = share // HEAD_DIM * rows + tile * slab_rows
            ask_ref[at : at + slab_rows] = slab[:, tile * HEAD_DIM : (tile + 1) * HEAD_DIM]


def join_kernel(*refs):
    for i, ref in enumerate(refs[:-1]):
        refs[-1][i] = ref[...]


def attend_kernel(rows, owners, *refs):
    got_refs, pair_refs, out_refs = refs[:owners], refs[owners:-owners], refs[-owners:]
    heads = out_refs[0].shape[0] // rows
    count = sum(ref.shape[0] for ref in pair_refs) * rows
    group = max(1, min(owners, 2**17 // (rows * count)))
    for head in range(heads):
        at, past = (slice((i * heads + head) * rows, (i * heads + head + 1) * rows) for i in range(2))
        keys = jnp.concatenate([ref[:, at].reshape(-1, HEAD_DIM) for ref in pair_refs], axis=0)
        values = jnp.concatenate([ref[:, past].reshape(-1, HEAD_DIM) for ref in pair_refs], axis=0)
        for first in range(0, owners, group):
            part = range(first, min(first + group, owners))
            queries = jnp.concatenate([got_refs[i][at] for i in part], axis=0)
            scores = lax.dot_general(
                queries, keys, (((1,), (1,)), ((), ())), preferred_element_type=jnp.float32
            ) * (HEAD_DIM ** (-0.5))
            peak = jnp.max(scores, axis=-1, keepdims=True)
            expo = jnp.exp(scores - peak)
            totals = jnp.sum(expo, axis=-1, keepdims=True)
            mixed = jnp.dot(expo.astype(jnp.bfloat16), values, preferred_element_type=jnp.float32)
            mixed = (mixed / totals).astype(jnp.bfloat16)
            for j, i in enumerate(part):
                out_refs[i][at] = mixed[j * rows : (j + 1) * rows]


def hint_kernel(layer_ref, weight_ref, gain_ref, *refs):
    got_refs, out_ref = refs[:-1], refs[-1]
    owners, slab_rows, _ = out_ref.shape
    tiles = weight_ref.shape[0] // HEAD_DIM
    slabs = [ref[ref.shape[0] - tiles * slab_rows :].astype(jnp.float32) for ref in got_refs]
    patches = [
        jnp.concatenate([slab[i * slab_rows : (i + 1) * slab_rows] for slab in slabs], axis=0)
        for i in range(tiles)
    ]
    patches = normed(jnp.concatenate(patches, axis=1), 1.0).astype(jnp.bfloat16)
    hint = jnp.dot(patches, weight_ref[...], preferred_element_type=jnp.float32)
    hint = hint.astype(jnp.bfloat16).astype(jnp.float32) * gain_ref[pl.ds(layer_ref[0], 1), :]
    me = lax.axis_index("ulysses")
    for step in range(owners):
        out_ref[partner(me, owners, step)] = hint[step * slab_rows : (step + 1) * slab_rows]


def finish_kernel(owners, hint_ref, *refs):
    back_refs, out_ref = refs[:-1], refs[-1]
    rows, feats = out_ref.shape
    share = feats // owners
    me = lax.axis_index("ulysses")
    for step, ref in enumerate(back_refs):
        for head in range(share // HEAD_DIM):
            start = partner(me, owners, step) * share + head * HEAD_DIM
            cols = pl.ds(pl.multiple_of(start, HEAD_DIM), HEAD_DIM)
            attended = ref[head * rows : (head + 1) * rows].astype(jnp.float32)
            out_ref[:, cols] = (attended + hint_ref[:, cols]).astype(jnp.bfloat16)


VMEM = pl.BlockSpec(memory_space=pltpu.VMEM)
SMEM = pl.BlockSpec(memory_space=pltpu.SMEM)
HBM = pl.BlockSpec(memory_space=pltpu.HBM)


def call(kernel, out_shape, specs, *operands, scratch=(), flops=0, nbytes=0):
    return pl.pallas_call(
        kernel,
        out_shape=out_shape,
        in_specs=specs,
        out_specs=jax.tree.map(lambda _: VMEM, out_shape),
        scratch_shapes=scratch,
        compiler_params=pltpu.CompilerParams(vmem_limit_bytes=32 * 2**20),
        cost_estimate=pl.CostEstimate(flops=flops, bytes_accessed=nbytes, transcendentals=0),
    )(*operands)


def shape(dims, dtype=jnp.bfloat16):
    return jax.ShapeDtypeStruct(dims, dtype)


def gather(pairs, axis):
    return [pairs] + [swap(pairs, axis, step) for step in range(lax.axis_size(axis) - 1, 0, -1)]


def exchange(arrays, axis):
    return [arrays[0]] + [swap(array, axis, step) for step, array in enumerate(arrays) if step]


def shards(
    query_proj,
    key_proj,
    value_proj,
    query_gain,
    key_gain,
    control,
    hint_weight,
    hint_gain,
    owner_map,
    layer_index,
):
    owners = lax.axis_size("ulysses")
    rows, feats = query_proj.shape
    width = control.shape[1]
    lines = rows * (feats // owners // HEAD_DIM)
    slab_lines = rows // owners * (width // HEAD_DIM)
    sources = (
        owner_map,
        query_proj,
        key_proj,
        value_proj,
        control,
        query_gain.reshape(1, feats),
        key_gain.reshape(1, feats),
    )
    sources = [pltpu.with_memory_space_constraint(source, pltpu.HBM) for source in sources]
    sent = call(
        functools.partial(pack_kernel, owners),
        [shape((2 * lines, HEAD_DIM))] * owners + [shape((lines + slab_lines, HEAD_DIM))] * owners,
        [HBM] * len(sources),
        *sources,
        scratch=[pltpu.SMEM(owner_map.shape, owner_map.dtype)]
        + [pltpu.VMEM(source.shape, source.dtype) for source in sources[1:]]
        + [
            pltpu.VMEM((3, rows, feats), jnp.bfloat16),
            pltpu.SemaphoreType.DMA((len(sources),)),
        ],
    )
    pairs = exchange(sent[:owners], "ulysses")
    near = gather(pairs[0][None], "blk")
    got = exchange(sent[owners:], "ulysses")
    joined = call(
        join_kernel, shape((owners - 1, 2 * lines, HEAD_DIM)), [VMEM] * (owners - 1), *pairs[1:]
    )
    held = near + gather(joined, "blk")
    hint = call(
        hint_kernel,
        shape((owners, rows // owners, feats), jnp.float32),
        [SMEM] + [VMEM] * (2 + owners),
        layer_index,
        hint_weight,
        hint_gain,
        *got,
        flops=2 * rows * width * feats,
        nbytes=2 * width * feats,
    )
    mixed = call(
        functools.partial(attend_kernel, rows, owners),
        [shape((lines, HEAD_DIM))] * owners,
        [VMEM] * (owners + len(held)),
        *got,
        *held,
        flops=2 * lines * sum(array.size for array in held),
        nbytes=2 * sum(array.size for array in held),
    )
    return call(
        functools.partial(finish_kernel, owners),
        shape((rows, feats)),
        [VMEM] * (owners + 1),
        hint.reshape(rows, feats),
        *exchange(mixed, "ulysses"),
    )


def solution(mesh):
    split = P(("groups", "blk", "ulysses"), None)
    return jax.shard_map(
        shards,
        mesh=mesh,
        in_specs=(
            split,
            split,
            split,
            P(),
            P(),
            split,
            P(),
            P(),
            split,
            P(("groups", "blk", "ulysses")),
        ),
        out_specs=split,
        check_vma=False,
    )
```

```python
import functools

import jax
import jax.numpy as jnp
from jax import lax
from jax.experimental import pallas as pl
from jax.experimental.pallas import tpu as pltpu
from jax.sharding import PartitionSpec as P

HEAD_DIM = 128
EPS = 1e-06


def normed(rows, gain):
    values = rows.astype(jnp.float32)
    scale = lax.rsqrt(jnp.mean(values * values, axis=-1, keepdims=True) + EPS)
    return values * scale * gain


def partner(me, size, step):
    if size & (size - 1) == 0:
        return me ^ step
    return (step + size - me) % size


def swap(array, axis, step):
    size = lax.axis_size(axis)
    return lax.ppermute(array, axis, [(i, partner(i, size, step)) for i in range(size)])


def pack_kernel(owners, *refs):
    total = (len(refs) - 2 * owners - 2) // 2
    sources, outs = refs[:total], refs[total : total + 2 * owners]
    held, (norm_ref, copy_sems) = refs[total + 2 * owners : -2], refs[-2:]
    copies = [
        pltpu.make_async_copy(source, buffer, copy_sems.at[i])
        for i, (source, buffer) in enumerate(zip(sources, held))
    ]
    for copy in copies:
        copy.start()
    owner_ref, q_ref, k_ref, v_ref, control_ref, qg_ref, kg_ref = held
    rows, feats = q_ref.shape
    share = feats // owners
    slab_rows, width = rows // owners, control_ref.shape[1]
    me = lax.axis_index("ulysses")
    for copy in copies:
        copy.wait()
    norm_ref[0] = normed(k_ref[...], kg_ref[...]).astype(jnp.bfloat16)
    norm_ref[1] = v_ref[...]
    norm_ref[2] = normed(q_ref[...], qg_ref[...]).astype(jnp.bfloat16)
    patches = control_ref[...].astype(jnp.float32)
    slabs = [patches[j * slab_rows : (j + 1) * slab_rows] for j in range(owners)]
    for step in range(owners):
        to = partner(me, owners, step)
        pair_ref, ask_ref = outs[step], outs[owners + step]
        for i, (out_ref, first) in enumerate(((pair_ref, 0), (pair_ref, 1), (ask_ref, 0))):
            for head in range(share // HEAD_DIM):
                cols = pl.ds(pl.multiple_of(to * share + head * HEAD_DIM, HEAD_DIM), HEAD_DIM)
                at = (first * (share // HEAD_DIM) + head) * rows
                out_ref[at : at + rows] = norm_ref[i, :, cols]
        slab = slabs[0]
        for j in range(1, owners):
            slab = jnp.where(owner_ref[0, j] == to, slabs[j], slab)
        slab = slab.astype(jnp.bfloat16)
        for tile in range(width // HEAD_DIM):
            at = share // HEAD_DIM * rows + tile * slab_rows
            ask_ref[at : at + slab_rows] = slab[:, tile * HEAD_DIM : (tile + 1) * HEAD_DIM]


def join_kernel(*refs):
    for i, ref in enumerate(refs[:-1]):
        refs[-1][i] = ref[...]


def attend_kernel(rows, owners, *refs):
    got_refs, pair_refs, out_refs = refs[:owners], refs[owners:-owners], refs[-owners:]
    heads = out_refs[0].shape[0] // rows
    count = sum(ref.shape[0] for ref in pair_refs) * rows
    group = max(1, min(owners, 2**17 // (rows * count)))
    for head in range(heads):
        at, past = (slice((i * heads + head) * rows, (i * heads + head + 1) * rows) for i in range(2))
        keys = jnp.concatenate([ref[:, at].reshape(-1, HEAD_DIM) for ref in pair_refs], axis=0)
        values = jnp.concatenate([ref[:, past].reshape(-1, HEAD_DIM) for ref in pair_refs], axis=0)
        for first in range(0, owners, group):
            part = range(first, min(first + group, owners))
            queries = jnp.concatenate([got_refs[i][at] for i in part], axis=0)
            scores = lax.dot_general(
                queries, keys, (((1,), (1,)), ((), ())), preferred_element_type=jnp.float32
            ) * (HEAD_DIM ** (-0.5))
            peak = jnp.max(scores, axis=-1, keepdims=True)
            expo = jnp.exp(scores - peak)
            totals = jnp.sum(expo, axis=-1, keepdims=True)
            mixed = jnp.dot(expo.astype(jnp.bfloat16), values, preferred_element_type=jnp.float32)
            mixed = (mixed / totals).astype(jnp.bfloat16)
            for j, i in enumerate(part):
                out_refs[i][at] = mixed[j * rows : (j + 1) * rows]


def hint_kernel(layer_ref, weight_ref, gain_ref, *refs):
    got_refs, out_ref = refs[:-1], refs[-1]
    owners, slab_rows, _ = out_ref.shape
    tiles = weight_ref.shape[0] // HEAD_DIM
    slabs = [ref[ref.shape[0] - tiles * slab_rows :].astype(jnp.float32) for ref in got_refs]
    patches = [
        jnp.concatenate([slab[i * slab_rows : (i + 1) * slab_rows] for slab in slabs], axis=0)
        for i in range(tiles)
    ]
    patches = normed(jnp.concatenate(patches, axis=1), 1.0).astype(jnp.bfloat16)
    hint = jnp.dot(patches, weight_ref[...], preferred_element_type=jnp.float32)
    hint = hint.astype(jnp.bfloat16).astype(jnp.float32) * gain_ref[pl.ds(layer_ref[0], 1), :]
    me = lax.axis_index("ulysses")
    for step in range(owners):
        out_ref[partner(me, owners, step)] = hint[step * slab_rows : (step + 1) * slab_rows]


def finish_kernel(owners, hint_ref, *refs):
    back_refs, out_ref = refs[:-1], refs[-1]
    rows, feats = out_ref.shape
    share = feats // owners
    me = lax.axis_index("ulysses")
    for step, ref in enumerate(back_refs):
        for head in range(share // HEAD_DIM):
            start = partner(me, owners, step) * share + head * HEAD_DIM
            cols = pl.ds(pl.multiple_of(start, HEAD_DIM), HEAD_DIM)
            attended = ref[head * rows : (head + 1) * rows].astype(jnp.float32)
            out_ref[:, cols] = (attended + hint_ref[:, cols]).astype(jnp.bfloat16)


VMEM = pl.BlockSpec(memory_space=pltpu.VMEM)
SMEM = pl.BlockSpec(memory_space=pltpu.SMEM)
HBM = pl.BlockSpec(memory_space=pltpu.HBM)


def call(kernel, out_shape, specs, *operands, scratch=(), flops=0, nbytes=0):
    return pl.pallas_call(
        kernel,
        out_shape=out_shape,
        in_specs=specs,
        out_specs=jax.tree.map(lambda _: VMEM, out_shape),
        scratch_shapes=scratch,
        compiler_params=pltpu.CompilerParams(vmem_limit_bytes=32 * 2**20),
        cost_estimate=pl.CostEstimate(flops=flops, bytes_accessed=nbytes, transcendentals=0),
    )(*operands)


def shape(dims, dtype=jnp.bfloat16):
    return jax.ShapeDtypeStruct(dims, dtype)


def gather(pairs, beside, axis):
    size = lax.axis_size(axis)
    if size & (size - 1):
        return [swap(pairs, axis, step) for step in range(size)], beside
    held = [pairs]
    step = size // 2
    while step:
        moved = [swap(array, axis, step) for array in held]
        if len(held) == 1:
            moved, beside = lax.optimization_barrier((moved, beside))
        held = held + moved
        step = step // 2
    return held, beside


def exchange(arrays, axis):
    return list(arrays[:1]) + [swap(array, axis, step) for step, array in enumerate(arrays) if step]


def shards(
    query_proj,
    key_proj,
    value_proj,
    query_gain,
    key_gain,
    control,
    hint_weight,
    hint_gain,
    owner_map,
    layer_index,
):
    owners = lax.axis_size("ulysses")
    rows, feats = query_proj.shape
    width = control.shape[1]
    lines = rows * (feats // owners // HEAD_DIM)
    slab_lines = rows // owners * (width // HEAD_DIM)
    sources = (
        owner_map,
        query_proj,
        key_proj,
        value_proj,
        control,
        query_gain.reshape(1, feats),
        key_gain.reshape(1, feats),
    )
    sources = [pltpu.with_memory_space_constraint(source, pltpu.HBM) for source in sources]
    sent = call(
        functools.partial(pack_kernel, owners),
        [shape((2 * lines, HEAD_DIM))] * owners + [shape((lines + slab_lines, HEAD_DIM))] * owners,
        [HBM] * len(sources),
        *sources,
        scratch=[pltpu.SMEM(owner_map.shape, owner_map.dtype)]
        + [pltpu.VMEM(source.shape, source.dtype) for source in sources[1:]]
        + [
            pltpu.VMEM((3, rows, feats), jnp.bfloat16),
            pltpu.SemaphoreType.DMA((len(sources),)),
        ],
    )
    pairs = exchange(sent[:owners], "ulysses")
    got = exchange(sent[owners:], "ulysses")
    joined = call(join_kernel, shape((owners, 2 * lines, HEAD_DIM)), [VMEM] * owners, *pairs)
    held, got = gather(joined, got, "blk")
    hint = call(
        hint_kernel,
        shape((owners, rows // owners, feats), jnp.float32),
        [SMEM] + [VMEM] * (2 + owners),
        layer_index,
        hint_weight,
        hint_gain,
        *got,
        flops=2 * rows * width * feats,
        nbytes=2 * width * feats,
    )
    mixed = call(
        functools.partial(attend_kernel, rows, owners),
        [shape((lines, HEAD_DIM))] * owners,
        [VMEM] * (owners + len(held)),
        *got,
        *held,
        flops=2 * lines * sum(array.size for array in held),
        nbytes=2 * sum(array.size for array in held),
    )
    return call(
        functools.partial(finish_kernel, owners),
        shape((rows, feats)),
        [VMEM] * (owners + 1),
        hint.reshape(rows, feats),
        *exchange(mixed, "ulysses"),
    )


def solution(mesh):
    split = P(("groups", "blk", "ulysses"), None)
    return jax.shard_map(
        shards,
        mesh=mesh,
        in_specs=(
            split,
            split,
            split,
            P(),
            P(),
            split,
            P(),
            P(),
            split,
            P(("groups", "blk", "ulysses")),
        ),
        out_specs=split,
        check_vma=False,
    )
```

```python
import functools

import jax
import jax.numpy as jnp
from jax import lax
from jax.experimental import pallas as pl
from jax.experimental.pallas import tpu as pltpu
from jax.sharding import PartitionSpec as P

HEAD_DIM = 128
EPS = 1e-06


def normed(rows, gain):
    values = rows.astype(jnp.float32)
    scale = lax.rsqrt(jnp.mean(values * values, axis=-1, keepdims=True) + EPS)
    return values * scale * gain


def partner(me, size, step):
    if size & (size - 1) == 0:
        return me ^ step
    return (step + size - me) % size


def steps_of(owners):
    return [0, *range(owners - 1, 0, -1)]


def swap(array, axis, step):
    size = lax.axis_size(axis)
    return lax.ppermute(array, axis, [(i, partner(i, size, step)) for i in range(size)])


def pack_kernel(owners, *refs):
    total = (len(refs) - owners - 2) // 2
    sources, out_refs = refs[:total], refs[total : total + owners]
    held, (norm_ref, copy_sems) = refs[total + owners : -2], refs[-2:]
    copies = [
        pltpu.make_async_copy(source, buffer, copy_sems.at[i])
        for i, (source, buffer) in enumerate(zip(sources, held))
    ]
    for copy in copies:
        copy.start()
    owner_ref, q_ref, k_ref, v_ref, control_ref, qg_ref, kg_ref = held
    rows, feats = q_ref.shape
    share = feats // owners
    slab_rows, width = rows // owners, control_ref.shape[1]
    me = lax.axis_index("ulysses")
    for copy in copies:
        copy.wait()
    norm_ref[0] = normed(k_ref[...], kg_ref[...]).astype(jnp.bfloat16)
    norm_ref[1] = v_ref[...]
    norm_ref[2] = normed(q_ref[...], qg_ref[...]).astype(jnp.bfloat16)
    patches = control_ref[...].astype(jnp.float32)
    slabs = [patches[j * slab_rows : (j + 1) * slab_rows] for j in range(owners)]
    for step, out_ref in zip(steps_of(owners), out_refs):
        to = partner(me, owners, step)
        at = 0
        for i in range(3):
            for head in range(share // HEAD_DIM):
                cols = pl.ds(pl.multiple_of(to * share + head * HEAD_DIM, HEAD_DIM), HEAD_DIM)
                out_ref[at : at + rows] = norm_ref[i, :, cols]
                at = at + rows
        slab = slabs[0]
        for j in range(1, owners):
            slab = jnp.where(owner_ref[0, j] == to, slabs[j], slab)
        slab = slab.astype(jnp.bfloat16)
        for tile in range(width // HEAD_DIM):
            out_ref[at : at + slab_rows] = slab[:, tile * HEAD_DIM : (tile + 1) * HEAD_DIM]
            at = at + slab_rows


def sort_kernel(rows, *refs):
    got_refs, (pair_ref, patch_ref) = refs[:-2], refs[-2:]
    owners = len(got_refs)
    slab_rows, width = rows // owners, patch_ref.shape[1]
    size = pair_ref.shape[1]
    start = 3 * size // 2
    for i, ref in enumerate(got_refs):
        pair_ref[i] = ref[:size]
    slabs = [ref[start:].astype(jnp.float32) for ref in got_refs]
    patches = [
        jnp.concatenate([slab[i * slab_rows : (i + 1) * slab_rows] for slab in slabs], axis=0)
        for i in range(width // HEAD_DIM)
    ]
    patch_ref[...] = normed(jnp.concatenate(patches, axis=1), 1.0).astype(jnp.bfloat16)


def attend_kernel(rows, owners, *refs):
    got_refs, pair_refs, out_refs = refs[:owners], refs[owners:-owners], refs[-owners:]
    heads = out_refs[0].shape[0] // rows
    count = len(pair_refs) * owners * rows
    group = max(1, min(owners, 2**17 // (rows * count)))
    for head in range(heads):
        at, past, ask = (slice((i * heads + head) * rows, (i * heads + head + 1) * rows) for i in range(3))
        keys = jnp.concatenate([ref[:, at].reshape(-1, HEAD_DIM) for ref in pair_refs], axis=0)
        values = jnp.concatenate([ref[:, past].reshape(-1, HEAD_DIM) for ref in pair_refs], axis=0)
        for first in range(0, owners, group):
            part = range(first, min(first + group, owners))
            queries = jnp.concatenate([got_refs[i][ask] for i in part], axis=0)
            scores = lax.dot_general(
                queries, keys, (((1,), (1,)), ((), ())), preferred_element_type=jnp.float32
            ) * (HEAD_DIM ** (-0.5))
            peak = jnp.max(scores, axis=-1, keepdims=True)
            expo = jnp.exp(scores - peak)
            totals = jnp.sum(expo, axis=-1, keepdims=True)
            mixed = jnp.dot(expo.astype(jnp.bfloat16), values, preferred_element_type=jnp.float32)
            mixed = (mixed / totals).astype(jnp.bfloat16)
            for j, i in enumerate(part):
                out_refs[i][at] = mixed[j * rows : (j + 1) * rows]


def hint_kernel(layer_ref, patch_ref, weight_ref, gain_ref, out_ref):
    owners, slab_rows, _ = out_ref.shape
    hint = jnp.dot(patch_ref[...], weight_ref[...], preferred_element_type=jnp.float32)
    hint = hint.astype(jnp.bfloat16).astype(jnp.float32) * gain_ref[pl.ds(layer_ref[0], 1), :]
    me = lax.axis_index("ulysses")
    for i, step in enumerate(steps_of(owners)):
        out_ref[partner(me, owners, step)] = hint[i * slab_rows : (i + 1) * slab_rows]


def finish_kernel(owners, hint_ref, *refs):
    back_refs, out_ref = refs[:-1], refs[-1]
    rows, feats = out_ref.shape
    share = feats // owners
    me = lax.axis_index("ulysses")
    for step, ref in zip(steps_of(owners), back_refs):
        for head in range(share // HEAD_DIM):
            start = partner(me, owners, step) * share + head * HEAD_DIM
            cols = pl.ds(pl.multiple_of(start, HEAD_DIM), HEAD_DIM)
            attended = ref[head * rows : (head + 1) * rows].astype(jnp.float32)
            out_ref[:, cols] = (attended + hint_ref[:, cols]).astype(jnp.bfloat16)


VMEM = pl.BlockSpec(memory_space=pltpu.VMEM)
SMEM = pl.BlockSpec(memory_space=pltpu.SMEM)
HBM = pl.BlockSpec(memory_space=pltpu.HBM)


def call(kernel, out_shape, specs, *operands, scratch=(), flops=0, nbytes=0):
    return pl.pallas_call(
        kernel,
        out_shape=out_shape,
        in_specs=specs,
        out_specs=jax.tree.map(lambda _: VMEM, out_shape),
        scratch_shapes=scratch,
        compiler_params=pltpu.CompilerParams(vmem_limit_bytes=32 * 2**20),
        cost_estimate=pl.CostEstimate(flops=flops, bytes_accessed=nbytes, transcendentals=0),
    )(*operands)


def shape(dims, dtype=jnp.bfloat16):
    return jax.ShapeDtypeStruct(dims, dtype)


def gather(pairs, beside, axis):
    size = lax.axis_size(axis)
    if size & (size - 1):
        return [swap(pairs, axis, step) for step in range(size)], beside
    held = [pairs]
    step = size // 2
    while step:
        moved = [swap(array, axis, step) for array in held]
        if len(held) == 1:
            moved, beside = lax.optimization_barrier((moved, beside))
        held = held + moved
        step = step // 2
    return held, beside


def exchange(arrays, axis):
    return [
        swap(array, axis, step) if step else array
        for step, array in zip(steps_of(lax.axis_size(axis)), arrays)
    ]


def shards(
    query_proj,
    key_proj,
    value_proj,
    query_gain,
    key_gain,
    control,
    hint_weight,
    hint_gain,
    owner_map,
    layer_index,
):
    owners = lax.axis_size("ulysses")
    rows, feats = query_proj.shape
    width = control.shape[1]
    lines = rows * (feats // owners // HEAD_DIM)
    slab_lines = rows // owners * (width // HEAD_DIM)
    sources = (
        owner_map,
        query_proj,
        key_proj,
        value_proj,
        control,
        query_gain.reshape(1, feats),
        key_gain.reshape(1, feats),
    )
    sources = [pltpu.with_memory_space_constraint(source, pltpu.HBM) for source in sources]
    sent = call(
        functools.partial(pack_kernel, owners),
        [shape((3 * lines + slab_lines, HEAD_DIM))] * owners,
        [HBM] * len(sources),
        *sources,
        scratch=[pltpu.SMEM(owner_map.shape, owner_map.dtype)]
        + [pltpu.VMEM(source.shape, source.dtype) for source in sources[1:]]
        + [
            pltpu.VMEM((3, rows, feats), jnp.bfloat16),
            pltpu.SemaphoreType.DMA((len(sources),)),
        ],
    )
    got = exchange(sent, "ulysses")
    pairs, patches = call(
        functools.partial(sort_kernel, rows),
        [shape((owners, 2 * lines, HEAD_DIM)), shape((rows, width))],
        [VMEM] * owners,
        *got,
    )
    hint = call(
        hint_kernel,
        shape((owners, rows // owners, feats), jnp.float32),
        [SMEM] + [VMEM] * 3,
        layer_index,
        patches,
        hint_weight,
        hint_gain,
        flops=2 * rows * width * feats,
        nbytes=2 * width * feats,
    )
    held, hint = gather(pairs, hint, "blk")
    mixed = call(
        functools.partial(attend_kernel, rows, owners),
        [shape((lines, HEAD_DIM))] * owners,
        [VMEM] * (owners + len(held)),
        *got,
        *held,
        flops=4 * lines * owners * len(held) * owners * rows * HEAD_DIM,
        nbytes=4 * len(held) * pairs.size,
    )
    return call(
        functools.partial(finish_kernel, owners),
        shape((rows, feats)),
        [VMEM] * (owners + 1),
        hint.reshape(rows, feats),
        *exchange(mixed, "ulysses"),
    )


def solution(mesh):
    split = P(("groups", "blk", "ulysses"), None)
    return jax.shard_map(
        shards,
        mesh=mesh,
        in_specs=(
            split,
            split,
            split,
            P(),
            P(),
            split,
            P(),
            P(),
            split,
            P(("groups", "blk", "ulysses")),
        ),
        out_specs=split,
        check_vma=False,
    )
```

```python
import functools

import jax
import jax.numpy as jnp
from jax import lax
from jax.experimental import pallas as pl
from jax.experimental.pallas import tpu as pltpu
from jax.sharding import PartitionSpec as P

HEAD_DIM = 128
EPS = 1e-06


def normed(rows, gain):
    values = rows.astype(jnp.float32)
    scale = lax.rsqrt(jnp.mean(values * values, axis=-1, keepdims=True) + EPS)
    return values * scale * gain


def partner(me, size, step):
    if size & (size - 1) == 0:
        return me ^ step
    return (step + size - me) % size


def steps_of(owners):
    return sorted(range(owners), key=lambda step: (step > 0, -step.bit_length(), step))


def swap(array, axis, step):
    size = lax.axis_size(axis)
    return lax.ppermute(array, axis, [(i, partner(i, size, step)) for i in range(size)])


def pack_kernel(owners, *refs):
    total = (len(refs) - owners - 2) // 2
    sources, out_refs = refs[:total], refs[total : total + owners]
    held, (norm_ref, copy_sems) = refs[total + owners : -2], refs[-2:]
    copies = [
        pltpu.make_async_copy(source, buffer, copy_sems.at[i])
        for i, (source, buffer) in enumerate(zip(sources, held))
    ]
    for copy in copies:
        copy.start()
    owner_ref, q_ref, k_ref, v_ref, control_ref, qg_ref, kg_ref = held
    rows, feats = q_ref.shape
    share = feats // owners
    slab_rows, width = rows // owners, control_ref.shape[1]
    me = lax.axis_index("ulysses")
    for copy in copies:
        copy.wait()
    norm_ref[0] = normed(k_ref[...], kg_ref[...]).astype(jnp.bfloat16)
    norm_ref[1] = v_ref[...]
    norm_ref[2] = normed(q_ref[...], qg_ref[...]).astype(jnp.bfloat16)
    patches = control_ref[...].astype(jnp.float32)
    slabs = [patches[j * slab_rows : (j + 1) * slab_rows] for j in range(owners)]
    for step, out_ref in zip(steps_of(owners), out_refs):
        to = partner(me, owners, step)
        at = 0
        for i in range(3):
            for head in range(share // HEAD_DIM):
                cols = pl.ds(pl.multiple_of(to * share + head * HEAD_DIM, HEAD_DIM), HEAD_DIM)
                out_ref[at : at + rows] = norm_ref[i, :, cols]
                at = at + rows
        slab = slabs[0]
        for j in range(1, owners):
            slab = jnp.where(owner_ref[0, j] == to, slabs[j], slab)
        slab = slab.astype(jnp.bfloat16)
        for tile in range(width // HEAD_DIM):
            out_ref[at : at + slab_rows] = slab[:, tile * HEAD_DIM : (tile + 1) * HEAD_DIM]
            at = at + slab_rows


def sort_kernel(rows, *refs):
    got_refs, (pair_ref, patch_ref) = refs[:-2], refs[-2:]
    owners = len(got_refs)
    slab_rows, width = rows // owners, patch_ref.shape[1]
    size = pair_ref.shape[1]
    start = 3 * size // 2
    for i, ref in enumerate(got_refs):
        pair_ref[i] = ref[:size]
    slabs = [ref[start:].astype(jnp.float32) for ref in got_refs]
    patches = [
        jnp.concatenate([slab[i * slab_rows : (i + 1) * slab_rows] for slab in slabs], axis=0)
        for i in range(width // HEAD_DIM)
    ]
    patch_ref[...] = normed(jnp.concatenate(patches, axis=1), 1.0).astype(jnp.bfloat16)


def attend_kernel(rows, owners, *refs):
    got_refs, pair_refs, out_refs = refs[:owners], refs[owners:-owners], refs[-owners:]
    heads = out_refs[0].shape[0] // rows
    count = len(pair_refs) * owners * rows
    group = max(1, min(owners, 2**17 // (rows * count)))
    for head in range(heads):
        at, past, ask = (slice((i * heads + head) * rows, (i * heads + head + 1) * rows) for i in range(3))
        keys = jnp.concatenate([ref[:, at].reshape(-1, HEAD_DIM) for ref in pair_refs], axis=0)
        values = jnp.concatenate([ref[:, past].reshape(-1, HEAD_DIM) for ref in pair_refs], axis=0)
        for first in range(0, owners, group):
            part = range(first, min(first + group, owners))
            queries = jnp.concatenate([got_refs[i][ask] for i in part], axis=0)
            scores = lax.dot_general(
                queries, keys, (((1,), (1,)), ((), ())), preferred_element_type=jnp.float32
            ) * (HEAD_DIM ** (-0.5))
            peak = jnp.max(scores, axis=-1, keepdims=True)
            expo = jnp.exp(scores - peak)
            totals = jnp.sum(expo, axis=-1, keepdims=True)
            mixed = jnp.dot(expo.astype(jnp.bfloat16), values, preferred_element_type=jnp.float32)
            mixed = (mixed / totals).astype(jnp.bfloat16)
            for j, i in enumerate(part):
                out_refs[i][at] = mixed[j * rows : (j + 1) * rows]


def hint_kernel(layer_ref, patch_ref, weight_ref, gain_ref, out_ref):
    owners, slab_rows, _ = out_ref.shape
    hint = jnp.dot(patch_ref[...], weight_ref[...], preferred_element_type=jnp.float32)
    hint = hint.astype(jnp.bfloat16).astype(jnp.float32) * gain_ref[pl.ds(layer_ref[0], 1), :]
    me = lax.axis_index("ulysses")
    for i, step in enumerate(steps_of(owners)):
        out_ref[partner(me, owners, step)] = hint[i * slab_rows : (i + 1) * slab_rows]


def finish_kernel(owners, hint_ref, *refs):
    back_refs, out_ref = refs[:-1], refs[-1]
    rows, feats = out_ref.shape
    share = feats // owners
    me = lax.axis_index("ulysses")
    for step, ref in zip(steps_of(owners), back_refs):
        for head in range(share // HEAD_DIM):
            start = partner(me, owners, step) * share + head * HEAD_DIM
            cols = pl.ds(pl.multiple_of(start, HEAD_DIM), HEAD_DIM)
            attended = ref[head * rows : (head + 1) * rows].astype(jnp.float32)
            out_ref[:, cols] = (attended + hint_ref[:, cols]).astype(jnp.bfloat16)


VMEM = pl.BlockSpec(memory_space=pltpu.VMEM)
SMEM = pl.BlockSpec(memory_space=pltpu.SMEM)
HBM = pl.BlockSpec(memory_space=pltpu.HBM)


def call(kernel, out_shape, specs, *operands, scratch=(), flops=0, nbytes=0):
    return pl.pallas_call(
        kernel,
        out_shape=out_shape,
        in_specs=specs,
        out_specs=jax.tree.map(lambda _: VMEM, out_shape),
        scratch_shapes=scratch,
        compiler_params=pltpu.CompilerParams(vmem_limit_bytes=32 * 2**20),
        cost_estimate=pl.CostEstimate(flops=flops, bytes_accessed=nbytes, transcendentals=0),
    )(*operands)


def shape(dims, dtype=jnp.bfloat16):
    return jax.ShapeDtypeStruct(dims, dtype)


def gather(pairs, beside, axis):
    size = lax.axis_size(axis)
    if size & (size - 1):
        return [swap(pairs, axis, step) for step in range(size)], beside
    held = [pairs]
    step = size // 2
    while step:
        moved = [swap(array, axis, step) for array in held]
        if len(held) == 1:
            moved, beside = lax.optimization_barrier((moved, beside))
        held = held + moved
        step = step // 2
    return held, beside


def exchange(arrays, axis):
    return [
        swap(array, axis, step) if step else array
        for step, array in zip(steps_of(lax.axis_size(axis)), arrays)
    ]


def shards(
    query_proj,
    key_proj,
    value_proj,
    query_gain,
    key_gain,
    control,
    hint_weight,
    hint_gain,
    owner_map,
    layer_index,
):
    owners = lax.axis_size("ulysses")
    rows, feats = query_proj.shape
    width = control.shape[1]
    lines = rows * (feats // owners // HEAD_DIM)
    slab_lines = rows // owners * (width // HEAD_DIM)
    sources = (
        owner_map,
        query_proj,
        key_proj,
        value_proj,
        control,
        query_gain.reshape(1, feats),
        key_gain.reshape(1, feats),
    )
    sources = [pltpu.with_memory_space_constraint(source, pltpu.HBM) for source in sources]
    sent = call(
        functools.partial(pack_kernel, owners),
        [shape((3 * lines + slab_lines, HEAD_DIM))] * owners,
        [HBM] * len(sources),
        *sources,
        scratch=[pltpu.SMEM(owner_map.shape, owner_map.dtype)]
        + [pltpu.VMEM(source.shape, source.dtype) for source in sources[1:]]
        + [
            pltpu.VMEM((3, rows, feats), jnp.bfloat16),
            pltpu.SemaphoreType.DMA((len(sources),)),
        ],
    )
    got = exchange(sent, "ulysses")
    pairs, patches = call(
        functools.partial(sort_kernel, rows),
        [shape((owners, 2 * lines, HEAD_DIM)), shape((rows, width))],
        [VMEM] * owners,
        *got,
    )
    hint = call(
        hint_kernel,
        shape((owners, rows // owners, feats), jnp.float32),
        [SMEM] + [VMEM] * 3,
        layer_index,
        patches,
        hint_weight,
        hint_gain,
        flops=2 * rows * width * feats,
        nbytes=2 * width * feats,
    )
    held, hint = gather(pairs, hint, "blk")
    mixed = call(
        functools.partial(attend_kernel, rows, owners),
        [shape((lines, HEAD_DIM))] * owners,
        [VMEM] * (owners + len(held)),
        *got,
        *held,
        flops=4 * lines * owners * len(held) * owners * rows * HEAD_DIM,
        nbytes=4 * len(held) * pairs.size,
    )
    return call(
        functools.partial(finish_kernel, owners),
        shape((rows, feats)),
        [VMEM] * (owners + 1),
        hint.reshape(rows, feats),
        *exchange(mixed, "ulysses"),
    )


def solution(mesh):
    split = P(("groups", "blk", "ulysses"), None)
    return jax.shard_map(
        shards,
        mesh=mesh,
        in_specs=(
            split,
            split,
            split,
            P(),
            P(),
            split,
            P(),
            P(),
            split,
            P(("groups", "blk", "ulysses")),
        ),
        out_specs=split,
        check_vma=False,
    )
```

```python
import functools

import jax
import jax.numpy as jnp
from jax import lax
from jax.experimental import pallas as pl
from jax.experimental.pallas import tpu as pltpu
from jax.sharding import PartitionSpec as P

HEAD_DIM = 128
EPS = 1e-06


def normed(rows, gain):
    values = rows.astype(jnp.float32)
    scale = lax.rsqrt(jnp.mean(values * values, axis=-1, keepdims=True) + EPS)
    return values * scale * gain


def partner(me, step):
    return me ^ step


def steps_of(owners):
    return [0, *range(owners - 1, 0, -1)]


def swap(array, axis, step):
    size = lax.axis_size(axis)
    return lax.ppermute(array, axis, [(i, partner(i, step)) for i in range(size)])


def pack_kernel(owners, *refs):
    total = (len(refs) - owners - 3) // 2
    sources, out_refs, own_ref = refs[:total], refs[total : total + owners], refs[total + owners]
    held, (norm_ref, copy_sems) = refs[total + owners + 1 : -2], refs[-2:]
    copies = [
        pltpu.make_async_copy(source, buffer, copy_sems.at[i])
        for i, (source, buffer) in enumerate(zip(sources, held))
    ]
    for copy in copies:
        copy.start()
    owner_ref, q_ref, k_ref, v_ref, control_ref, qg_ref, kg_ref = held
    rows, feats = q_ref.shape
    share = feats // owners
    slab_rows, width = rows // owners, control_ref.shape[1]
    me = lax.axis_index("ulysses")
    for copy in copies:
        copy.wait()
    norm_ref[0] = normed(k_ref[...], kg_ref[...]).astype(jnp.bfloat16)
    norm_ref[1] = v_ref[...]
    norm_ref[2] = normed(q_ref[...], qg_ref[...]).astype(jnp.bfloat16)
    patches = control_ref[...].astype(jnp.float32)
    slabs = [patches[j * slab_rows : (j + 1) * slab_rows] for j in range(owners)]
    for step, out_ref in zip(steps_of(owners), out_refs):
        to = partner(me, step)
        at = 0
        for i in range(3):
            for head in range(share // HEAD_DIM):
                cols = pl.ds(pl.multiple_of(to * share + head * HEAD_DIM, HEAD_DIM), HEAD_DIM)
                lines = norm_ref[i, :, cols]
                out_ref[at : at + rows] = lines
                if step == 0 and i < 2:
                    own_ref[0, at : at + rows] = lines
                at = at + rows
        slab = slabs[0]
        for j in range(1, owners):
            slab = jnp.where(owner_ref[0, j] == to, slabs[j], slab)
        slab = slab.astype(jnp.bfloat16)
        for tile in range(width // HEAD_DIM):
            out_ref[at : at + slab_rows] = slab[:, tile * HEAD_DIM : (tile + 1) * HEAD_DIM]
            at = at + slab_rows


def sort_kernel(rows, *refs):
    got_refs, (pair_ref, rest_ref, patch_ref) = refs[:-3], refs[-3:]
    owners = len(got_refs)
    slab_rows, width = rows // owners, patch_ref.shape[1]
    size = pair_ref.shape[1]
    start = 3 * size // 2
    for i, ref in enumerate(got_refs):
        pair_ref[i] = ref[:size]
        if i:
            rest_ref[i - 1] = ref[:size]
    slabs = [ref[start:].astype(jnp.float32) for ref in got_refs]
    patches = [
        jnp.concatenate([slab[i * slab_rows : (i + 1) * slab_rows] for slab in slabs], axis=0)
        for i in range(width // HEAD_DIM)
    ]
    patch_ref[...] = normed(jnp.concatenate(patches, axis=1), 1.0).astype(jnp.bfloat16)


def attend_kernel(rows, owners, *refs):
    got_refs, pair_refs, out_refs = refs[:owners], refs[owners:-owners], refs[-owners:]
    heads = out_refs[0].shape[0] // rows
    count = sum(ref.shape[0] for ref in pair_refs) * rows
    group = max(1, min(owners, 2**17 // (rows * count)))
    for head in range(heads):
        at, past, ask = (slice((i * heads + head) * rows, (i * heads + head + 1) * rows) for i in range(3))
        keys = jnp.concatenate([ref[:, at].reshape(-1, HEAD_DIM) for ref in pair_refs], axis=0)
        values = jnp.concatenate([ref[:, past].reshape(-1, HEAD_DIM) for ref in pair_refs], axis=0)
        for first in range(0, owners, group):
            part = range(first, min(first + group, owners))
            queries = jnp.concatenate([got_refs[i][ask] for i in part], axis=0)
            scores = lax.dot_general(
                queries, keys, (((1,), (1,)), ((), ())), preferred_element_type=jnp.float32
            ) * (HEAD_DIM ** (-0.5))
            peak = jnp.max(scores, axis=-1, keepdims=True)
            expo = jnp.exp(scores - peak)
            totals = jnp.sum(expo, axis=-1, keepdims=True)
            mixed = jnp.dot(expo.astype(jnp.bfloat16), values, preferred_element_type=jnp.float32)
            mixed = (mixed / totals).astype(jnp.bfloat16)
            for j, i in enumerate(part):
                out_refs[i][at] = mixed[j * rows : (j + 1) * rows]


def hint_kernel(layer_ref, patch_ref, weight_ref, gain_ref, out_ref):
    owners, slab_rows, _ = out_ref.shape
    hint = jnp.dot(patch_ref[...], weight_ref[...], preferred_element_type=jnp.float32)
    hint = hint.astype(jnp.bfloat16).astype(jnp.float32) * gain_ref[pl.ds(layer_ref[0], 1), :]
    me = lax.axis_index("ulysses")
    for i, step in enumerate(steps_of(owners)):
        out_ref[partner(me, step)] = hint[i * slab_rows : (i + 1) * slab_rows]


def finish_kernel(owners, hint_ref, *refs):
    back_refs, out_ref = refs[:-1], refs[-1]
    rows, feats = out_ref.shape
    share = feats // owners
    me = lax.axis_index("ulysses")
    for step, ref in zip(steps_of(owners), back_refs):
        for head in range(share // HEAD_DIM):
            start = partner(me, step) * share + head * HEAD_DIM
            cols = pl.ds(pl.multiple_of(start, HEAD_DIM), HEAD_DIM)
            attended = ref[head * rows : (head + 1) * rows].astype(jnp.float32)
            out_ref[:, cols] = (attended + hint_ref[:, cols]).astype(jnp.bfloat16)


VMEM = pl.BlockSpec(memory_space=pltpu.VMEM)
SMEM = pl.BlockSpec(memory_space=pltpu.SMEM)
HBM = pl.BlockSpec(memory_space=pltpu.HBM)


def call(kernel, out_shape, specs, *operands, scratch=(), flops=0, nbytes=0):
    return pl.pallas_call(
        kernel,
        out_shape=out_shape,
        in_specs=specs,
        out_specs=jax.tree.map(lambda _: VMEM, out_shape),
        scratch_shapes=scratch,
        compiler_params=pltpu.CompilerParams(vmem_limit_bytes=32 * 2**20),
        cost_estimate=pl.CostEstimate(flops=flops, bytes_accessed=nbytes, transcendentals=0),
    )(*operands)


def shape(dims, dtype=jnp.bfloat16):
    return jax.ShapeDtypeStruct(dims, dtype)


def gather(held, step, axis):
    while step:
        held = held + [swap(array, axis, step) for array in held]
        step = step // 2
    return held


def exchange(arrays, axis):
    return [
        swap(array, axis, step) if step else array
        for step, array in zip(steps_of(lax.axis_size(axis)), arrays)
    ]


def shards(
    query_proj,
    key_proj,
    value_proj,
    query_gain,
    key_gain,
    control,
    hint_weight,
    hint_gain,
    owner_map,
    layer_index,
):
    owners = lax.axis_size("ulysses")
    rows, feats = query_proj.shape
    width = control.shape[1]
    lines = rows * (feats // owners // HEAD_DIM)
    slab_lines = rows // owners * (width // HEAD_DIM)
    sources = (
        owner_map,
        query_proj,
        key_proj,
        value_proj,
        control,
        query_gain.reshape(1, feats),
        key_gain.reshape(1, feats),
    )
    sources = [pltpu.with_memory_space_constraint(source, pltpu.HBM) for source in sources]
    sent = call(
        functools.partial(pack_kernel, owners),
        [shape((3 * lines + slab_lines, HEAD_DIM))] * owners + [shape((1, 2 * lines, HEAD_DIM))],
        [HBM] * len(sources),
        *sources,
        scratch=[pltpu.SMEM(owner_map.shape, owner_map.dtype)]
        + [pltpu.VMEM(source.shape, source.dtype) for source in sources[1:]]
        + [
            pltpu.VMEM((3, rows, feats), jnp.bfloat16),
            pltpu.SemaphoreType.DMA((len(sources),)),
        ],
    )
    half = lax.axis_size("blk") // 2
    own_moved = swap(sent[owners], "blk", half)
    got, own_moved = lax.optimization_barrier((exchange(sent[:owners], "ulysses"), own_moved))
    pairs, rest, patches = call(
        functools.partial(sort_kernel, rows),
        [
            shape((owners, 2 * lines, HEAD_DIM)),
            shape((owners - 1, 2 * lines, HEAD_DIM)),
            shape((rows, width)),
        ],
        [VMEM] * owners,
        *got,
    )
    hint = call(
        hint_kernel,
        shape((owners, rows // owners, feats), jnp.float32),
        [SMEM] + [VMEM] * 3,
        layer_index,
        patches,
        hint_weight,
        hint_gain,
        flops=2 * rows * width * feats,
        nbytes=2 * width * feats,
    )
    moved = swap(rest, "blk", half)
    held = gather([own_moved], half // 2, "blk")
    moved, held, hint = lax.optimization_barrier((moved, held, hint))
    held = held + gather([pairs, moved], half // 2, "blk")
    mixed = call(
        functools.partial(attend_kernel, rows, owners),
        [shape((lines, HEAD_DIM))] * owners,
        [VMEM] * (owners + len(held)),
        *got,
        *held,
        flops=2 * lines * sum(array.size for array in held),
        nbytes=2 * sum(array.size for array in held),
    )
    return call(
        functools.partial(finish_kernel, owners),
        shape((rows, feats)),
        [VMEM] * (owners + 1),
        hint.reshape(rows, feats),
        *exchange(mixed, "ulysses"),
    )


def solution(mesh):
    split = P(("groups", "blk", "ulysses"), None)
    return jax.shard_map(
        shards,
        mesh=mesh,
        in_specs=(
            split,
            split,
            split,
            P(),
            P(),
            split,
            P(),
            P(),
            split,
            P(("groups", "blk", "ulysses")),
        ),
        out_specs=split,
        check_vma=False,
    )
```

```python
import functools

import jax
import jax.numpy as jnp
from jax import lax
from jax.experimental import pallas as pl
from jax.experimental.pallas import tpu as pltpu
from jax.sharding import PartitionSpec as P

HEAD_DIM = 128
EPS = 1e-06


def normed(rows, gain):
    values = rows.astype(jnp.float32)
    scale = lax.rsqrt(jnp.mean(values * values, axis=-1, keepdims=True) + EPS)
    return values * scale * gain


def partner(me, step):
    return me ^ step


def steps_in(owners):
    return sorted(range(owners), key=lambda step: (step > 0, -step.bit_length(), step))


def steps_back(owners):
    return [0, *range(owners - 1, 0, -1)]


def swap(array, axis, step):
    size = lax.axis_size(axis)
    return lax.ppermute(array, axis, [(i, partner(i, step)) for i in range(size)])


def pack_kernel(owners, *refs):
    total = (len(refs) - owners - 3) // 2
    sources, out_refs, own_ref = refs[:total], refs[total : total + owners], refs[total + owners]
    held, (norm_ref, copy_sems) = refs[total + owners + 1 : -2], refs[-2:]
    copies = [
        pltpu.make_async_copy(source, buffer, copy_sems.at[i])
        for i, (source, buffer) in enumerate(zip(sources, held))
    ]
    for copy in copies:
        copy.start()
    owner_ref, q_ref, k_ref, v_ref, control_ref, qg_ref, kg_ref = held
    rows, feats = q_ref.shape
    share = feats // owners
    slab_rows, width = rows // owners, control_ref.shape[1]
    me = lax.axis_index("ulysses")
    for copy in copies:
        copy.wait()
    norm_ref[0] = normed(k_ref[...], kg_ref[...]).astype(jnp.bfloat16)
    norm_ref[1] = v_ref[...]
    norm_ref[2] = normed(q_ref[...], qg_ref[...]).astype(jnp.bfloat16)
    patches = control_ref[...].astype(jnp.float32)
    slabs = [patches[j * slab_rows : (j + 1) * slab_rows] for j in range(owners)]
    for step, out_ref in zip(steps_in(owners), out_refs):
        to = partner(me, step)
        at = 0
        for i in range(3):
            for head in range(share // HEAD_DIM):
                cols = pl.ds(pl.multiple_of(to * share + head * HEAD_DIM, HEAD_DIM), HEAD_DIM)
                lines = norm_ref[i, :, cols]
                out_ref[at : at + rows] = lines
                if step == 0 and i < 2:
                    own_ref[0, at : at + rows] = lines
                at = at + rows
        slab = slabs[0]
        for j in range(1, owners):
            slab = jnp.where(owner_ref[0, j] == to, slabs[j], slab)
        slab = slab.astype(jnp.bfloat16)
        for tile in range(width // HEAD_DIM):
            out_ref[at : at + slab_rows] = slab[:, tile * HEAD_DIM : (tile + 1) * HEAD_DIM]
            at = at + slab_rows


def sort_kernel(rows, *refs):
    got_refs, (pair_ref, rest_ref, patch_ref) = refs[:-3], refs[-3:]
    owners = len(got_refs)
    slab_rows, width = rows // owners, patch_ref.shape[1]
    size = pair_ref.shape[1]
    start = 3 * size // 2
    for i, ref in enumerate(got_refs):
        pair_ref[i] = ref[:size]
        if i:
            rest_ref[i - 1] = ref[:size]
    slabs = [ref[start:].astype(jnp.float32) for ref in got_refs]
    patches = [
        jnp.concatenate([slab[i * slab_rows : (i + 1) * slab_rows] for slab in slabs], axis=0)
        for i in range(width // HEAD_DIM)
    ]
    patch_ref[...] = normed(jnp.concatenate(patches, axis=1), 1.0).astype(jnp.bfloat16)


def fold(rows, got_refs, pair_refs, use):
    owners = len(got_refs)
    heads = pair_refs[0].shape[1] // (2 * rows)
    count = sum(ref.shape[0] for ref in pair_refs) * rows
    group = max(1, min(owners, 2**17 // (rows * count)))
    for head in range(heads):
        at, past, ask = (
            slice((i * heads + head) * rows, (i * heads + head + 1) * rows) for i in range(3)
        )
        keys = jnp.concatenate([ref[:, at].reshape(-1, HEAD_DIM) for ref in pair_refs], axis=0)
        values = jnp.concatenate([ref[:, past].reshape(-1, HEAD_DIM) for ref in pair_refs], axis=0)
        for first in range(0, owners, group):
            queries = [ref[ask] for ref in got_refs[first : first + group]]
            scores = lax.dot_general(
                jnp.concatenate(queries, axis=0),
                keys,
                (((1,), (1,)), ((), ())),
                preferred_element_type=jnp.float32,
            ) * (HEAD_DIM ** (-0.5))
            use(head, first, len(queries), scores, values)


def weigh(scores, peak, values):
    expo = jnp.exp(scores - peak)
    mixed = jnp.dot(expo.astype(jnp.bfloat16), values, preferred_element_type=jnp.float32)
    return jnp.sum(expo, axis=-1, keepdims=True), mixed


def early_kernel(rows, owners, *refs):
    peak_ref, total_ref, accum_ref = refs[-3:]

    def use(head, first, many, scores, values):
        at = slice(first * rows, (first + many) * rows)
        peak = jnp.max(scores, axis=-1, keepdims=True)
        peak_ref[head, at] = peak
        total_ref[head, at], accum_ref[head, at] = weigh(scores, peak, values)

    fold(rows, refs[:owners], refs[owners:-3], use)


def late_kernel(rows, owners, *refs):
    (peak_ref, total_ref, accum_ref), refs = refs[:3], refs[3:]
    out_refs = refs[-owners:]
    places = [steps_in(owners).index(step) for step in steps_back(owners)]

    def use(head, first, many, scores, values):
        at = slice(first * rows, (first + many) * rows)
        before = peak_ref[head, at]
        peak = jnp.maximum(before, jnp.max(scores, axis=-1, keepdims=True))
        totals, mixed = weigh(scores, peak, values)
        correction = jnp.exp(before - peak)
        totals = total_ref[head, at] * correction + totals
        mixed = (accum_ref[head, at] * correction + mixed) / totals
        mixed = mixed.astype(jnp.bfloat16)
        for i in range(many):
            out_ref = out_refs[places.index(first + i)]
            out_ref[head * rows : (head + 1) * rows] = mixed[i * rows : (i + 1) * rows]

    fold(rows, refs[:owners], refs[owners:-owners], use)


def hint_kernel(layer_ref, patch_ref, weight_ref, gain_ref, out_ref):
    owners, slab_rows, _ = out_ref.shape
    hint = jnp.dot(patch_ref[...], weight_ref[...], preferred_element_type=jnp.float32)
    hint = hint.astype(jnp.bfloat16).astype(jnp.float32) * gain_ref[pl.ds(layer_ref[0], 1), :]
    me = lax.axis_index("ulysses")
    for i, step in enumerate(steps_in(owners)):
        out_ref[partner(me, step)] = hint[i * slab_rows : (i + 1) * slab_rows]


def finish_kernel(owners, hint_ref, *refs):
    back_refs, out_ref = refs[:-1], refs[-1]
    rows, feats = out_ref.shape
    share = feats // owners
    me = lax.axis_index("ulysses")
    for step, ref in zip(steps_back(owners), back_refs):
        for head in range(share // HEAD_DIM):
            start = partner(me, step) * share + head * HEAD_DIM
            cols = pl.ds(pl.multiple_of(start, HEAD_DIM), HEAD_DIM)
            attended = ref[head * rows : (head + 1) * rows].astype(jnp.float32)
            out_ref[:, cols] = (attended + hint_ref[:, cols]).astype(jnp.bfloat16)


VMEM = pl.BlockSpec(memory_space=pltpu.VMEM)
SMEM = pl.BlockSpec(memory_space=pltpu.SMEM)
HBM = pl.BlockSpec(memory_space=pltpu.HBM)


def call(kernel, out_shape, specs, *operands, scratch=(), flops=0, nbytes=0):
    return pl.pallas_call(
        kernel,
        out_shape=out_shape,
        in_specs=specs,
        out_specs=jax.tree.map(lambda _: VMEM, out_shape),
        scratch_shapes=scratch,
        compiler_params=pltpu.CompilerParams(vmem_limit_bytes=32 * 2**20),
        cost_estimate=pl.CostEstimate(flops=flops, bytes_accessed=nbytes, transcendentals=0),
    )(*operands)


def shape(dims, dtype=jnp.bfloat16):
    return jax.ShapeDtypeStruct(dims, dtype)


def gather(held, step, axis):
    while step:
        held = held + [swap(array, axis, step) for array in held]
        step = step // 2
    return held


def exchange(arrays, steps, axis):
    return [swap(array, axis, step) if step else array for step, array in zip(steps, arrays)]


def shards(
    query_proj,
    key_proj,
    value_proj,
    query_gain,
    key_gain,
    control,
    hint_weight,
    hint_gain,
    owner_map,
    layer_index,
):
    owners = lax.axis_size("ulysses")
    rows, feats = query_proj.shape
    width = control.shape[1]
    lines = rows * (feats // owners // HEAD_DIM)
    slab_lines = rows // owners * (width // HEAD_DIM)
    sources = (
        owner_map,
        query_proj,
        key_proj,
        value_proj,
        control,
        query_gain.reshape(1, feats),
        key_gain.reshape(1, feats),
    )
    sources = [pltpu.with_memory_space_constraint(source, pltpu.HBM) for source in sources]
    sent = call(
        functools.partial(pack_kernel, owners),
        [shape((3 * lines + slab_lines, HEAD_DIM))] * owners + [shape((1, 2 * lines, HEAD_DIM))],
        [HBM] * len(sources),
        *sources,
        scratch=[pltpu.SMEM(owner_map.shape, owner_map.dtype)]
        + [pltpu.VMEM(source.shape, source.dtype) for source in sources[1:]]
        + [
            pltpu.VMEM((3, rows, feats), jnp.bfloat16),
            pltpu.SemaphoreType.DMA((len(sources),)),
        ],
    )
    half = lax.axis_size("blk") // 2
    own_moved = swap(sent[owners], "blk", half)
    got, own_moved = lax.optimization_barrier((exchange(sent[:owners], steps_in(owners), "ulysses"), own_moved))
    pairs, rest, patches = call(
        functools.partial(sort_kernel, rows),
        [
            shape((owners, 2 * lines, HEAD_DIM)),
            shape((owners - 1, 2 * lines, HEAD_DIM)),
            shape((rows, width)),
        ],
        [VMEM] * owners,
        *got,
    )
    hint = call(
        hint_kernel,
        shape((owners, rows // owners, feats), jnp.float32),
        [SMEM] + [VMEM] * 3,
        layer_index,
        patches,
        hint_weight,
        hint_gain,
        flops=2 * rows * width * feats,
        nbytes=2 * width * feats,
    )
    moved = swap(rest, "blk", half)
    held = gather([own_moved], half // 2, "blk")
    moved, held, hint = lax.optimization_barrier((moved, held, hint))
    moved = gather([moved], half // 2, "blk")
    early = held + gather([pairs], half // 2, "blk") + moved[: len(moved) // 2]
    late = moved[len(moved) // 2 :]
    heads, asks = lines // rows, owners * rows
    state = call(
        functools.partial(early_kernel, rows, owners),
        [
            shape((heads, asks, 1), jnp.float32),
            shape((heads, asks, 1), jnp.float32),
            shape((heads, asks, HEAD_DIM), jnp.float32),
        ],
        [VMEM] * (owners + len(early)),
        *got,
        *early,
        flops=2 * asks * sum(array.size for array in early),
        nbytes=2 * sum(array.size for array in early),
    )
    mixed = call(
        functools.partial(late_kernel, rows, owners),
        [shape((lines, HEAD_DIM))] * owners,
        [VMEM] * (3 + owners + len(late)),
        *state,
        *got,
        *late,
        flops=2 * asks * sum(array.size for array in late),
        nbytes=2 * sum(array.size for array in late),
    )
    return call(
        functools.partial(finish_kernel, owners),
        shape((rows, feats)),
        [VMEM] * (owners + 1),
        hint.reshape(rows, feats),
        *exchange(mixed, steps_back(owners), "ulysses"),
    )


def solution(mesh):
    split = P(("groups", "blk", "ulysses"), None)
    return jax.shard_map(
        shards,
        mesh=mesh,
        in_specs=(
            split,
            split,
            split,
            P(),
            P(),
            split,
            P(),
            P(),
            split,
            P(("groups", "blk", "ulysses")),
        ),
        out_specs=split,
        check_vma=False,
    )
```

```python
import functools

import jax
import jax.numpy as jnp
from jax import lax
from jax.experimental import pallas as pl
from jax.experimental.pallas import tpu as pltpu
from jax.sharding import PartitionSpec as P

HEAD_DIM = 128
EPS = 1e-06


def normed(rows, gain):
    values = rows.astype(jnp.float32)
    scale = lax.rsqrt(jnp.mean(values * values, axis=-1, keepdims=True) + EPS)
    return values * scale * gain


def partner(me, step):
    return me ^ step


def steps_in(owners):
    return sorted(range(owners), key=lambda step: (step > 0, -step.bit_length(), step))


def steps_back(owners):
    return [0, *range(owners - 1, 0, -1)]


def swap(array, axis, step):
    size = lax.axis_size(axis)
    return lax.ppermute(array, axis, [(i, partner(i, step)) for i in range(size)])


def pack_kernel(owners, *refs):
    total = (len(refs) - owners - 3) // 2
    sources, out_refs, own_ref = refs[:total], refs[total : total + owners], refs[total + owners]
    held, (norm_ref, copy_sems) = refs[total + owners + 1 : -2], refs[-2:]
    copies = [
        pltpu.make_async_copy(source, buffer, copy_sems.at[i])
        for i, (source, buffer) in enumerate(zip(sources, held))
    ]
    for copy in copies:
        copy.start()
    kg_ref, k_ref, qg_ref, q_ref, v_ref, owner_ref, control_ref = held
    rows, feats = q_ref.shape
    share = feats // owners
    slab_rows, width = rows // owners, control_ref.shape[1]
    me = lax.axis_index("ulysses")
    copies[0].wait()
    copies[1].wait()
    norm_ref[0] = normed(k_ref[...], kg_ref[...]).astype(jnp.bfloat16)
    copies[2].wait()
    copies[3].wait()
    norm_ref[2] = normed(q_ref[...], qg_ref[...]).astype(jnp.bfloat16)
    for copy in copies[4:]:
        copy.wait()
    norm_ref[1] = v_ref[...]
    patches = control_ref[...].astype(jnp.float32)
    slabs = [patches[j * slab_rows : (j + 1) * slab_rows] for j in range(owners)]
    for step, out_ref in zip(steps_in(owners), out_refs):
        to = partner(me, step)
        at = 0
        for i in range(3):
            for head in range(share // HEAD_DIM):
                cols = pl.ds(pl.multiple_of(to * share + head * HEAD_DIM, HEAD_DIM), HEAD_DIM)
                lines = norm_ref[i, :, cols]
                out_ref[at : at + rows] = lines
                if step == 0 and i < 2:
                    own_ref[0, at : at + rows] = lines
                at = at + rows
        slab = slabs[0]
        for j in range(1, owners):
            slab = jnp.where(owner_ref[0, j] == to, slabs[j], slab)
        slab = slab.astype(jnp.bfloat16)
        for tile in range(width // HEAD_DIM):
            out_ref[at : at + slab_rows] = slab[:, tile * HEAD_DIM : (tile + 1) * HEAD_DIM]
            at = at + slab_rows


def sort_kernel(rows, *refs):
    got_refs, (pair_ref, rest_ref, patch_ref) = refs[:-3], refs[-3:]
    owners = len(got_refs)
    slab_rows, width = rows // owners, patch_ref.shape[1]
    size = pair_ref.shape[1]
    start = 3 * size // 2
    for i, ref in enumerate(got_refs):
        pair_ref[i] = ref[:size]
        if i:
            rest_ref[i - 1] = ref[:size]
    slabs = [ref[start:].astype(jnp.float32) for ref in got_refs]
    patches = [
        jnp.concatenate([slab[i * slab_rows : (i + 1) * slab_rows] for slab in slabs], axis=0)
        for i in range(width // HEAD_DIM)
    ]
    patch_ref[...] = normed(jnp.concatenate(patches, axis=1), 1.0).astype(jnp.bfloat16)


def fold(rows, got_refs, pair_refs, use):
    owners = len(got_refs)
    heads = pair_refs[0].shape[1] // (2 * rows)
    count = sum(ref.shape[0] for ref in pair_refs) * rows
    group = max(1, min(owners, 2**17 // (rows * count)))
    spans = [slice(i * rows, (i + 1) * rows) for i in range(2 * heads)]
    pieces = [
        jnp.concatenate([ref[:, span].reshape(-1, HEAD_DIM) for ref in pair_refs], axis=0)
        for span in spans
    ]
    ones = jnp.ones((count, HEAD_DIM), jnp.bfloat16)
    values = [jnp.concatenate([piece, ones], axis=1) for piece in pieces[heads:]]
    for first in range(0, owners, group):
        many = min(group, owners - first)
        scores = []
        for head in range(heads):
            ask = spans[0].stop * (2 * heads + head)
            queries = [ref[ask : ask + rows] for ref in got_refs[first : first + many]]
            scores.append(
                lax.dot_general(
                    jnp.concatenate(queries, axis=0),
                    pieces[head],
                    (((1,), (1,)), ((), ())),
                    preferred_element_type=jnp.float32,
                )
            )
        scores = jnp.concatenate(scores, axis=0) * (HEAD_DIM ** (-0.5))
        use(slice(first * rows, (first + many) * rows), scores, values)


def weigh(scores, peak, values):
    probs = jnp.exp(scores - peak).astype(jnp.bfloat16)
    each = probs.shape[0] // len(values)
    mixed = [
        jnp.dot(
            probs[i * each : (i + 1) * each], value, preferred_element_type=jnp.float32
        )
        for i, value in enumerate(values)
    ]
    mixed = jnp.concatenate(mixed, axis=0)
    return mixed[:, HEAD_DIM:], mixed[:, :HEAD_DIM]


def early_kernel(rows, owners, *refs):
    state_refs = refs[-3:]

    def use(at, scores, values):
        peak = jnp.max(scores, axis=-1, keepdims=True)
        totals, mixed = weigh(scores, peak, values)
        each = mixed.shape[0] // len(values)
        for ref, state in zip(state_refs, (jnp.broadcast_to(peak, mixed.shape), totals, mixed)):
            for head in range(len(values)):
                ref[head, at] = state[head * each : (head + 1) * each]

    fold(rows, refs[:owners], refs[owners:-3], use)


def late_kernel(rows, owners, *refs):
    state_refs, refs = refs[:3], refs[3:]
    out_refs = refs[-owners:]
    places = [steps_back(owners).index(step) for step in steps_in(owners)]

    def use(at, scores, values):
        heads = range(len(values))
        before, totals, accum = (
            jnp.concatenate([ref[head, at] for head in heads], axis=0) for ref in state_refs
        )
        most = jnp.max(scores, axis=-1, keepdims=True)
        peak = jnp.maximum(before, most)
        correction = jnp.exp(before - peak)
        keys = scores.shape[1]
        new_totals, mixed = weigh(scores, peak[:, : keys if keys < HEAD_DIM else 1], values)
        mixed = (accum * correction + mixed) / (totals * correction + new_totals)
        mixed = mixed.astype(jnp.bfloat16)
        many = (at.stop - at.start) // rows
        for i in range(len(values) * many):
            head, source = divmod(i, many)
            out_ref = out_refs[places[at.start // rows + source]]
            out_ref[head * rows : (head + 1) * rows] = mixed[i * rows : (i + 1) * rows]

    fold(rows, refs[:owners], refs[owners:-owners], use)


def hint_kernel(layer_ref, patch_ref, weight_ref, gain_ref, out_ref):
    owners, slab_rows, _ = out_ref.shape
    hint = jnp.dot(patch_ref[...], weight_ref[...], preferred_element_type=jnp.float32)
    hint = hint.astype(jnp.bfloat16).astype(jnp.float32) * gain_ref[pl.ds(layer_ref[0], 1), :]
    me = lax.axis_index("ulysses")
    for i, step in enumerate(steps_in(owners)):
        out_ref[partner(me, step)] = hint[i * slab_rows : (i + 1) * slab_rows]


def finish_kernel(owners, hint_ref, *refs):
    back_refs, out_ref = refs[:-1], refs[-1]
    rows, feats = out_ref.shape
    share = feats // owners
    me = lax.axis_index("ulysses")
    for step, ref in zip(steps_back(owners), back_refs):
        for head in range(share // HEAD_DIM):
            start = partner(me, step) * share + head * HEAD_DIM
            cols = pl.ds(pl.multiple_of(start, HEAD_DIM), HEAD_DIM)
            attended = ref[head * rows : (head + 1) * rows].astype(jnp.float32)
            out_ref[:, cols] = (attended + hint_ref[:, cols]).astype(jnp.bfloat16)


VMEM = pl.BlockSpec(memory_space=pltpu.VMEM)
SMEM = pl.BlockSpec(memory_space=pltpu.SMEM)
HBM = pl.BlockSpec(memory_space=pltpu.HBM)


def call(kernel, out_shape, specs, *operands, scratch=(), flops=0, nbytes=0):
    return pl.pallas_call(
        kernel,
        out_shape=out_shape,
        in_specs=specs,
        out_specs=jax.tree.map(lambda _: VMEM, out_shape),
        scratch_shapes=scratch,
        compiler_params=pltpu.CompilerParams(vmem_limit_bytes=32 * 2**20),
        cost_estimate=pl.CostEstimate(flops=flops, bytes_accessed=nbytes, transcendentals=0),
    )(*operands)


def shape(dims, dtype=jnp.bfloat16):
    return jax.ShapeDtypeStruct(dims, dtype)


def gather(held, step, axis):
    while step:
        held = held + [swap(array, axis, step) for array in held]
        step = step // 2
    return held


def exchange(arrays, steps, axis):
    return [swap(array, axis, step) if step else array for step, array in zip(steps, arrays)]


def shards(
    query_proj,
    key_proj,
    value_proj,
    query_gain,
    key_gain,
    control,
    hint_weight,
    hint_gain,
    owner_map,
    layer_index,
):
    owners = lax.axis_size("ulysses")
    rows, feats = query_proj.shape
    width = control.shape[1]
    lines = rows * (feats // owners // HEAD_DIM)
    slab_lines = rows // owners * (width // HEAD_DIM)
    sources = (
        key_gain.reshape(1, feats),
        key_proj,
        query_gain.reshape(1, feats),
        query_proj,
        value_proj,
        owner_map,
        control,
    )
    sources = [pltpu.with_memory_space_constraint(source, pltpu.HBM) for source in sources]
    sent = call(
        functools.partial(pack_kernel, owners),
        [shape((3 * lines + slab_lines, HEAD_DIM))] * owners + [shape((1, 2 * lines, HEAD_DIM))],
        [HBM] * len(sources),
        *sources,
        scratch=[
            (pltpu.SMEM if source.dtype == jnp.int32 else pltpu.VMEM)(source.shape, source.dtype)
            for source in sources
        ]
        + [
            pltpu.VMEM((3, rows, feats), jnp.bfloat16),
            pltpu.SemaphoreType.DMA((len(sources),)),
        ],
    )
    half = lax.axis_size("blk") // 2
    own_moved = swap(sent[owners], "blk", half)
    got, own_moved = lax.optimization_barrier((exchange(sent[:owners], steps_in(owners), "ulysses"), own_moved))
    pairs, rest, patches = call(
        functools.partial(sort_kernel, rows),
        [
            shape((owners, 2 * lines, HEAD_DIM)),
            shape((owners - 1, 2 * lines, HEAD_DIM)),
            shape((rows, width)),
        ],
        [VMEM] * owners,
        *got,
    )
    hint = call(
        hint_kernel,
        shape((owners, rows // owners, feats), jnp.float32),
        [SMEM] + [VMEM] * 3,
        layer_index,
        patches,
        hint_weight,
        hint_gain,
        flops=2 * rows * width * feats,
        nbytes=2 * width * feats,
    )
    moved = swap(rest, "blk", half)
    held = gather([own_moved], half // 2, "blk")
    moved, held, hint = lax.optimization_barrier((moved, held, hint))
    moved = gather([moved], half // 2, "blk")
    early = held + gather([pairs], half // 2, "blk") + moved[: len(moved) // 2]
    late = moved[len(moved) // 2 :]
    heads, asks = lines // rows, owners * rows
    state = call(
        functools.partial(early_kernel, rows, owners),
        [
            shape((heads, asks, HEAD_DIM), jnp.float32),
        ]
        * 3,
        [VMEM] * (owners + len(early)),
        *got,
        *early,
        flops=2 * asks * sum(array.size for array in early),
        nbytes=2 * sum(array.size for array in early),
    )
    mixed = call(
        functools.partial(late_kernel, rows, owners),
        [shape((lines, HEAD_DIM))] * owners,
        [VMEM] * (3 + owners + len(late)),
        *state,
        *got,
        *late,
        flops=2 * asks * sum(array.size for array in late),
        nbytes=2 * sum(array.size for array in late),
    )
    return call(
        functools.partial(finish_kernel, owners),
        shape((rows, feats)),
        [VMEM] * (owners + 1),
        hint.reshape(rows, feats),
        *exchange(mixed, steps_back(owners), "ulysses"),
    )


def solution(mesh):
    split = P(("groups", "blk", "ulysses"), None)
    return jax.shard_map(
        shards,
        mesh=mesh,
        in_specs=(
            split,
            split,
            split,
            P(),
            P(),
            split,
            P(),
            P(),
            split,
            P(("groups", "blk", "ulysses")),
        ),
        out_specs=split,
        check_vma=False,
    )
```

```python
import functools

import jax
import jax.numpy as jnp
from jax import lax
from jax.experimental import pallas as pl
from jax.experimental.pallas import tpu as pltpu
from jax.sharding import PartitionSpec as P

HEAD_DIM = 128
EPS = 1e-06


def normed(rows, gain):
    values = rows.astype(jnp.float32)
    scale = lax.rsqrt(jnp.mean(values * values, axis=-1, keepdims=True) + EPS)
    return values * scale * gain


def partner(me, step):
    return me ^ step


def steps_in(owners):
    return sorted(range(owners), key=lambda step: (step > 0, -step.bit_length(), step))


def steps_back(owners):
    return [0, *range(owners - 1, 0, -1)]


def swap(array, axis, step):
    size = lax.axis_size(axis)
    return lax.ppermute(array, axis, [(i, partner(i, step)) for i in range(size)])


def pack_kernel(owners, *refs):
    total = (len(refs) - owners - 3) // 2
    sources, out_refs, own_ref = refs[:total], refs[total : total + owners], refs[total + owners]
    held, (norm_ref, copy_sems) = refs[total + owners + 1 : -2], refs[-2:]
    copies = [
        pltpu.make_async_copy(source, buffer, copy_sems.at[i])
        for i, (source, buffer) in enumerate(zip(sources, held))
    ]
    for copy in copies:
        copy.start()
    kg_ref, k_ref, qg_ref, q_ref, v_ref, owner_ref, control_ref = held
    rows, feats = q_ref.shape
    share = feats // owners
    slab_rows, width = rows // owners, control_ref.shape[1]
    me = lax.axis_index("ulysses")
    copies[0].wait()
    copies[1].wait()
    norm_ref[0] = normed(k_ref[...], kg_ref[...]).astype(jnp.bfloat16)
    copies[2].wait()
    copies[3].wait()
    norm_ref[2] = normed(q_ref[...], qg_ref[...]).astype(jnp.bfloat16)
    for copy in copies[4:]:
        copy.wait()
    norm_ref[1] = v_ref[...]
    patches = control_ref[...].astype(jnp.float32)
    slabs = [patches[j * slab_rows : (j + 1) * slab_rows] for j in range(owners)]
    for step, out_ref in zip(steps_in(owners), out_refs):
        to = partner(me, step)
        at = 0
        for i in range(3):
            for head in range(share // HEAD_DIM):
                cols = pl.ds(pl.multiple_of(to * share + head * HEAD_DIM, HEAD_DIM), HEAD_DIM)
                lines = norm_ref[i, :, cols]
                out_ref[at : at + rows] = lines
                if step == 0 and i < 2:
                    own_ref[0, at : at + rows] = lines
                at = at + rows
        slab = slabs[0]
        for j in range(1, owners):
            slab = jnp.where(owner_ref[0, j] == to, slabs[j], slab)
        slab = slab.astype(jnp.bfloat16)
        for tile in range(width // HEAD_DIM):
            out_ref[at : at + slab_rows] = slab[:, tile * HEAD_DIM : (tile + 1) * HEAD_DIM]
            at = at + slab_rows


def sort_kernel(rows, *refs):
    got_refs, (pair_ref, rest_ref, patch_ref) = refs[:-3], refs[-3:]
    owners = len(got_refs)
    slab_rows, width = rows // owners, patch_ref.shape[1]
    size = pair_ref.shape[1]
    start = 3 * size // 2
    for i, ref in enumerate(got_refs):
        pair_ref[i] = ref[:size]
        if i:
            rest_ref[i - 1] = ref[:size]
    slabs = [ref[start:].astype(jnp.float32) for ref in got_refs]
    patches = [
        jnp.concatenate([slab[i * slab_rows : (i + 1) * slab_rows] for slab in slabs], axis=0)
        for i in range(width // HEAD_DIM)
    ]
    patch_ref[...] = normed(jnp.concatenate(patches, axis=1), 1.0).astype(jnp.bfloat16)


def fold(rows, got_refs, pair_refs, sides, use):
    owners = len(got_refs)
    heads = pair_refs[0].shape[1] // (2 * rows)
    whole, odd, even = pair_refs[: -2 * sides], pair_refs[-2 * sides : -sides], pair_refs[-sides:]
    count = sum(ref.shape[0] for ref in (*whole, *odd)) * rows
    group = max(1, min(owners, 2**17 // (rows * count)))
    spans = [slice(i * rows, (i + 1) * rows) for i in range(2 * heads)]
    pieces = []
    for span in spans:
        parts = [ref[:, span] for ref in whole]
        parts = parts + [one[:, span] + other[:, span] for one, other in zip(odd, even)]
        pieces.append(jnp.concatenate([part.reshape(-1, HEAD_DIM) for part in parts], axis=0))
    ones = jnp.ones((count, HEAD_DIM), jnp.bfloat16)
    values = [jnp.concatenate([piece, ones], axis=1) for piece in pieces[heads:]]
    for first in range(0, owners, group):
        many = min(group, owners - first)
        scores = []
        for head in range(heads):
            ask = spans[0].stop * (2 * heads + head)
            queries = [ref[ask : ask + rows] for ref in got_refs[first : first + many]]
            scores.append(
                lax.dot_general(
                    jnp.concatenate(queries, axis=0),
                    pieces[head],
                    (((1,), (1,)), ((), ())),
                    preferred_element_type=jnp.float32,
                )
            )
        scores = jnp.concatenate(scores, axis=0) * (HEAD_DIM ** (-0.5))
        use(slice(first * rows, (first + many) * rows), scores, values)


def weigh(scores, peak, values):
    probs = jnp.exp(scores - peak).astype(jnp.bfloat16)
    each = probs.shape[0] // len(values)
    mixed = [
        jnp.dot(
            probs[i * each : (i + 1) * each], value, preferred_element_type=jnp.float32
        )
        for i, value in enumerate(values)
    ]
    mixed = jnp.concatenate(mixed, axis=0)
    return mixed[:, HEAD_DIM:], mixed[:, :HEAD_DIM]


def early_kernel(rows, owners, sides, *refs):
    state_refs = refs[-3:]

    def use(at, scores, values):
        peak = jnp.max(scores, axis=-1, keepdims=True)
        totals, mixed = weigh(scores, peak, values)
        each = mixed.shape[0] // len(values)
        for ref, state in zip(state_refs, (jnp.broadcast_to(peak, mixed.shape), totals, mixed)):
            for head in range(len(values)):
                ref[head, at] = state[head * each : (head + 1) * each]

    fold(rows, refs[:owners], refs[owners:-3], sides, use)


def late_kernel(rows, owners, sides, *refs):
    state_refs, refs = refs[:3], refs[3:]
    out_refs = refs[-owners:]
    places = [steps_back(owners).index(step) for step in steps_in(owners)]

    def use(at, scores, values):
        heads = range(len(values))
        before, totals, accum = (
            jnp.concatenate([ref[head, at] for head in heads], axis=0) for ref in state_refs
        )
        most = jnp.max(scores, axis=-1, keepdims=True)
        peak = jnp.maximum(before, most)
        correction = jnp.exp(before - peak)
        keys = scores.shape[1]
        new_totals, mixed = weigh(scores, peak[:, : keys if keys < HEAD_DIM else 1], values)
        mixed = (accum * correction + mixed) / (totals * correction + new_totals)
        mixed = mixed.astype(jnp.bfloat16)
        many = (at.stop - at.start) // rows
        for i in range(len(values) * many):
            head, source = divmod(i, many)
            out_ref = out_refs[places[at.start // rows + source]]
            out_ref[head * rows : (head + 1) * rows] = mixed[i * rows : (i + 1) * rows]

    fold(rows, refs[:owners], refs[owners:-owners], sides, use)


def hint_kernel(layer_ref, patch_ref, weight_ref, gain_ref, out_ref):
    owners, slab_rows, _ = out_ref.shape
    hint = jnp.dot(patch_ref[...], weight_ref[...], preferred_element_type=jnp.float32)
    hint = hint.astype(jnp.bfloat16).astype(jnp.float32) * gain_ref[pl.ds(layer_ref[0], 1), :]
    me = lax.axis_index("ulysses")
    for i, step in enumerate(steps_in(owners)):
        out_ref[partner(me, step)] = hint[i * slab_rows : (i + 1) * slab_rows]


def finish_kernel(owners, hint_ref, *refs):
    back_refs, out_ref = refs[:-1], refs[-1]
    rows, feats = out_ref.shape
    share = feats // owners
    me = lax.axis_index("ulysses")
    for step, ref in zip(steps_back(owners), back_refs):
        for head in range(share // HEAD_DIM):
            start = partner(me, step) * share + head * HEAD_DIM
            cols = pl.ds(pl.multiple_of(start, HEAD_DIM), HEAD_DIM)
            attended = ref[head * rows : (head + 1) * rows].astype(jnp.float32)
            out_ref[:, cols] = (attended + hint_ref[:, cols]).astype(jnp.bfloat16)


VMEM = pl.BlockSpec(memory_space=pltpu.VMEM)
SMEM = pl.BlockSpec(memory_space=pltpu.SMEM)
HBM = pl.BlockSpec(memory_space=pltpu.HBM)


def call(kernel, out_shape, specs, *operands, scratch=(), flops=0, nbytes=0):
    return pl.pallas_call(
        kernel,
        out_shape=out_shape,
        in_specs=specs,
        out_specs=jax.tree.map(lambda _: VMEM, out_shape),
        scratch_shapes=scratch,
        compiler_params=pltpu.CompilerParams(vmem_limit_bytes=32 * 2**20),
        cost_estimate=pl.CostEstimate(flops=flops, bytes_accessed=nbytes, transcendentals=0),
    )(*operands)


def shape(dims, dtype=jnp.bfloat16):
    return jax.ShapeDtypeStruct(dims, dtype)


def gather(held, step, axis):
    while step:
        held = held + [swap(array, axis, step) for array in held]
        step = step // 2
    return held


def swap_side(array, axis, step, side):
    size = lax.axis_size(axis)
    return lax.ppermute(array, axis, [(i, partner(i, step)) for i in range(side, size, 2)])


def gather_side(array, axis, side):
    held, step = [array], lax.axis_size(axis) // 2
    while step > 1:
        held = held + [swap_side(array, axis, step, side) for array in held]
        step = step // 2
    return held[1:]


def exchange(arrays, steps, axis):
    return [swap(array, axis, step) if step else array for step, array in zip(steps, arrays)]


def shards(
    query_proj,
    key_proj,
    value_proj,
    query_gain,
    key_gain,
    control,
    hint_weight,
    hint_gain,
    owner_map,
    layer_index,
):
    owners = lax.axis_size("ulysses")
    rows, feats = query_proj.shape
    width = control.shape[1]
    lines = rows * (feats // owners // HEAD_DIM)
    slab_lines = rows // owners * (width // HEAD_DIM)
    sources = (
        key_gain.reshape(1, feats),
        key_proj,
        query_gain.reshape(1, feats),
        query_proj,
        value_proj,
        owner_map,
        control,
    )
    sources = [pltpu.with_memory_space_constraint(source, pltpu.HBM) for source in sources]
    sent = call(
        functools.partial(pack_kernel, owners),
        [shape((3 * lines + slab_lines, HEAD_DIM))] * owners + [shape((1, 2 * lines, HEAD_DIM))],
        [HBM] * len(sources),
        *sources,
        scratch=[
            (pltpu.SMEM if source.dtype == jnp.int32 else pltpu.VMEM)(source.shape, source.dtype)
            for source in sources
        ]
        + [
            pltpu.VMEM((3, rows, feats), jnp.bfloat16),
            pltpu.SemaphoreType.DMA((len(sources),)),
        ],
    )
    half = lax.axis_size("blk") // 2
    own_moved = swap(sent[owners], "blk", half)
    got, own_moved = lax.optimization_barrier((exchange(sent[:owners], steps_in(owners), "ulysses"), own_moved))
    pairs, rest, patches = call(
        functools.partial(sort_kernel, rows),
        [
            shape((owners, 2 * lines, HEAD_DIM)),
            shape((owners - 1, 2 * lines, HEAD_DIM)),
            shape((rows, width)),
        ],
        [VMEM] * owners,
        *got,
    )
    hint = call(
        hint_kernel,
        shape((owners, rows // owners, feats), jnp.float32),
        [SMEM] + [VMEM] * 3,
        layer_index,
        patches,
        hint_weight,
        hint_gain,
        flops=2 * rows * width * feats,
        nbytes=2 * width * feats,
    )
    held = gather([own_moved], half // 2, "blk")
    odd, even = (gather_side(rest, "blk", side) for side in (1, 0))
    odd_sent = [swap_side(array, "blk", 1, 1) for array in odd]
    even, odd_sent, held, hint = lax.optimization_barrier((even, odd_sent, held, hint))
    even_sent = [swap_side(array, "blk", 1, 0) for array in even]
    early = held + gather([pairs], half // 2, "blk") + odd + even
    late = odd_sent + even_sent
    heads, asks = lines // rows, owners * rows
    state = call(
        functools.partial(early_kernel, rows, owners, len(odd)),
        [
            shape((heads, asks, HEAD_DIM), jnp.float32),
        ]
        * 3,
        [VMEM] * (owners + len(early)),
        *got,
        *early,
        flops=2 * asks * sum(array.size for array in early),
        nbytes=2 * sum(array.size for array in early),
    )
    mixed = call(
        functools.partial(late_kernel, rows, owners, len(late) // 2),
        [shape((lines, HEAD_DIM))] * owners,
        [VMEM] * (3 + owners + len(late)),
        *state,
        *got,
        *late,
        flops=2 * asks * sum(array.size for array in late),
        nbytes=2 * sum(array.size for array in late),
    )
    return call(
        functools.partial(finish_kernel, owners),
        shape((rows, feats)),
        [VMEM] * (owners + 1),
        hint.reshape(rows, feats),
        *exchange(mixed, steps_back(owners), "ulysses"),
    )


def solution(mesh):
    split = P(("groups", "blk", "ulysses"), None)
    return jax.shard_map(
        shards,
        mesh=mesh,
        in_specs=(
            split,
            split,
            split,
            P(),
            P(),
            split,
            P(),
            P(),
            split,
            P(("groups", "blk", "ulysses")),
        ),
        out_specs=split,
        check_vma=False,
    )
```

```python
import functools

import jax
import jax.numpy as jnp
from jax import lax
from jax.experimental import pallas as pl
from jax.experimental.pallas import tpu as pltpu
from jax.sharding import PartitionSpec as P

HEAD_DIM = 128
EPS = 1e-06


def normed(rows, gain):
    values = rows.astype(jnp.float32)
    scale = lax.rsqrt(jnp.mean(values * values, axis=-1, keepdims=True) + EPS)
    return values * scale * gain


def partner(me, step):
    return me ^ step


def steps_in(owners):
    return sorted(range(owners), key=lambda step: (step > 0, -step.bit_length(), step))


def step_pairs(owners):
    return range(2, owners, 2)


def swap(array, axis, step):
    size = lax.axis_size(axis)
    return lax.ppermute(array, axis, [(i, partner(i, step)) for i in range(size)])


def pack_kernel(owners, *refs):
    total = (len(refs) - owners - 3) // 2
    sources, out_refs, own_ref = refs[:total], refs[total : total + owners], refs[total + owners]
    held, (norm_ref, copy_sems) = refs[total + owners + 1 : -2], refs[-2:]
    copies = [
        pltpu.make_async_copy(source, buffer, copy_sems.at[i])
        for i, (source, buffer) in enumerate(zip(sources, held))
    ]
    for copy in copies:
        copy.start()
    kg_ref, k_ref, qg_ref, q_ref, v_ref, owner_ref, control_ref = held
    rows, feats = q_ref.shape
    share = feats // owners
    slab_rows, width = rows // owners, control_ref.shape[1]
    me = lax.axis_index("ulysses")
    copies[0].wait()
    copies[1].wait()
    norm_ref[0] = normed(k_ref[...], kg_ref[...]).astype(jnp.bfloat16)
    copies[2].wait()
    copies[3].wait()
    norm_ref[2] = normed(q_ref[...], qg_ref[...]).astype(jnp.bfloat16)
    for copy in copies[4:]:
        copy.wait()
    norm_ref[1] = v_ref[...]
    patches = control_ref[...].astype(jnp.float32)
    slabs = [patches[j * slab_rows : (j + 1) * slab_rows] for j in range(owners)]
    for step, out_ref in zip(steps_in(owners), out_refs):
        to = partner(me, step)
        at = 0
        for i in range(3):
            for head in range(share // HEAD_DIM):
                cols = pl.ds(pl.multiple_of(to * share + head * HEAD_DIM, HEAD_DIM), HEAD_DIM)
                lines = norm_ref[i, :, cols]
                out_ref[at : at + rows] = lines
                if step == 0 and i < 2:
                    own_ref[0, at : at + rows] = lines
                at = at + rows
        slab = slabs[0]
        for j in range(1, owners):
            slab = jnp.where(owner_ref[0, j] == to, slabs[j], slab)
        slab = slab.astype(jnp.bfloat16)
        for tile in range(width // HEAD_DIM):
            out_ref[at : at + slab_rows] = slab[:, tile * HEAD_DIM : (tile + 1) * HEAD_DIM]
            at = at + slab_rows


def sort_kernel(rows, *refs):
    got_refs, (pair_ref, rest_ref, patch_ref, ask_ref, give_ref) = refs[:-5], refs[-5:]
    owners = len(got_refs)
    slab_rows, width = rows // owners, patch_ref.shape[1]
    size, lines = pair_ref.shape[1], ask_ref.shape[1]
    asks = {step: ref.at[size : size + lines] for step, ref in zip(steps_in(owners), got_refs)}
    ask_ref[0] = asks[0][...]
    ask_ref[1] = asks[1][...]
    odd = lax.axis_index("blk") & 1
    for side in range(2):

        @pl.when(odd == side)
        def _():
            for i, step in enumerate(step_pairs(owners)):
                ask_ref[2 + i] = asks[step + side][...]
                give_ref[i] = asks[step + 1 - side][...]

    for i, ref in enumerate(got_refs):
        pair_ref[i] = ref[:size]
        if i:
            rest_ref[i - 1] = ref[:size]
    slabs = [ref[size + lines :].astype(jnp.float32) for ref in got_refs]
    patches = [
        jnp.concatenate([slab[i * slab_rows : (i + 1) * slab_rows] for slab in slabs], axis=0)
        for i in range(width // HEAD_DIM)
    ]
    patch_ref[...] = normed(jnp.concatenate(patches, axis=1), 1.0).astype(jnp.bfloat16)


def queries_of(ask_ref, taken_ref):
    both = [(ask_ref.at[2 + i], taken_ref.at[i]) for i in range(taken_ref.shape[0])]
    return [ask_ref.at[0], ask_ref.at[1], *(view for pair in both for view in pair)]


def fold(rows, ask_refs, pair_refs, use):
    owners = len(ask_refs)
    heads = pair_refs[0].shape[1] // (2 * rows)
    count = sum(ref.shape[0] for ref in pair_refs) * rows
    group = max(1, min(owners, 2**17 // (rows * count)))
    spans = [slice(i * rows, (i + 1) * rows) for i in range(2 * heads)]
    pieces = [
        jnp.concatenate([ref[:, span].reshape(-1, HEAD_DIM) for ref in pair_refs], axis=0)
        for span in spans
    ]
    ones = jnp.ones((count, HEAD_DIM), jnp.bfloat16)
    values = [jnp.concatenate([piece, ones], axis=1) for piece in pieces[heads:]]
    for first in range(0, owners, group):
        many = min(group, owners - first)
        scores = []
        for head in range(heads):
            queries = [ref[spans[head]] for ref in ask_refs[first : first + many]]
            scores.append(
                lax.dot_general(
                    jnp.concatenate(queries, axis=0),
                    pieces[head],
                    (((1,), (1,)), ((), ())),
                    preferred_element_type=jnp.float32,
                )
            )
        scores = jnp.concatenate(scores, axis=0) * (HEAD_DIM ** (-0.5))
        use(slice(first * rows, (first + many) * rows), scores, values)


def weigh(scores, peak, values):
    probs = jnp.exp(scores - peak).astype(jnp.bfloat16)
    each = probs.shape[0] // len(values)
    mixed = [
        jnp.dot(
            probs[i * each : (i + 1) * each], value, preferred_element_type=jnp.float32
        )
        for i, value in enumerate(values)
    ]
    mixed = jnp.concatenate(mixed, axis=0)
    return mixed[:, HEAD_DIM:], mixed[:, :HEAD_DIM]


def early_kernel(rows, *refs):
    state_refs = refs[-3:]

    def use(at, scores, values):
        peak = jnp.max(scores, axis=-1, keepdims=True)
        totals, mixed = weigh(scores, peak, values)
        each = mixed.shape[0] // len(values)
        for ref, state in zip(state_refs, (jnp.broadcast_to(peak, mixed.shape), totals, mixed)):
            for head in range(len(values)):
                ref[head, at] = state[head * each : (head + 1) * each]

    fold(rows, queries_of(*refs[:2]), refs[2:-3], use)


def late_kernel(rows, *refs):
    state_refs, refs = refs[:3], refs[3:]
    asks = queries_of(*refs[:2])
    outs = refs[0].shape[0]
    out_refs = refs[-outs:]

    def use(at, scores, values):
        heads = range(len(values))
        before, totals, accum = (
            jnp.concatenate([ref[head, at] for head in heads], axis=0) for ref in state_refs
        )
        most = jnp.max(scores, axis=-1, keepdims=True)
        peak = jnp.maximum(before, most)
        correction = jnp.exp(before - peak)
        keys = scores.shape[1]
        new_totals, mixed = weigh(scores, peak[:, : keys if keys < HEAD_DIM else 1], values)
        mixed = (accum * correction + mixed) / (totals * correction + new_totals)
        mixed = mixed.astype(jnp.bfloat16)
        many = (at.stop - at.start) // rows
        for i in range(len(values) * many):
            head, source = divmod(i, many)
            source = source + at.start // rows
            place, half = (source, 0) if source < 2 else divmod(source + 2, 2)
            start = (half * len(values) + head) * rows
            out_refs[place][start : start + rows] = mixed[i * rows : (i + 1) * rows]

    fold(rows, asks, refs[2:-outs], use)


def hint_kernel(layer_ref, patch_ref, weight_ref, gain_ref, out_ref):
    owners, slab_rows, _ = out_ref.shape
    hint = jnp.dot(patch_ref[...], weight_ref[...], preferred_element_type=jnp.float32)
    hint = hint.astype(jnp.bfloat16).astype(jnp.float32) * gain_ref[pl.ds(layer_ref[0], 1), :]
    me = lax.axis_index("ulysses")
    for i, step in enumerate(steps_in(owners)):
        out_ref[partner(me, step)] = hint[i * slab_rows : (i + 1) * slab_rows]


def finish_kernel(owners, hint_ref, own_ref, near_ref, *refs):
    far_refs, out_ref = refs[:-1], refs[-1]
    rows, feats = out_ref.shape
    share = feats // owners
    lines = own_ref.shape[0]
    me, odd = lax.axis_index("ulysses"), lax.axis_index("blk") & 1
    parts = [(0, own_ref, 0), (1, near_ref, 0)]
    for step, kept, crossed in zip(step_pairs(owners), far_refs[::2], far_refs[1::2]):
        parts = parts + [(step + odd, kept, 0), (step + 1 - odd, crossed, lines)]
    for step, ref, first in parts:
        for head in range(share // HEAD_DIM):
            start = partner(me, step) * share + head * HEAD_DIM
            cols = pl.ds(pl.multiple_of(start, HEAD_DIM), HEAD_DIM)
            at = first + head * rows
            attended = ref[at : at + rows].astype(jnp.float32)
            out_ref[:, cols] = (attended + hint_ref[:, cols]).astype(jnp.bfloat16)


VMEM = pl.BlockSpec(memory_space=pltpu.VMEM)
SMEM = pl.BlockSpec(memory_space=pltpu.SMEM)
HBM = pl.BlockSpec(memory_space=pltpu.HBM)


def call(kernel, out_shape, specs, *operands, scratch=(), flops=0, nbytes=0):
    return pl.pallas_call(
        kernel,
        out_shape=out_shape,
        in_specs=specs,
        out_specs=jax.tree.map(lambda _: VMEM, out_shape),
        scratch_shapes=scratch,
        compiler_params=pltpu.CompilerParams(vmem_limit_bytes=32 * 2**20),
        cost_estimate=pl.CostEstimate(flops=flops, bytes_accessed=nbytes, transcendentals=0),
    )(*operands)


def shape(dims, dtype=jnp.bfloat16):
    return jax.ShapeDtypeStruct(dims, dtype)


def swap_far(array, step):
    blocks, owners = lax.axis_size("blk"), lax.axis_size("ulysses")
    pairs = [
        (block * owners + i, block * owners + partner(i, step + (block & 1)))
        for block in range(blocks)
        for i in range(owners)
    ]
    return lax.ppermute(array, ("blk", "ulysses"), pairs)


def gather(held, step, axis):
    while step:
        held = held + [swap(array, axis, step) for array in held]
        step = step // 2
    return held


def exchange(arrays, steps, axis):
    return [swap(array, axis, step) if step else array for step, array in zip(steps, arrays)]


def shards(
    query_proj,
    key_proj,
    value_proj,
    query_gain,
    key_gain,
    control,
    hint_weight,
    hint_gain,
    owner_map,
    layer_index,
):
    owners = lax.axis_size("ulysses")
    rows, feats = query_proj.shape
    width = control.shape[1]
    lines = rows * (feats // owners // HEAD_DIM)
    slab_lines = rows // owners * (width // HEAD_DIM)
    sources = (
        key_gain.reshape(1, feats),
        key_proj,
        query_gain.reshape(1, feats),
        query_proj,
        value_proj,
        owner_map,
        control,
    )
    sources = [pltpu.with_memory_space_constraint(source, pltpu.HBM) for source in sources]
    sent = call(
        functools.partial(pack_kernel, owners),
        [shape((3 * lines + slab_lines, HEAD_DIM))] * owners + [shape((1, 2 * lines, HEAD_DIM))],
        [HBM] * len(sources),
        *sources,
        scratch=[
            (pltpu.SMEM if source.dtype == jnp.int32 else pltpu.VMEM)(source.shape, source.dtype)
            for source in sources
        ]
        + [
            pltpu.VMEM((3, rows, feats), jnp.bfloat16),
            pltpu.SemaphoreType.DMA((len(sources),)),
        ],
    )
    half = lax.axis_size("blk") // 2
    own_moved = swap(sent[owners], "blk", half)
    got, own_moved = lax.optimization_barrier((exchange(sent[:owners], steps_in(owners), "ulysses"), own_moved))
    pairs, rest, patches, asks, gives = call(
        functools.partial(sort_kernel, rows),
        [
            shape((owners, 2 * lines, HEAD_DIM)),
            shape((owners - 1, 2 * lines, HEAD_DIM)),
            shape((rows, width)),
            shape((owners // 2 + 1, lines, HEAD_DIM)),
            shape((owners // 2 - 1, lines, HEAD_DIM)),
        ],
        [VMEM] * owners,
        *got,
    )
    hint = call(
        hint_kernel,
        shape((owners, rows // owners, feats), jnp.float32),
        [SMEM] + [VMEM] * 3,
        layer_index,
        patches,
        hint_weight,
        hint_gain,
        flops=2 * rows * width * feats,
        nbytes=2 * width * feats,
    )
    moved = swap(rest, "blk", half)
    held = gather([own_moved], half // 2, "blk")
    taken = swap(gives, "blk", 1)
    moved, held, taken, hint = lax.optimization_barrier((moved, held, taken, hint))
    moved = gather([moved], half // 2, "blk")
    early = held + gather([pairs], half // 2, "blk") + moved[: len(moved) // 2]
    late = moved[len(moved) // 2 :]
    heads, many = lines // rows, owners * rows
    state = call(
        functools.partial(early_kernel, rows),
        [
            shape((heads, many, HEAD_DIM), jnp.float32),
        ]
        * 3,
        [VMEM] * (2 + len(early)),
        asks,
        taken,
        *early,
        flops=2 * many * sum(array.size for array in early),
        nbytes=2 * sum(array.size for array in early),
    )
    mixed = call(
        functools.partial(late_kernel, rows),
        [shape((lines, HEAD_DIM))] * 2 + [shape((2 * lines, HEAD_DIM))] * (owners // 2 - 1),
        [VMEM] * (5 + len(late)),
        *state,
        asks,
        taken,
        *late,
        flops=2 * many * sum(array.size for array in late),
        nbytes=2 * sum(array.size for array in late),
    )
    kept = [swap_far(array, step) for array, step in zip(mixed[2:], step_pairs(owners))]
    kept, near = lax.optimization_barrier((kept, swap(mixed[1], "ulysses", 1)))
    far = [array for one in kept for array in (one, swap(one, "blk", 1))]
    return call(
        functools.partial(finish_kernel, owners),
        shape((rows, feats)),
        [VMEM] * (3 + len(far)),
        hint.reshape(rows, feats),
        mixed[0],
        near,
        *far,
    )


def solution(mesh):
    split = P(("groups", "blk", "ulysses"), None)
    return jax.shard_map(
        shards,
        mesh=mesh,
        in_specs=(
            split,
            split,
            split,
            P(),
            P(),
            split,
            P(),
            P(),
            split,
            P(("groups", "blk", "ulysses")),
        ),
        out_specs=split,
        check_vma=False,
    )
```

```python
import functools

import jax
import jax.numpy as jnp
from jax import lax
from jax.experimental import pallas as pl
from jax.experimental.pallas import tpu as pltpu
from jax.sharding import PartitionSpec as P

HEAD_DIM = 128
EPS = 1e-06


def normed(rows, gain):
    values = rows.astype(jnp.float32)
    scale = lax.rsqrt(jnp.mean(values * values, axis=-1, keepdims=True) + EPS)
    return values * scale * gain


def partner(me, step):
    return me ^ step


def steps_in(owners):
    return sorted(range(owners), key=lambda step: (step > 0, -step.bit_length(), step))


def step_pairs(owners):
    return range(2, owners, 2)


def swap(array, axis, step):
    size = lax.axis_size(axis)
    return lax.ppermute(array, axis, [(i, partner(i, step)) for i in range(size)])


def pack_kernel(owners, *refs):
    total = (len(refs) - owners - 3) // 2
    sources, out_refs, own_ref = refs[:total], refs[total : total + owners], refs[total + owners]
    held, (norm_ref, copy_sems) = refs[total + owners + 1 : -2], refs[-2:]
    copies = [
        pltpu.make_async_copy(source, buffer, copy_sems.at[i])
        for i, (source, buffer) in enumerate(zip(sources, held))
    ]
    for copy in copies:
        copy.start()
    kg_ref, k_ref, qg_ref, q_ref, v_ref, owner_ref, control_ref = held
    rows, feats = q_ref.shape
    share = feats // owners
    slab_rows, width = rows // owners, control_ref.shape[1]
    me = lax.axis_index("ulysses")
    copies[0].wait()
    copies[1].wait()
    norm_ref[0] = normed(k_ref[...], kg_ref[...]).astype(jnp.bfloat16)
    copies[2].wait()
    copies[3].wait()
    norm_ref[2] = normed(q_ref[...], qg_ref[...]).astype(jnp.bfloat16)
    for copy in copies[4:]:
        copy.wait()
    norm_ref[1] = v_ref[...]
    patches = control_ref[...].astype(jnp.float32)
    slabs = [patches[j * slab_rows : (j + 1) * slab_rows] for j in range(owners)]
    for step, out_ref in zip(steps_in(owners), out_refs):
        to = partner(me, step)
        at = 0
        for i in range(3):
            for head in range(share // HEAD_DIM):
                cols = pl.ds(pl.multiple_of(to * share + head * HEAD_DIM, HEAD_DIM), HEAD_DIM)
                lines = norm_ref[i, :, cols]
                out_ref[at : at + rows] = lines
                if step == 0 and i < 2:
                    own_ref[0, at : at + rows] = lines
                at = at + rows
        slab = slabs[0]
        for j in range(1, owners):
            slab = jnp.where(owner_ref[0, j] == to, slabs[j], slab)
        slab = slab.astype(jnp.bfloat16)
        for tile in range(width // HEAD_DIM):
            out_ref[at : at + slab_rows] = slab[:, tile * HEAD_DIM : (tile + 1) * HEAD_DIM]
            at = at + slab_rows


def sort_kernel(rows, *refs):
    got_refs, (pair_ref, rest_ref, patch_ref, ask_ref, give_ref) = refs[:-5], refs[-5:]
    owners = len(got_refs)
    slab_rows, width = rows // owners, patch_ref.shape[1]
    size, lines = pair_ref.shape[1], ask_ref.shape[1]
    asks = {step: ref.at[size : size + lines] for step, ref in zip(steps_in(owners), got_refs)}
    ask_ref[0] = asks[0][...]
    ask_ref[1] = asks[1][...]
    odd = lax.axis_index("blk") & 1
    for side in range(2):

        @pl.when(odd == side)
        def _():
            for i, step in enumerate(step_pairs(owners)):
                ask_ref[2 + i] = asks[step + side][...]
                give_ref[i] = asks[step + 1 - side][...]

    for i, ref in enumerate(got_refs):
        pair_ref[i] = ref[:size]
        if i:
            rest_ref[i - 1] = ref[:size]
    slabs = [ref[size + lines :].astype(jnp.float32) for ref in got_refs]
    patches = [
        jnp.concatenate([slab[i * slab_rows : (i + 1) * slab_rows] for slab in slabs], axis=0)
        for i in range(width // HEAD_DIM)
    ]
    patch_ref[...] = normed(jnp.concatenate(patches, axis=1), 1.0).astype(jnp.bfloat16)


def queries_of(ask_ref, taken_ref):
    both = [(ask_ref.at[2 + i], taken_ref.at[i]) for i in range(taken_ref.shape[0])]
    return [ask_ref.at[0], ask_ref.at[1], *(view for pair in both for view in pair)]


def fold(rows, ask_refs, pair_refs, use):
    owners = len(ask_refs)
    heads = pair_refs[0].shape[1] // (2 * rows)
    count = sum(ref.shape[0] for ref in pair_refs) * rows
    group = max(1, min(owners, 2**17 // (rows * count)))
    spans = [slice(i * rows, (i + 1) * rows) for i in range(2 * heads)]
    pieces = [
        jnp.concatenate([ref[:, span].reshape(-1, HEAD_DIM) for ref in pair_refs], axis=0)
        for span in spans
    ]
    ones = jnp.ones((count, HEAD_DIM), jnp.bfloat16)
    values = [jnp.concatenate([piece, ones], axis=1) for piece in pieces[heads:]]
    for first in range(0, owners, group):
        many = min(group, owners - first)
        scores = []
        for head in range(heads):
            queries = [ref[spans[head]] for ref in ask_refs[first : first + many]]
            scores.append(
                lax.dot_general(
                    jnp.concatenate(queries, axis=0),
                    pieces[head],
                    (((1,), (1,)), ((), ())),
                    preferred_element_type=jnp.float32,
                )
            )
        scores = jnp.concatenate(scores, axis=0) * (HEAD_DIM ** (-0.5))
        use(slice(first * rows, (first + many) * rows), scores, values)


def weigh(scores, peak, values):
    probs = jnp.exp(scores - peak).astype(jnp.bfloat16)
    each = probs.shape[0] // len(values)
    mixed = [
        jnp.dot(
            probs[i * each : (i + 1) * each], value, preferred_element_type=jnp.float32
        )
        for i, value in enumerate(values)
    ]
    mixed = jnp.concatenate(mixed, axis=0)
    return mixed[:, HEAD_DIM:], mixed[:, :HEAD_DIM]


def early_kernel(rows, *refs):
    state_refs = refs[-3:]

    def use(at, scores, values):
        peak = jnp.max(scores, axis=-1, keepdims=True)
        totals, mixed = weigh(scores, peak, values)
        each = mixed.shape[0] // len(values)
        for ref, state in zip(state_refs, (jnp.broadcast_to(peak, mixed.shape), totals, mixed)):
            for head in range(len(values)):
                ref[head, at] = state[head * each : (head + 1) * each]

    fold(rows, queries_of(*refs[:2]), refs[2:-3], use)


def late_kernel(rows, *refs):
    state_refs, refs = refs[:3], refs[3:]
    asks = queries_of(*refs[:2])
    outs = refs[0].shape[0]
    out_refs = refs[-outs:]

    def use(at, scores, values):
        heads = range(len(values))
        before, totals, accum = (
            jnp.concatenate([ref[head, at] for head in heads], axis=0) for ref in state_refs
        )
        most = jnp.max(scores, axis=-1, keepdims=True)
        peak = jnp.maximum(before, most)
        correction = jnp.exp(before - peak)
        keys = scores.shape[1]
        new_totals, mixed = weigh(scores, peak[:, : keys if keys < HEAD_DIM else 1], values)
        mixed = (accum * correction + mixed) / (totals * correction + new_totals)
        many = (at.stop - at.start) // rows
        for i in range(len(values) * many):
            head, source = divmod(i, many)
            source = source + at.start // rows
            place, half = (source, 0) if source < 2 else divmod(source + 2, 2)
            start = (half * len(values) + head) * rows
            out_ref = out_refs[place]
            out_ref[start : start + rows] = mixed[i * rows : (i + 1) * rows].astype(out_ref.dtype)

    fold(rows, asks, refs[2:-outs], use)


def hint_kernel(layer_ref, patch_ref, weight_ref, gain_ref, out_ref):
    owners, slab_rows, _ = out_ref.shape
    hint = jnp.dot(patch_ref[...], weight_ref[...], preferred_element_type=jnp.float32)
    hint = hint.astype(jnp.bfloat16).astype(jnp.float32) * gain_ref[pl.ds(layer_ref[0], 1), :]
    me = lax.axis_index("ulysses")
    for i, step in enumerate(steps_in(owners)):
        out_ref[partner(me, step)] = hint[i * slab_rows : (i + 1) * slab_rows]


def finish_kernel(owners, hint_ref, own_ref, near_ref, *refs):
    far_refs, out_ref = refs[:-1], refs[-1]
    rows, feats = out_ref.shape
    share = feats // owners
    lines = own_ref.shape[0]
    me, odd = lax.axis_index("ulysses"), lax.axis_index("blk") & 1
    parts = [(0, own_ref, 0), (1, near_ref, 0)]
    for step, kept, crossed in zip(step_pairs(owners), far_refs[::2], far_refs[1::2]):
        parts = parts + [(step + odd, kept, 0), (step + 1 - odd, crossed, lines)]
    for step, ref, first in parts:
        for head in range(share // HEAD_DIM):
            start = partner(me, step) * share + head * HEAD_DIM
            cols = pl.ds(pl.multiple_of(start, HEAD_DIM), HEAD_DIM)
            at = first + head * rows
            attended = ref[at : at + rows].astype(jnp.bfloat16).astype(jnp.float32)
            out_ref[:, cols] = (attended + hint_ref[:, cols]).astype(jnp.bfloat16)


VMEM = pl.BlockSpec(memory_space=pltpu.VMEM)
SMEM = pl.BlockSpec(memory_space=pltpu.SMEM)
HBM = pl.BlockSpec(memory_space=pltpu.HBM)


def call(kernel, out_shape, specs, *operands, scratch=(), flops=0, nbytes=0):
    return pl.pallas_call(
        kernel,
        out_shape=out_shape,
        in_specs=specs,
        out_specs=jax.tree.map(lambda _: VMEM, out_shape),
        scratch_shapes=scratch,
        compiler_params=pltpu.CompilerParams(vmem_limit_bytes=32 * 2**20),
        cost_estimate=pl.CostEstimate(flops=flops, bytes_accessed=nbytes, transcendentals=0),
    )(*operands)


def shape(dims, dtype=jnp.bfloat16):
    return jax.ShapeDtypeStruct(dims, dtype)


def swap_far(array, step):
    blocks, owners = lax.axis_size("blk"), lax.axis_size("ulysses")
    pairs = [
        (block * owners + i, block * owners + partner(i, step + (block & 1)))
        for block in range(blocks)
        for i in range(owners)
    ]
    return lax.ppermute(array, ("blk", "ulysses"), pairs)


def gather(held, step, axis):
    while step:
        held = held + [swap(array, axis, step) for array in held]
        step = step // 2
    return held


def exchange(arrays, steps, axis):
    return [swap(array, axis, step) if step else array for step, array in zip(steps, arrays)]


def shards(
    query_proj,
    key_proj,
    value_proj,
    query_gain,
    key_gain,
    control,
    hint_weight,
    hint_gain,
    owner_map,
    layer_index,
):
    owners = lax.axis_size("ulysses")
    rows, feats = query_proj.shape
    width = control.shape[1]
    lines = rows * (feats // owners // HEAD_DIM)
    slab_lines = rows // owners * (width // HEAD_DIM)
    sources = (
        key_gain.reshape(1, feats),
        key_proj,
        query_gain.reshape(1, feats),
        query_proj,
        value_proj,
        owner_map,
        control,
    )
    sources = [pltpu.with_memory_space_constraint(source, pltpu.HBM) for source in sources]
    sent = call(
        functools.partial(pack_kernel, owners),
        [shape((3 * lines + slab_lines, HEAD_DIM))] * owners + [shape((1, 2 * lines, HEAD_DIM))],
        [HBM] * len(sources),
        *sources,
        scratch=[
            (pltpu.SMEM if source.dtype == jnp.int32 else pltpu.VMEM)(source.shape, source.dtype)
            for source in sources
        ]
        + [
            pltpu.VMEM((3, rows, feats), jnp.bfloat16),
            pltpu.SemaphoreType.DMA((len(sources),)),
        ],
    )
    half = lax.axis_size("blk") // 2
    own_moved = swap(sent[owners], "blk", half)
    got, own_moved = lax.optimization_barrier((exchange(sent[:owners], steps_in(owners), "ulysses"), own_moved))
    pairs, rest, patches, asks, gives = call(
        functools.partial(sort_kernel, rows),
        [
            shape((owners, 2 * lines, HEAD_DIM)),
            shape((owners - 1, 2 * lines, HEAD_DIM)),
            shape((rows, width)),
            shape((owners // 2 + 1, lines, HEAD_DIM)),
            shape((owners // 2 - 1, lines, HEAD_DIM)),
        ],
        [VMEM] * owners,
        *got,
    )
    hint = call(
        hint_kernel,
        shape((owners, rows // owners, feats), jnp.float32),
        [SMEM] + [VMEM] * 3,
        layer_index,
        patches,
        hint_weight,
        hint_gain,
        flops=2 * rows * width * feats,
        nbytes=2 * width * feats,
    )
    moved = swap(rest, "blk", half)
    held = gather([own_moved], half // 2, "blk")
    taken = swap(gives, "blk", 1)
    moved, held, taken, hint = lax.optimization_barrier((moved, held, taken, hint))
    moved = gather([moved], half // 2, "blk")
    early = held + gather([pairs], half // 2, "blk") + moved[: len(moved) // 2]
    late = moved[len(moved) // 2 :]
    heads, many = lines // rows, owners * rows
    state = call(
        functools.partial(early_kernel, rows),
        [
            shape((heads, many, HEAD_DIM), jnp.float32),
        ]
        * 3,
        [VMEM] * (2 + len(early)),
        asks,
        taken,
        *early,
        flops=2 * many * sum(array.size for array in early),
        nbytes=2 * sum(array.size for array in early),
    )
    mixed = call(
        functools.partial(late_kernel, rows),
        [shape((lines, HEAD_DIM)), shape((lines, HEAD_DIM), jnp.float32)]
        + [shape((2 * lines, HEAD_DIM))] * (owners // 2 - 1),
        [VMEM] * (5 + len(late)),
        *state,
        asks,
        taken,
        *late,
        flops=2 * many * sum(array.size for array in late),
        nbytes=2 * sum(array.size for array in late),
    )
    kept = [swap_far(array, step) for array, step in zip(mixed[2:], step_pairs(owners))]
    near = swap(mixed[1], "ulysses", 1)
    far = [array for one in kept for array in (one, swap(one, "blk", 1))]
    return call(
        functools.partial(finish_kernel, owners),
        shape((rows, feats)),
        [VMEM] * (3 + len(far)),
        hint.reshape(rows, feats),
        mixed[0],
        near,
        *far,
    )


def solution(mesh):
    split = P(("groups", "blk", "ulysses"), None)
    return jax.shard_map(
        shards,
        mesh=mesh,
        in_specs=(
            split,
            split,
            split,
            P(),
            P(),
            split,
            P(),
            P(),
            split,
            P(("groups", "blk", "ulysses")),
        ),
        out_specs=split,
        check_vma=False,
    )
```

```python
import functools

import jax
import jax.numpy as jnp
from jax import lax
from jax.experimental import pallas as pl
from jax.experimental.pallas import tpu as pltpu
from jax.sharding import PartitionSpec as P

HEAD_DIM = 128
EPS = 1e-06


def normed(rows, gain):
    values = rows.astype(jnp.float32)
    scale = lax.rsqrt(jnp.mean(values * values, axis=-1, keepdims=True) + EPS)
    return values * scale * gain


def partner(me, step):
    return me ^ step


def steps_in(owners, side):
    if side:
        return list(range(owners))
    return sorted(range(owners), key=lambda step: (step > 0, -step.bit_length(), step))


def partners_in(owners):
    me, odd = lax.axis_index("ulysses"), lax.axis_index("blk") & 1
    both = zip(steps_in(owners, 0), steps_in(owners, 1))
    return [partner(me, step + odd * (other - step)) for step, other in both]


def step_pairs(owners):
    return range(2, owners, 2)


def swap(array, axis, step):
    size = lax.axis_size(axis)
    return lax.ppermute(array, axis, [(i, partner(i, step)) for i in range(size)])


def pack_kernel(owners, *refs):
    total = (len(refs) - owners - 3) // 2
    sources, out_refs, own_ref = refs[:total], refs[total : total + owners], refs[total + owners]
    held, (norm_ref, copy_sems) = refs[total + owners + 1 : -2], refs[-2:]
    copies = [
        pltpu.make_async_copy(source, buffer, copy_sems.at[i])
        for i, (source, buffer) in enumerate(zip(sources, held))
    ]
    for copy in copies:
        copy.start()
    kg_ref, k_ref, qg_ref, q_ref, v_ref, owner_ref, control_ref = held
    rows, feats = q_ref.shape
    share = feats // owners
    slab_rows, width = rows // owners, control_ref.shape[1]
    copies[0].wait()
    copies[1].wait()
    norm_ref[0] = normed(k_ref[...], kg_ref[...]).astype(jnp.bfloat16)
    copies[2].wait()
    copies[3].wait()
    norm_ref[2] = normed(q_ref[...], qg_ref[...]).astype(jnp.bfloat16)
    for copy in copies[4:]:
        copy.wait()
    norm_ref[1] = v_ref[...]
    patches = control_ref[...].astype(jnp.float32)
    slabs = [patches[j * slab_rows : (j + 1) * slab_rows] for j in range(owners)]
    for slot, (to, out_ref) in enumerate(zip(partners_in(owners), out_refs)):
        at = 0
        for i in range(3):
            for head in range(share // HEAD_DIM):
                cols = pl.ds(pl.multiple_of(to * share + head * HEAD_DIM, HEAD_DIM), HEAD_DIM)
                lines = norm_ref[i, :, cols]
                out_ref[at : at + rows] = lines
                if slot == 0 and i < 2:
                    own_ref[0, at : at + rows] = lines
                at = at + rows
        slab = slabs[0]
        for j in range(1, owners):
            slab = jnp.where(owner_ref[0, j] == to, slabs[j], slab)
        slab = slab.astype(jnp.bfloat16)
        for tile in range(width // HEAD_DIM):
            out_ref[at : at + slab_rows] = slab[:, tile * HEAD_DIM : (tile + 1) * HEAD_DIM]
            at = at + slab_rows


def sort_kernel(rows, *refs):
    got_refs, (pair_ref, rest_ref, patch_ref, ask_ref, give_ref) = refs[:-5], refs[-5:]
    owners = len(got_refs)
    slab_rows, width = rows // owners, patch_ref.shape[1]
    size, lines = pair_ref.shape[1], ask_ref.shape[1]
    views = [ref.at[size : size + lines] for ref in got_refs]
    ask_ref[0] = views[0][...]
    odd = lax.axis_index("blk") & 1
    for side in range(2):

        @pl.when(odd == side)
        def _():
            asks = dict(zip(steps_in(owners, side), views))
            ask_ref[1] = asks[1][...]
            for i, step in enumerate(step_pairs(owners)):
                ask_ref[2 + i] = asks[step + side][...]
                give_ref[i] = asks[step + 1 - side][...]

    for i, ref in enumerate(got_refs):
        pair_ref[i] = ref[:size]
        if i:
            rest_ref[i - 1] = ref[:size]
    slabs = [ref[size + lines :].astype(jnp.float32) for ref in got_refs]
    patches = [
        jnp.concatenate([slab[i * slab_rows : (i + 1) * slab_rows] for slab in slabs], axis=0)
        for i in range(width // HEAD_DIM)
    ]
    patch_ref[...] = normed(jnp.concatenate(patches, axis=1), 1.0).astype(jnp.bfloat16)


def queries_of(ask_ref, taken_ref):
    both = [(ask_ref.at[2 + i], taken_ref.at[i]) for i in range(taken_ref.shape[0])]
    return [ask_ref.at[0], ask_ref.at[1], *(view for pair in both for view in pair)]


def fold(rows, ask_refs, pair_refs, use):
    owners = len(ask_refs)
    heads = pair_refs[0].shape[1] // (2 * rows)
    count = sum(ref.shape[0] for ref in pair_refs) * rows
    group = max(1, min(owners, 2**17 // (rows * count)))
    spans = [slice(i * rows, (i + 1) * rows) for i in range(2 * heads)]
    pieces = [
        jnp.concatenate([ref[:, span].reshape(-1, HEAD_DIM) for ref in pair_refs], axis=0)
        for span in spans
    ]
    ones = jnp.ones((count, HEAD_DIM), jnp.bfloat16)
    values = [jnp.concatenate([piece, ones], axis=1) for piece in pieces[heads:]]
    for first in range(0, owners, group):
        many = min(group, owners - first)
        scores = []
        for head in range(heads):
            queries = [ref[spans[head]] for ref in ask_refs[first : first + many]]
            scores.append(
                lax.dot_general(
                    jnp.concatenate(queries, axis=0),
                    pieces[head],
                    (((1,), (1,)), ((), ())),
                    preferred_element_type=jnp.float32,
                )
            )
        scores = jnp.concatenate(scores, axis=0) * (HEAD_DIM ** (-0.5))
        use(slice(first * rows, (first + many) * rows), scores, values)


def weigh(scores, peak, values):
    probs = jnp.exp(scores - peak).astype(jnp.bfloat16)
    each = probs.shape[0] // len(values)
    mixed = [
        jnp.dot(
            probs[i * each : (i + 1) * each], value, preferred_element_type=jnp.float32
        )
        for i, value in enumerate(values)
    ]
    mixed = jnp.concatenate(mixed, axis=0)
    return mixed[:, HEAD_DIM:], mixed[:, :HEAD_DIM]


def early_kernel(rows, *refs):
    state_refs = refs[-3:]

    def use(at, scores, values):
        peak = jnp.max(scores, axis=-1, keepdims=True)
        totals, mixed = weigh(scores, peak, values)
        each = mixed.shape[0] // len(values)
        for ref, state in zip(state_refs, (jnp.broadcast_to(peak, mixed.shape), totals, mixed)):
            for head in range(len(values)):
                ref[head, at] = state[head * each : (head + 1) * each]

    fold(rows, queries_of(*refs[:2]), refs[2:-3], use)


def late_kernel(rows, *refs):
    state_refs, refs = refs[:3], refs[3:]
    asks = queries_of(*refs[:2])
    outs = refs[0].shape[0]
    out_refs = refs[-outs:]

    def use(at, scores, values):
        heads = range(len(values))
        before, totals, accum = (
            jnp.concatenate([ref[head, at] for head in heads], axis=0) for ref in state_refs
        )
        most = jnp.max(scores, axis=-1, keepdims=True)
        peak = jnp.maximum(before, most)
        correction = jnp.exp(before - peak)
        keys = scores.shape[1]
        new_totals, mixed = weigh(scores, peak[:, : keys if keys < HEAD_DIM else 1], values)
        mixed = (accum * correction + mixed) / (totals * correction + new_totals)
        many = (at.stop - at.start) // rows
        for i in range(len(values) * many):
            head, source = divmod(i, many)
            source = source + at.start // rows
            place, half = (source, 0) if source < 2 else divmod(source + 2, 2)
            start = (half * len(values) + head) * rows
            out_ref = out_refs[place]
            out_ref[start : start + rows] = mixed[i * rows : (i + 1) * rows].astype(out_ref.dtype)

    fold(rows, asks, refs[2:-outs], use)


def hint_kernel(layer_ref, patch_ref, weight_ref, gain_ref, out_ref):
    owners, slab_rows, _ = out_ref.shape
    hint = jnp.dot(patch_ref[...], weight_ref[...], preferred_element_type=jnp.float32)
    hint = hint.astype(jnp.bfloat16).astype(jnp.float32) * gain_ref[pl.ds(layer_ref[0], 1), :]
    for i, source in enumerate(partners_in(owners)):
        out_ref[source] = hint[i * slab_rows : (i + 1) * slab_rows]


def finish_kernel(owners, hint_ref, own_ref, near_ref, *refs):
    far_refs, out_ref = refs[:-1], refs[-1]
    rows, feats = out_ref.shape
    share = feats // owners
    lines = own_ref.shape[0]
    me, odd = lax.axis_index("ulysses"), lax.axis_index("blk") & 1
    parts = [(0, own_ref, 0), (1, near_ref, 0)]
    for step, kept, crossed in zip(step_pairs(owners), far_refs[::2], far_refs[1::2]):
        parts = parts + [(step + odd, kept, 0), (step + 1 - odd, crossed, lines)]
    for step, ref, first in parts:
        for head in range(share // HEAD_DIM):
            start = partner(me, step) * share + head * HEAD_DIM
            cols = pl.ds(pl.multiple_of(start, HEAD_DIM), HEAD_DIM)
            at = first + head * rows
            attended = ref[at : at + rows].astype(jnp.bfloat16).astype(jnp.float32)
            out_ref[:, cols] = (attended + hint_ref[:, cols]).astype(jnp.bfloat16)


VMEM = pl.BlockSpec(memory_space=pltpu.VMEM)
SMEM = pl.BlockSpec(memory_space=pltpu.SMEM)
HBM = pl.BlockSpec(memory_space=pltpu.HBM)


def call(kernel, out_shape, specs, *operands, scratch=(), flops=0, nbytes=0):
    return pl.pallas_call(
        kernel,
        out_shape=out_shape,
        in_specs=specs,
        out_specs=jax.tree.map(lambda _: VMEM, out_shape),
        scratch_shapes=scratch,
        compiler_params=pltpu.CompilerParams(vmem_limit_bytes=32 * 2**20),
        cost_estimate=pl.CostEstimate(flops=flops, bytes_accessed=nbytes, transcendentals=0),
    )(*operands)


def shape(dims, dtype=jnp.bfloat16):
    return jax.ShapeDtypeStruct(dims, dtype)


def gather(held, step, axis):
    while step:
        held = held + [swap(array, axis, step) for array in held]
        step = step // 2
    return held


def swap_sides(array, steps):
    blocks, owners = lax.axis_size("blk"), lax.axis_size("ulysses")
    pairs = [
        (block * owners + i, block * owners + partner(i, steps[block & 1]))
        for block in range(blocks)
        for i in range(owners)
    ]
    return lax.ppermute(array, ("blk", "ulysses"), pairs)


def exchange(arrays):
    both = zip(steps_in(len(arrays), 0), steps_in(len(arrays), 1))
    return [swap_sides(array, steps) if any(steps) else array for array, steps in zip(arrays, both)]


def shards(
    query_proj,
    key_proj,
    value_proj,
    query_gain,
    key_gain,
    control,
    hint_weight,
    hint_gain,
    owner_map,
    layer_index,
):
    owners = lax.axis_size("ulysses")
    rows, feats = query_proj.shape
    width = control.shape[1]
    lines = rows * (feats // owners // HEAD_DIM)
    slab_lines = rows // owners * (width // HEAD_DIM)
    sources = (
        key_gain.reshape(1, feats),
        key_proj,
        query_gain.reshape(1, feats),
        query_proj,
        value_proj,
        owner_map,
        control,
    )
    sources = [pltpu.with_memory_space_constraint(source, pltpu.HBM) for source in sources]
    sent = call(
        functools.partial(pack_kernel, owners),
        [shape((3 * lines + slab_lines, HEAD_DIM))] * owners + [shape((1, 2 * lines, HEAD_DIM))],
        [HBM] * len(sources),
        *sources,
        scratch=[
            (pltpu.SMEM if source.dtype == jnp.int32 else pltpu.VMEM)(source.shape, source.dtype)
            for source in sources
        ]
        + [
            pltpu.VMEM((3, rows, feats), jnp.bfloat16),
            pltpu.SemaphoreType.DMA((len(sources),)),
        ],
    )
    half = lax.axis_size("blk") // 2
    own_moved = swap(sent[owners], "blk", half)
    got, own_moved = lax.optimization_barrier((exchange(sent[:owners]), own_moved))
    pairs, rest, patches, asks, gives = call(
        functools.partial(sort_kernel, rows),
        [
            shape((owners, 2 * lines, HEAD_DIM)),
            shape((owners - 1, 2 * lines, HEAD_DIM)),
            shape((rows, width)),
            shape((owners // 2 + 1, lines, HEAD_DIM)),
            shape((owners // 2 - 1, lines, HEAD_DIM)),
        ],
        [VMEM] * owners,
        *got,
    )
    hint = call(
        hint_kernel,
        shape((owners, rows // owners, feats), jnp.float32),
        [SMEM] + [VMEM] * 3,
        layer_index,
        patches,
        hint_weight,
        hint_gain,
        flops=2 * rows * width * feats,
        nbytes=2 * width * feats,
    )
    moved = swap(rest, "blk", half)
    held = gather([own_moved], half // 2, "blk")
    taken = swap(gives, "blk", 1)
    moved, held, taken, hint = lax.optimization_barrier((moved, held, taken, hint))
    moved = gather([moved], half // 2, "blk")
    early = held + gather([pairs], half // 2, "blk") + moved[: len(moved) // 2]
    late = moved[len(moved) // 2 :]
    heads, many = lines // rows, owners * rows
    state = call(
        functools.partial(early_kernel, rows),
        [
            shape((heads, many, HEAD_DIM), jnp.float32),
        ]
        * 3,
        [VMEM] * (2 + len(early)),
        asks,
        taken,
        *early,
        flops=2 * many * sum(array.size for array in early),
        nbytes=2 * sum(array.size for array in early),
    )
    mixed = call(
        functools.partial(late_kernel, rows),
        [shape((lines, HEAD_DIM)), shape((lines, HEAD_DIM), jnp.float32)]
        + [shape((2 * lines, HEAD_DIM))] * (owners // 2 - 1),
        [VMEM] * (5 + len(late)),
        *state,
        asks,
        taken,
        *late,
        flops=2 * many * sum(array.size for array in late),
        nbytes=2 * sum(array.size for array in late),
    )
    kept = [
        swap_sides(array, (step, step + 1)) for array, step in zip(mixed[2:], step_pairs(owners))
    ]
    near = swap(mixed[1], "ulysses", 1)
    far = [array for one in kept for array in (one, swap(one, "blk", 1))]
    return call(
        functools.partial(finish_kernel, owners),
        shape((rows, feats)),
        [VMEM] * (3 + len(far)),
        hint.reshape(rows, feats),
        mixed[0],
        near,
        *far,
    )


def solution(mesh):
    split = P(("groups", "blk", "ulysses"), None)
    return jax.shard_map(
        shards,
        mesh=mesh,
        in_specs=(
            split,
            split,
            split,
            P(),
            P(),
            split,
            P(),
            P(),
            split,
            P(("groups", "blk", "ulysses")),
        ),
        out_specs=split,
        check_vma=False,
    )
```

```python
import functools

import jax
import jax.numpy as jnp
from jax import lax
from jax.experimental import pallas as pl
from jax.experimental.pallas import tpu as pltpu
from jax.sharding import PartitionSpec as P

HEAD_DIM = 128
EPS = 1e-06


def normed(rows, gain):
    values = rows.astype(jnp.float32)
    scale = lax.rsqrt(jnp.mean(values * values, axis=-1, keepdims=True) + EPS)
    return values * scale * gain


def partner(me, step):
    return me ^ step


def steps_in(owners):
    return sorted(range(owners), key=lambda step: (step > 0, -step.bit_length(), step))


def step_pairs(owners):
    return range(2, owners, 2)


def swap(array, axis, step):
    size = lax.axis_size(axis)
    return lax.ppermute(array, axis, [(i, partner(i, step)) for i in range(size)])


def pack_kernel(owners, *refs):
    total = (len(refs) - owners - 3) // 2
    sources, out_refs, own_ref = refs[:total], refs[total : total + owners], refs[total + owners]
    held, (norm_ref, copy_sems) = refs[total + owners + 1 : -2], refs[-2:]
    copies = [
        pltpu.make_async_copy(source, buffer, copy_sems.at[i])
        for i, (source, buffer) in enumerate(zip(sources, held))
    ]
    for copy in copies:
        copy.start()
    owner_ref, control_ref, kg_ref, k_ref, qg_ref, q_ref, v_ref = held
    rows, feats = q_ref.shape
    share = feats // owners
    slab_rows, width = rows // owners, control_ref.shape[1]
    me = lax.axis_index("ulysses")
    copies[0].wait()
    copies[1].wait()
    patches = control_ref[...].astype(jnp.float32)
    slabs = [patches[j * slab_rows : (j + 1) * slab_rows] for j in range(owners)]
    for step, out_ref in zip(steps_in(owners), out_refs):
        to = partner(me, step)
        slab = slabs[0]
        for j in range(1, owners):
            slab = jnp.where(owner_ref[0, j] == to, slabs[j], slab)
        slab = slab.astype(jnp.bfloat16)
        for tile in range(width // HEAD_DIM):
            at = 3 * share // HEAD_DIM * rows + tile * slab_rows
            out_ref[at : at + slab_rows] = slab[:, tile * HEAD_DIM : (tile + 1) * HEAD_DIM]
    copies[2].wait()
    copies[3].wait()
    norm_ref[0] = normed(k_ref[...], kg_ref[...]).astype(jnp.bfloat16)
    copies[4].wait()
    copies[5].wait()
    norm_ref[2] = normed(q_ref[...], qg_ref[...]).astype(jnp.bfloat16)
    copies[6].wait()
    norm_ref[1] = v_ref[...]
    for step, out_ref in zip(steps_in(owners), out_refs):
        to = partner(me, step)
        at = 0
        for i in range(3):
            for head in range(share // HEAD_DIM):
                cols = pl.ds(pl.multiple_of(to * share + head * HEAD_DIM, HEAD_DIM), HEAD_DIM)
                lines = norm_ref[i, :, cols]
                out_ref[at : at + rows] = lines
                if step == 0 and i < 2:
                    own_ref[0, at : at + rows] = lines
                at = at + rows


def sort_kernel(*refs):
    got_refs, (pair_ref, rest_ref, ask_ref, give_ref) = refs[:-4], refs[-4:]
    owners = len(got_refs)
    size, lines = pair_ref.shape[1], ask_ref.shape[1]
    asks = {step: ref.at[size : size + lines] for step, ref in zip(steps_in(owners), got_refs)}
    ask_ref[0] = asks[0][...]
    ask_ref[1] = asks[1][...]
    odd = lax.axis_index("blk") & 1
    for side in range(2):

        @pl.when(odd == side)
        def _():
            for i, step in enumerate(step_pairs(owners)):
                ask_ref[2 + i] = asks[step + side][...]
                give_ref[i] = asks[step + 1 - side][...]

    for i, ref in enumerate(got_refs):
        pair_ref[i] = ref[:size]
        if i:
            rest_ref[i - 1] = ref[:size]


def queries_of(ask_ref, taken_ref):
    both = [(ask_ref.at[2 + i], taken_ref.at[i]) for i in range(taken_ref.shape[0])]
    return [ask_ref.at[0], ask_ref.at[1], *(view for pair in both for view in pair)]


def fold(rows, ask_refs, pair_refs, use):
    owners = len(ask_refs)
    heads = pair_refs[0].shape[1] // (2 * rows)
    count = sum(ref.shape[0] for ref in pair_refs) * rows
    group = max(1, min(owners, 2**17 // (rows * count)))
    spans = [slice(i * rows, (i + 1) * rows) for i in range(2 * heads)]
    pieces = [
        jnp.concatenate([ref[:, span].reshape(-1, HEAD_DIM) for ref in pair_refs], axis=0)
        for span in spans
    ]
    ones = jnp.ones((count, HEAD_DIM), jnp.bfloat16)
    values = [jnp.concatenate([piece, ones], axis=1) for piece in pieces[heads:]]
    for first in range(0, owners, group):
        many = min(group, owners - first)
        scores = []
        for head in range(heads):
            queries = [ref[spans[head]] for ref in ask_refs[first : first + many]]
            scores.append(
                lax.dot_general(
                    jnp.concatenate(queries, axis=0),
                    pieces[head],
                    (((1,), (1,)), ((), ())),
                    preferred_element_type=jnp.float32,
                )
            )
        scores = jnp.concatenate(scores, axis=0) * (HEAD_DIM ** (-0.5))
        use(slice(first * rows, (first + many) * rows), scores, values)


def weigh(scores, peak, values):
    probs = jnp.exp(scores - peak).astype(jnp.bfloat16)
    each = probs.shape[0] // len(values)
    mixed = [
        jnp.dot(
            probs[i * each : (i + 1) * each], value, preferred_element_type=jnp.float32
        )
        for i, value in enumerate(values)
    ]
    mixed = jnp.concatenate(mixed, axis=0)
    return mixed[:, HEAD_DIM:], mixed[:, :HEAD_DIM]


def early_kernel(rows, *refs):
    state_refs = refs[-3:]

    def use(at, scores, values):
        peak = jnp.max(scores, axis=-1, keepdims=True)
        totals, mixed = weigh(scores, peak, values)
        each = mixed.shape[0] // len(values)
        for ref, state in zip(state_refs, (jnp.broadcast_to(peak, mixed.shape), totals, mixed)):
            for head in range(len(values)):
                ref[head, at] = state[head * each : (head + 1) * each]

    fold(rows, queries_of(*refs[:2]), refs[2:-3], use)


def late_kernel(rows, *refs):
    state_refs, refs = refs[:3], refs[3:]
    asks = queries_of(*refs[:2])
    outs = refs[0].shape[0]
    out_refs = refs[-outs:]

    def use(at, scores, values):
        heads = range(len(values))
        before, totals, accum = (
            jnp.concatenate([ref[head, at] for head in heads], axis=0) for ref in state_refs
        )
        most = jnp.max(scores, axis=-1, keepdims=True)
        peak = jnp.maximum(before, most)
        correction = jnp.exp(before - peak)
        keys = scores.shape[1]
        new_totals, mixed = weigh(scores, peak[:, : keys if keys < HEAD_DIM else 1], values)
        mixed = (accum * correction + mixed) / (totals * correction + new_totals)
        many = (at.stop - at.start) // rows
        for i in range(len(values) * many):
            head, source = divmod(i, many)
            source = source + at.start // rows
            place, half = (source, 0) if source < 2 else divmod(source + 2, 2)
            start = (half * len(values) + head) * rows
            out_ref = out_refs[place]
            out_ref[start : start + rows] = mixed[i * rows : (i + 1) * rows].astype(out_ref.dtype)

    fold(rows, asks, refs[2:-outs], use)


def hint_kernel(layer_ref, weight_ref, gain_ref, *refs):
    got_refs, out_ref = refs[:-1], refs[-1]
    owners, slab_rows, _ = out_ref.shape
    tiles = weight_ref.shape[0] // HEAD_DIM
    start = got_refs[0].shape[0] - tiles * slab_rows
    slabs = [ref[start:].astype(jnp.float32) for ref in got_refs]
    patches = [
        jnp.concatenate([slab[i * slab_rows : (i + 1) * slab_rows] for slab in slabs], axis=0)
        for i in range(tiles)
    ]
    patches = normed(jnp.concatenate(patches, axis=1), 1.0).astype(jnp.bfloat16)
    hint = jnp.dot(patches, weight_ref[...], preferred_element_type=jnp.float32)
    hint = hint.astype(jnp.bfloat16).astype(jnp.float32) * gain_ref[pl.ds(layer_ref[0], 1), :]
    me = lax.axis_index("ulysses")
    for i, step in enumerate(steps_in(owners)):
        out_ref[partner(me, step)] = hint[i * slab_rows : (i + 1) * slab_rows]


def finish_kernel(owners, hint_ref, own_ref, near_ref, *refs):
    far_refs, out_ref = refs[:-1], refs[-1]
    rows, feats = out_ref.shape
    share = feats // owners
    lines = own_ref.shape[0]
    me, odd = lax.axis_index("ulysses"), lax.axis_index("blk") & 1
    parts = [(0, own_ref, 0), (1, near_ref, 0)]
    for step, kept, crossed in zip(step_pairs(owners), far_refs[::2], far_refs[1::2]):
        parts = parts + [(step + odd, kept, 0), (step + 1 - odd, crossed, lines)]
    for step, ref, first in parts:
        for head in range(share // HEAD_DIM):
            start = partner(me, step) * share + head * HEAD_DIM
            cols = pl.ds(pl.multiple_of(start, HEAD_DIM), HEAD_DIM)
            at = first + head * rows
            attended = ref[at : at + rows].astype(jnp.bfloat16).astype(jnp.float32)
            out_ref[:, cols] = (attended + hint_ref[:, cols]).astype(jnp.bfloat16)


VMEM = pl.BlockSpec(memory_space=pltpu.VMEM)
SMEM = pl.BlockSpec(memory_space=pltpu.SMEM)
HBM = pl.BlockSpec(memory_space=pltpu.HBM)


def call(kernel, out_shape, specs, *operands, scratch=(), flops=0, nbytes=0):
    return pl.pallas_call(
        kernel,
        out_shape=out_shape,
        in_specs=specs,
        out_specs=jax.tree.map(lambda _: VMEM, out_shape),
        scratch_shapes=scratch,
        compiler_params=pltpu.CompilerParams(vmem_limit_bytes=32 * 2**20),
        cost_estimate=pl.CostEstimate(flops=flops, bytes_accessed=nbytes, transcendentals=0),
    )(*operands)


def shape(dims, dtype=jnp.bfloat16):
    return jax.ShapeDtypeStruct(dims, dtype)


def swap_far(array, step):
    blocks, owners = lax.axis_size("blk"), lax.axis_size("ulysses")
    pairs = [
        (block * owners + i, block * owners + partner(i, step + (block & 1)))
        for block in range(blocks)
        for i in range(owners)
    ]
    return lax.ppermute(array, ("blk", "ulysses"), pairs)


def gather(held, step, axis):
    while step:
        held = held + [swap(array, axis, step) for array in held]
        step = step // 2
    return held


def exchange(arrays, steps, axis):
    return [swap(array, axis, step) if step else array for step, array in zip(steps, arrays)]


def shards(
    query_proj,
    key_proj,
    value_proj,
    query_gain,
    key_gain,
    control,
    hint_weight,
    hint_gain,
    owner_map,
    layer_index,
):
    owners = lax.axis_size("ulysses")
    rows, feats = query_proj.shape
    width = control.shape[1]
    lines = rows * (feats // owners // HEAD_DIM)
    slab_lines = rows // owners * (width // HEAD_DIM)
    sources = (
        owner_map,
        control,
        key_gain.reshape(1, feats),
        key_proj,
        query_gain.reshape(1, feats),
        query_proj,
        value_proj,
    )
    sources = [pltpu.with_memory_space_constraint(source, pltpu.HBM) for source in sources]
    sent = call(
        functools.partial(pack_kernel, owners),
        [shape((3 * lines + slab_lines, HEAD_DIM))] * owners + [shape((1, 2 * lines, HEAD_DIM))],
        [HBM] * len(sources),
        *sources,
        scratch=[
            (pltpu.SMEM if source.dtype == jnp.int32 else pltpu.VMEM)(source.shape, source.dtype)
            for source in sources
        ]
        + [
            pltpu.VMEM((3, rows, feats), jnp.bfloat16),
            pltpu.SemaphoreType.DMA((len(sources),)),
        ],
    )
    half = lax.axis_size("blk") // 2
    own_moved = swap(sent[owners], "blk", half)
    got, own_moved = lax.optimization_barrier((exchange(sent[:owners], steps_in(owners), "ulysses"), own_moved))
    pairs, rest, asks, gives = call(
        sort_kernel,
        [
            shape((owners, 2 * lines, HEAD_DIM)),
            shape((owners - 1, 2 * lines, HEAD_DIM)),
            shape((owners // 2 + 1, lines, HEAD_DIM)),
            shape((owners // 2 - 1, lines, HEAD_DIM)),
        ],
        [VMEM] * owners,
        *got,
    )
    hint = call(
        hint_kernel,
        shape((owners, rows // owners, feats), jnp.float32),
        [SMEM] + [VMEM] * (2 + owners),
        layer_index,
        hint_weight,
        hint_gain,
        *got,
        flops=2 * rows * width * feats,
        nbytes=2 * width * feats,
    )
    moved = swap(rest, "blk", half)
    held = gather([own_moved], half // 2, "blk")
    taken = swap(gives, "blk", 1)
    moved, held, taken, hint = lax.optimization_barrier((moved, held, taken, hint))
    moved = gather([moved], half // 2, "blk")
    early = held + gather([pairs], half // 2, "blk") + moved[: len(moved) // 2]
    late = moved[len(moved) // 2 :]
    heads, many = lines // rows, owners * rows
    state = call(
        functools.partial(early_kernel, rows),
        [
            shape((heads, many, HEAD_DIM), jnp.float32),
        ]
        * 3,
        [VMEM] * (2 + len(early)),
        asks,
        taken,
        *early,
        flops=2 * many * sum(array.size for array in early),
        nbytes=2 * sum(array.size for array in early),
    )
    mixed = call(
        functools.partial(late_kernel, rows),
        [shape((lines, HEAD_DIM)), shape((lines, HEAD_DIM), jnp.float32)]
        + [shape((2 * lines, HEAD_DIM))] * (owners // 2 - 1),
        [VMEM] * (5 + len(late)),
        *state,
        asks,
        taken,
        *late,
        flops=2 * many * sum(array.size for array in late),
        nbytes=2 * sum(array.size for array in late),
    )
    kept = [swap_far(array, step) for array, step in zip(mixed[2:], step_pairs(owners))]
    near = swap(mixed[1], "ulysses", 1)
    far = [array for one in kept for array in (one, swap(one, "blk", 1))]
    return call(
        functools.partial(finish_kernel, owners),
        shape((rows, feats)),
        [VMEM] * (3 + len(far)),
        hint.reshape(rows, feats),
        mixed[0],
        near,
        *far,
    )


def solution(mesh):
    split = P(("groups", "blk", "ulysses"), None)
    return jax.shard_map(
        shards,
        mesh=mesh,
        in_specs=(
            split,
            split,
            split,
            P(),
            P(),
            split,
            P(),
            P(),
            split,
            P(("groups", "blk", "ulysses")),
        ),
        out_specs=split,
        check_vma=False,
    )
```

```python
import functools

import jax
import jax.numpy as jnp
from jax import lax
from jax.experimental import pallas as pl
from jax.experimental.pallas import tpu as pltpu
from jax.sharding import PartitionSpec as P

HEAD_DIM = 128
EPS = 1e-06


def normed(rows, gain):
    values = rows.astype(jnp.float32)
    scale = lax.rsqrt(jnp.mean(values * values, axis=-1, keepdims=True) + EPS)
    return values * scale * gain


def partner(me, step):
    return me ^ step


def steps_in(owners):
    return sorted(range(owners), key=lambda step: (step > 0, -step.bit_length(), step))


def step_pairs(owners):
    return range(2, owners, 2)


def swap(array, axis, step):
    size = lax.axis_size(axis)
    return lax.ppermute(array, axis, [(i, partner(i, step)) for i in range(size)])


def pack_kernel(owners, *refs):
    total = (len(refs) - owners - 3) // 2
    sources, out_refs, own_ref = refs[:total], refs[total : total + owners], refs[total + owners]
    held, (norm_ref, copy_sems) = refs[total + owners + 1 : -2], refs[-2:]
    copies = [
        pltpu.make_async_copy(source, buffer, copy_sems.at[i])
        for i, (source, buffer) in enumerate(zip(sources, held))
    ]
    for copy in copies:
        copy.start()
    owner_ref, control_ref, kg_ref, k_ref, qg_ref, q_ref, v_ref = held
    rows, feats = q_ref.shape
    share = feats // owners
    slab_rows, width = rows // owners, control_ref.shape[1]
    me = lax.axis_index("ulysses")
    copies[0].wait()
    copies[1].wait()
    patches = control_ref[...].astype(jnp.float32)
    slabs = [patches[j * slab_rows : (j + 1) * slab_rows] for j in range(owners)]
    for step, out_ref in zip(steps_in(owners), out_refs):
        to = partner(me, step)
        slab = slabs[0]
        for j in range(1, owners):
            slab = jnp.where(owner_ref[0, j] == to, slabs[j], slab)
        slab = slab.astype(jnp.bfloat16)
        for tile in range(width // HEAD_DIM):
            at = 3 * share // HEAD_DIM * rows + tile * slab_rows
            out_ref[at : at + slab_rows] = slab[:, tile * HEAD_DIM : (tile + 1) * HEAD_DIM]
    copies[2].wait()
    copies[3].wait()
    norm_ref[0] = normed(k_ref[...], kg_ref[...]).astype(jnp.bfloat16)
    copies[4].wait()
    copies[5].wait()
    norm_ref[2] = normed(q_ref[...], qg_ref[...]).astype(jnp.bfloat16)
    copies[6].wait()
    norm_ref[1] = v_ref[...]
    for step, out_ref in zip(steps_in(owners), out_refs):
        to = partner(me, step)
        at = 0
        for i in range(3):
            for head in range(share // HEAD_DIM):
                cols = pl.ds(pl.multiple_of(to * share + head * HEAD_DIM, HEAD_DIM), HEAD_DIM)
                lines = norm_ref[i, :, cols]
                out_ref[at : at + rows] = lines
                if step == 0 and i < 2:
                    own_ref[0, at : at + rows] = lines
                at = at + rows


def sort_kernel(*refs):
    got_refs, (pair_ref, rest_ref, ask_ref, give_ref) = refs[:-4], refs[-4:]
    owners = len(got_refs)
    size, lines = pair_ref.shape[1], ask_ref.shape[1]
    asks = {step: ref.at[size : size + lines] for step, ref in zip(steps_in(owners), got_refs)}
    ask_ref[0] = asks[0][...]
    ask_ref[1] = asks[1][...]
    odd = lax.axis_index("blk") & 1
    for side in range(2):

        @pl.when(odd == side)
        def _():
            for i, step in enumerate(step_pairs(owners)):
                ask_ref[2 + i] = asks[step + side][...]
                give_ref[i] = asks[step + 1 - side][...]

    for i, ref in enumerate(got_refs):
        pair_ref[i] = ref[:size]
        if i:
            rest_ref[i - 1] = ref[:size]


def queries_of(ask_ref, taken_ref):
    both = [(ask_ref.at[2 + i], taken_ref.at[i]) for i in range(taken_ref.shape[0])]
    return [ask_ref.at[0], ask_ref.at[1], *(view for pair in both for view in pair)]


def fold(rows, ask_refs, pair_refs, use):
    owners = len(ask_refs)
    heads = pair_refs[0].shape[1] // (2 * rows)
    count = sum(ref.shape[0] for ref in pair_refs) * rows
    group = max(1, min(owners, 2**17 // (rows * count)))
    spans = [slice(i * rows, (i + 1) * rows) for i in range(2 * heads)]
    pieces = [
        jnp.concatenate([ref[:, span].reshape(-1, HEAD_DIM) for ref in pair_refs], axis=0)
        for span in spans
    ]
    ones = jnp.ones((count, HEAD_DIM), jnp.bfloat16)
    values = [jnp.concatenate([piece, ones], axis=1) for piece in pieces[heads:]]
    for first in range(0, owners, group):
        many = min(group, owners - first)
        scores = []
        for head in range(heads):
            queries = [ref[spans[head]] for ref in ask_refs[first : first + many]]
            scores.append(
                lax.dot_general(
                    jnp.concatenate(queries, axis=0),
                    pieces[head],
                    (((1,), (1,)), ((), ())),
                    preferred_element_type=jnp.float32,
                )
            )
        scores = jnp.concatenate(scores, axis=0) * (HEAD_DIM ** (-0.5))
        use(slice(first * rows, (first + many) * rows), scores, values)


def weigh(scores, peak, values):
    probs = jnp.exp(scores - peak).astype(jnp.bfloat16)
    each = probs.shape[0] // len(values)
    mixed = [
        jnp.dot(
            probs[i * each : (i + 1) * each], value, preferred_element_type=jnp.float32
        )
        for i, value in enumerate(values)
    ]
    mixed = jnp.concatenate(mixed, axis=0)
    return mixed[:, HEAD_DIM:], mixed[:, :HEAD_DIM]


def early_kernel(rows, *refs):
    state_refs = refs[-3:]

    def use(at, scores, values):
        peak = jnp.max(scores, axis=-1, keepdims=True)
        totals, mixed = weigh(scores, peak, values)
        each = mixed.shape[0] // len(values)
        for ref, state in zip(state_refs, (jnp.broadcast_to(peak, mixed.shape), totals, mixed)):
            for head in range(len(values)):
                ref[head, at] = state[head * each : (head + 1) * each]

    fold(rows, queries_of(*refs[:2]), refs[2:-3], use)


def late_kernel(rows, *refs):
    state_refs, refs = refs[:3], refs[3:]
    asks = queries_of(*refs[:2])
    outs = refs[0].shape[0]
    out_refs = refs[-outs:]

    def use(at, scores, values):
        heads = range(len(values))
        before, totals, accum = (
            jnp.concatenate([ref[head, at] for head in heads], axis=0) for ref in state_refs
        )
        most = jnp.max(scores, axis=-1, keepdims=True)
        peak = jnp.maximum(before, most)
        correction = jnp.exp(before - peak)
        keys = scores.shape[1]
        new_totals, mixed = weigh(scores, peak[:, : keys if keys < HEAD_DIM else 1], values)
        mixed = (accum * correction + mixed) / (totals * correction + new_totals)
        many = (at.stop - at.start) // rows
        for i in range(len(values) * many):
            head, source = divmod(i, many)
            source = source + at.start // rows
            place, half = (source, 0) if source < 2 else divmod(source + 2, 2)
            start = (half * len(values) + head) * rows
            out_ref = out_refs[place]
            out_ref[start : start + rows] = mixed[i * rows : (i + 1) * rows].astype(out_ref.dtype)

    fold(rows, asks, refs[2:-outs], use)


def hint_kernel(layer_ref, weight_ref, gain_ref, *refs):
    got_refs, out_ref = refs[:-1], refs[-1]
    owners, slab_rows, _ = out_ref.shape
    tiles = weight_ref.shape[0] // HEAD_DIM
    start = got_refs[0].shape[0] - tiles * slab_rows
    slabs = [ref[start:].astype(jnp.float32) for ref in got_refs]
    patches = [
        jnp.concatenate([slab[i * slab_rows : (i + 1) * slab_rows] for slab in slabs], axis=0)
        for i in range(tiles)
    ]
    patches = normed(jnp.concatenate(patches, axis=1), 1.0).astype(jnp.bfloat16)
    hint = jnp.dot(patches, weight_ref[...], preferred_element_type=jnp.float32)
    hint = hint.astype(jnp.bfloat16).astype(jnp.float32) * gain_ref[pl.ds(layer_ref[0], 1), :]
    me = lax.axis_index("ulysses")
    for i, step in enumerate(steps_in(owners)):
        out_ref[partner(me, step)] = hint[i * slab_rows : (i + 1) * slab_rows]


def finish_kernel(owners, hint_ref, own_ref, near_ref, *refs):
    far_refs, (out_ref, held_ref, copy_sems) = refs[:-3], refs[-3:]
    rows, feats = out_ref.shape
    share = feats // owners
    lines = own_ref.shape[0]
    me, odd = lax.axis_index("ulysses"), lax.axis_index("blk") & 1
    parts = [(0, own_ref, 0), (1, near_ref, 0)]
    for step, kept, crossed in zip(step_pairs(owners), far_refs[::2], far_refs[1::2]):
        parts = parts + [(step + odd, kept, 0), (step + 1 - odd, crossed, lines)]
    pieces = copy_sems.shape[0]
    many = rows // pieces
    copies = []
    for piece in range(pieces):
        span = pl.ds(piece * many, many)
        for step, ref, first in parts:
            for head in range(share // HEAD_DIM):
                start = partner(me, step) * share + head * HEAD_DIM
                cols = pl.ds(pl.multiple_of(start, HEAD_DIM), HEAD_DIM)
                at = first + head * rows + piece * many
                attended = ref[at : at + many].astype(jnp.bfloat16).astype(jnp.float32)
                held_ref[span, cols] = (attended + hint_ref[span, cols]).astype(jnp.bfloat16)
        copy = pltpu.make_async_copy(held_ref.at[span], out_ref.at[span], copy_sems.at[piece])
        copy.start()
        copies.append(copy)
    for copy in copies:
        copy.wait()


VMEM = pl.BlockSpec(memory_space=pltpu.VMEM)
SMEM = pl.BlockSpec(memory_space=pltpu.SMEM)
HBM = pl.BlockSpec(memory_space=pltpu.HBM)


def call(kernel, out_shape, specs, *operands, out=None, scratch=(), flops=0, nbytes=0):
    return pl.pallas_call(
        kernel,
        out_shape=out_shape,
        in_specs=specs,
        out_specs=jax.tree.map(lambda _: out or VMEM, out_shape),
        scratch_shapes=scratch,
        compiler_params=pltpu.CompilerParams(vmem_limit_bytes=32 * 2**20),
        cost_estimate=pl.CostEstimate(flops=flops, bytes_accessed=nbytes, transcendentals=0),
    )(*operands)


def shape(dims, dtype=jnp.bfloat16):
    return jax.ShapeDtypeStruct(dims, dtype)


def swap_far(array, step):
    blocks, owners = lax.axis_size("blk"), lax.axis_size("ulysses")
    pairs = [
        (block * owners + i, block * owners + partner(i, step + (block & 1)))
        for block in range(blocks)
        for i in range(owners)
    ]
    return lax.ppermute(array, ("blk", "ulysses"), pairs)


def gather(held, step, axis):
    while step:
        held = held + [swap(array, axis, step) for array in held]
        step = step // 2
    return held


def exchange(arrays, steps, axis):
    return [swap(array, axis, step) if step else array for step, array in zip(steps, arrays)]


def shards(
    query_proj,
    key_proj,
    value_proj,
    query_gain,
    key_gain,
    control,
    hint_weight,
    hint_gain,
    owner_map,
    layer_index,
):
    owners = lax.axis_size("ulysses")
    rows, feats = query_proj.shape
    width = control.shape[1]
    lines = rows * (feats // owners // HEAD_DIM)
    slab_lines = rows // owners * (width // HEAD_DIM)
    sources = (
        owner_map,
        control,
        key_gain.reshape(1, feats),
        key_proj,
        query_gain.reshape(1, feats),
        query_proj,
        value_proj,
    )
    sources = [pltpu.with_memory_space_constraint(source, pltpu.HBM) for source in sources]
    sent = call(
        functools.partial(pack_kernel, owners),
        [shape((3 * lines + slab_lines, HEAD_DIM))] * owners + [shape((1, 2 * lines, HEAD_DIM))],
        [HBM] * len(sources),
        *sources,
        scratch=[
            (pltpu.SMEM if source.dtype == jnp.int32 else pltpu.VMEM)(source.shape, source.dtype)
            for source in sources
        ]
        + [
            pltpu.VMEM((3, rows, feats), jnp.bfloat16),
            pltpu.SemaphoreType.DMA((len(sources),)),
        ],
    )
    half = lax.axis_size("blk") // 2
    own_moved = swap(sent[owners], "blk", half)
    got, own_moved = lax.optimization_barrier((exchange(sent[:owners], steps_in(owners), "ulysses"), own_moved))
    pairs, rest, asks, gives = call(
        sort_kernel,
        [
            shape((owners, 2 * lines, HEAD_DIM)),
            shape((owners - 1, 2 * lines, HEAD_DIM)),
            shape((owners // 2 + 1, lines, HEAD_DIM)),
            shape((owners // 2 - 1, lines, HEAD_DIM)),
        ],
        [VMEM] * owners,
        *got,
    )
    hint = call(
        hint_kernel,
        shape((owners, rows // owners, feats), jnp.float32),
        [SMEM] + [VMEM] * (2 + owners),
        layer_index,
        hint_weight,
        hint_gain,
        *got,
        flops=2 * rows * width * feats,
        nbytes=2 * width * feats,
    )
    moved = swap(rest, "blk", half)
    held = gather([own_moved], half // 2, "blk")
    taken = swap(gives, "blk", 1)
    moved, held, taken, hint = lax.optimization_barrier((moved, held, taken, hint))
    moved = gather([moved], half // 2, "blk")
    early = held + gather([pairs], half // 2, "blk") + moved[: len(moved) // 2]
    late = moved[len(moved) // 2 :]
    heads, many = lines // rows, owners * rows
    state = call(
        functools.partial(early_kernel, rows),
        [
            shape((heads, many, HEAD_DIM), jnp.float32),
        ]
        * 3,
        [VMEM] * (2 + len(early)),
        asks,
        taken,
        *early,
        flops=2 * many * sum(array.size for array in early),
        nbytes=2 * sum(array.size for array in early),
    )
    mixed = call(
        functools.partial(late_kernel, rows),
        [shape((lines, HEAD_DIM)), shape((lines, HEAD_DIM), jnp.float32)]
        + [shape((2 * lines, HEAD_DIM))] * (owners // 2 - 1),
        [VMEM] * (5 + len(late)),
        *state,
        asks,
        taken,
        *late,
        flops=2 * many * sum(array.size for array in late),
        nbytes=2 * sum(array.size for array in late),
    )
    kept = [swap_far(array, step) for array, step in zip(mixed[2:], step_pairs(owners))]
    near = swap(mixed[1], "ulysses", 1)
    far = [array for one in kept for array in (one, swap(one, "blk", 1))]
    return call(
        functools.partial(finish_kernel, owners),
        shape((rows, feats)),
        [VMEM] * (3 + len(far)),
        hint.reshape(rows, feats),
        mixed[0],
        near,
        *far,
        out=HBM,
        scratch=[
            pltpu.VMEM((rows, feats), jnp.bfloat16),
            pltpu.SemaphoreType.DMA((2 if rows % 32 == 0 else 1,)),
        ],
    )


def solution(mesh):
    split = P(("groups", "blk", "ulysses"), None)
    return jax.shard_map(
        shards,
        mesh=mesh,
        in_specs=(
            split,
            split,
            split,
            P(),
            P(),
            split,
            P(),
            P(),
            split,
            P(("groups", "blk", "ulysses")),
        ),
        out_specs=split,
        check_vma=False,
    )
```

```python
import functools

import jax
import jax.numpy as jnp
from jax import lax
from jax.experimental import pallas as pl
from jax.experimental.pallas import tpu as pltpu
from jax.sharding import PartitionSpec as P

HEAD_DIM = 128
EPS = 1e-06


def normed(rows, gain):
    values = rows.astype(jnp.float32)
    scale = lax.rsqrt(jnp.mean(values * values, axis=-1, keepdims=True) + EPS)
    return values * scale * gain


def partner(me, step):
    return me ^ step


def steps_in(owners):
    return sorted(range(owners), key=lambda step: (step > 0, -step.bit_length(), step))


def step_pairs(owners):
    return range(2, owners, 2)


def swap(array, axis, step):
    size = lax.axis_size(axis)
    return lax.ppermute(array, axis, [(i, partner(i, step)) for i in range(size)])


def pack_kernel(owners, *refs):
    total = (len(refs) - owners - 3) // 2
    sources, out_refs, own_ref = refs[:total], refs[total : total + owners], refs[total + owners]
    held, (norm_ref, copy_sems) = refs[total + owners + 1 : -2], refs[-2:]
    copies = [
        pltpu.make_async_copy(source, buffer, copy_sems.at[i])
        for i, (source, buffer) in enumerate(zip(sources, held))
    ]
    for copy in copies:
        copy.start()
    owner_ref, control_ref, kg_ref, k_ref, qg_ref, q_ref, v_ref = held
    rows, feats = q_ref.shape
    share = feats // owners
    slab_rows, width = rows // owners, control_ref.shape[1]
    me = lax.axis_index("ulysses")
    copies[0].wait()
    copies[1].wait()
    patches = control_ref[...].astype(jnp.float32)
    slabs = [patches[j * slab_rows : (j + 1) * slab_rows] for j in range(owners)]
    for step, out_ref in zip(steps_in(owners), out_refs):
        to = partner(me, step)
        slab = slabs[0]
        for j in range(1, owners):
            slab = jnp.where(owner_ref[0, j] == to, slabs[j], slab)
        slab = slab.astype(jnp.bfloat16)
        for tile in range(width // HEAD_DIM):
            at = 3 * share // HEAD_DIM * rows + tile * slab_rows
            out_ref[at : at + slab_rows] = slab[:, tile * HEAD_DIM : (tile + 1) * HEAD_DIM]
    copies[2].wait()
    copies[3].wait()
    norm_ref[0] = normed(k_ref[...], kg_ref[...]).astype(jnp.bfloat16)
    copies[4].wait()
    copies[5].wait()
    norm_ref[1] = normed(q_ref[...], qg_ref[...]).astype(jnp.bfloat16)
    copies[6].wait()
    for step, out_ref in zip(steps_in(owners), out_refs):
        to = partner(me, step)
        at = 0
        for i in range(3):
            for head in range(share // HEAD_DIM):
                cols = pl.ds(pl.multiple_of(to * share + head * HEAD_DIM, HEAD_DIM), HEAD_DIM)
                lines = v_ref[:, cols] if i == 1 else norm_ref[i // 2, :, cols]
                out_ref[at : at + rows] = lines
                if step == 0 and i < 2:
                    own_ref[0, at : at + rows] = lines
                at = at + rows


def sort_kernel(*refs):
    got_refs, (pair_ref, rest_ref, ask_ref, give_ref) = refs[:-4], refs[-4:]
    owners = len(got_refs)
    size, lines = pair_ref.shape[1], ask_ref.shape[1]
    asks = {step: ref.at[size : size + lines] for step, ref in zip(steps_in(owners), got_refs)}
    ask_ref[0] = asks[0][...]
    ask_ref[1] = asks[1][...]
    odd = lax.axis_index("blk") & 1
    for side in range(2):

        @pl.when(odd == side)
        def _():
            for i, step in enumerate(step_pairs(owners)):
                ask_ref[2 + i] = asks[step + side][...]
                give_ref[i] = asks[step + 1 - side][...]

    for i, ref in enumerate(got_refs):
        pair_ref[i] = ref[:size]
        if i:
            rest_ref[i - 1] = ref[:size]


def queries_of(ask_ref, taken_ref):
    both = [(ask_ref.at[2 + i], taken_ref.at[i]) for i in range(taken_ref.shape[0])]
    return [ask_ref.at[0], ask_ref.at[1], *(view for pair in both for view in pair)]


def fold(rows, ask_refs, pair_refs, use):
    owners = len(ask_refs)
    heads = pair_refs[0].shape[1] // (2 * rows)
    count = sum(ref.shape[0] for ref in pair_refs) * rows
    group = max(1, min(owners, 2**17 // (rows * count)))
    spans = [slice(i * rows, (i + 1) * rows) for i in range(2 * heads)]
    pieces = [
        jnp.concatenate([ref[:, span].reshape(-1, HEAD_DIM) for ref in pair_refs], axis=0)
        for span in spans
    ]
    ones = jnp.ones((count, HEAD_DIM), jnp.bfloat16)
    values = [jnp.concatenate([piece, ones], axis=1) for piece in pieces[heads:]]
    for first in range(0, owners, group):
        many = min(group, owners - first)
        scores = []
        for head in range(heads):
            queries = [ref[spans[head]] for ref in ask_refs[first : first + many]]
            scores.append(
                lax.dot_general(
                    jnp.concatenate(queries, axis=0),
                    pieces[head],
                    (((1,), (1,)), ((), ())),
                    preferred_element_type=jnp.float32,
                )
            )
        scores = jnp.concatenate(scores, axis=0) * (HEAD_DIM ** (-0.5))
        use(slice(first * rows, (first + many) * rows), scores, values)


def weigh(scores, peak, values):
    probs = jnp.exp(scores - peak).astype(jnp.bfloat16)
    each = probs.shape[0] // len(values)
    mixed = [
        jnp.dot(
            probs[i * each : (i + 1) * each], value, preferred_element_type=jnp.float32
        )
        for i, value in enumerate(values)
    ]
    mixed = jnp.concatenate(mixed, axis=0)
    return mixed[:, HEAD_DIM:], mixed[:, :HEAD_DIM]


def early_kernel(rows, *refs):
    state_refs = refs[-3:]

    def use(at, scores, values):
        peak = jnp.max(scores, axis=-1, keepdims=True)
        totals, mixed = weigh(scores, peak, values)
        each = mixed.shape[0] // len(values)
        for ref, state in zip(state_refs, (jnp.broadcast_to(peak, mixed.shape), totals, mixed)):
            for head in range(len(values)):
                ref[head, at] = state[head * each : (head + 1) * each]

    fold(rows, queries_of(*refs[:2]), refs[2:-3], use)


def late_kernel(rows, *refs):
    state_refs, refs = refs[:3], refs[3:]
    asks = queries_of(*refs[:2])
    outs = refs[0].shape[0]
    out_refs = refs[-outs:]

    def use(at, scores, values):
        heads = range(len(values))
        before, totals, accum = (
            jnp.concatenate([ref[head, at] for head in heads], axis=0) for ref in state_refs
        )
        most = jnp.max(scores, axis=-1, keepdims=True)
        peak = jnp.maximum(before, most)
        correction = jnp.exp(before - peak)
        keys = scores.shape[1]
        new_totals, mixed = weigh(scores, peak[:, : keys if keys < HEAD_DIM else 1], values)
        mixed = (accum * correction + mixed) / (totals * correction + new_totals)
        many = (at.stop - at.start) // rows
        for i in range(len(values) * many):
            head, source = divmod(i, many)
            source = source + at.start // rows
            place, half = (source, 0) if source < 2 else divmod(source + 2, 2)
            start = (half * len(values) + head) * rows
            out_ref = out_refs[place]
            out_ref[start : start + rows] = mixed[i * rows : (i + 1) * rows].astype(out_ref.dtype)

    fold(rows, asks, refs[2:-outs], use)


def hint_kernel(layer_ref, weight_ref, gain_ref, *refs):
    got_refs, out_ref = refs[:-1], refs[-1]
    owners, slab_rows, _ = out_ref.shape
    tiles = weight_ref.shape[0] // HEAD_DIM
    start = got_refs[0].shape[0] - tiles * slab_rows
    slabs = [ref[start:].astype(jnp.float32) for ref in got_refs]
    patches = [
        jnp.concatenate([slab[i * slab_rows : (i + 1) * slab_rows] for slab in slabs], axis=0)
        for i in range(tiles)
    ]
    patches = normed(jnp.concatenate(patches, axis=1), 1.0).astype(jnp.bfloat16)
    hint = jnp.dot(patches, weight_ref[...], preferred_element_type=jnp.float32)
    hint = hint.astype(jnp.bfloat16).astype(jnp.float32) * gain_ref[pl.ds(layer_ref[0], 1), :]
    me = lax.axis_index("ulysses")
    for i, step in enumerate(steps_in(owners)):
        out_ref[partner(me, step)] = hint[i * slab_rows : (i + 1) * slab_rows]


def finish_kernel(owners, hint_ref, own_ref, near_ref, *refs):
    far_refs, out_ref = refs[:-1], refs[-1]
    rows, feats = out_ref.shape
    share = feats // owners
    lines = own_ref.shape[0]
    me, odd = lax.axis_index("ulysses"), lax.axis_index("blk") & 1
    parts = [(0, own_ref, 0), (1, near_ref, 0)]
    for step, kept, crossed in zip(step_pairs(owners), far_refs[::2], far_refs[1::2]):
        parts = parts + [(step + odd, kept, 0), (step + 1 - odd, crossed, lines)]
    for step, ref, first in parts:
        for head in range(share // HEAD_DIM):
            start = partner(me, step) * share + head * HEAD_DIM
            cols = pl.ds(pl.multiple_of(start, HEAD_DIM), HEAD_DIM)
            at = first + head * rows
            attended = ref[at : at + rows].astype(jnp.bfloat16).astype(jnp.float32)
            out_ref[:, cols] = (attended + hint_ref[:, cols]).astype(jnp.bfloat16)


VMEM = pl.BlockSpec(memory_space=pltpu.VMEM)
SMEM = pl.BlockSpec(memory_space=pltpu.SMEM)
HBM = pl.BlockSpec(memory_space=pltpu.HBM)


def call(kernel, out_shape, specs, *operands, scratch=(), flops=0, nbytes=0):
    return pl.pallas_call(
        kernel,
        out_shape=out_shape,
        in_specs=specs,
        out_specs=jax.tree.map(lambda _: VMEM, out_shape),
        scratch_shapes=scratch,
        compiler_params=pltpu.CompilerParams(vmem_limit_bytes=32 * 2**20),
        cost_estimate=pl.CostEstimate(flops=flops, bytes_accessed=nbytes, transcendentals=0),
    )(*operands)


def shape(dims, dtype=jnp.bfloat16):
    return jax.ShapeDtypeStruct(dims, dtype)


def swap_far(array, step):
    blocks, owners = lax.axis_size("blk"), lax.axis_size("ulysses")
    pairs = [
        (block * owners + i, block * owners + partner(i, step + (block & 1)))
        for block in range(blocks)
        for i in range(owners)
    ]
    return lax.ppermute(array, ("blk", "ulysses"), pairs)


def gather(held, step, axis):
    while step:
        held = held + [swap(array, axis, step) for array in held]
        step = step // 2
    return held


def exchange(arrays, steps, axis):
    return [swap(array, axis, step) if step else array for step, array in zip(steps, arrays)]


def shards(
    query_proj,
    key_proj,
    value_proj,
    query_gain,
    key_gain,
    control,
    hint_weight,
    hint_gain,
    owner_map,
    layer_index,
):
    owners = lax.axis_size("ulysses")
    rows, feats = query_proj.shape
    width = control.shape[1]
    lines = rows * (feats // owners // HEAD_DIM)
    slab_lines = rows // owners * (width // HEAD_DIM)
    sources = (
        owner_map,
        control,
        key_gain.reshape(1, feats),
        key_proj,
        query_gain.reshape(1, feats),
        query_proj,
        value_proj,
    )
    sources = [pltpu.with_memory_space_constraint(source, pltpu.HBM) for source in sources]
    sent = call(
        functools.partial(pack_kernel, owners),
        [shape((3 * lines + slab_lines, HEAD_DIM))] * owners + [shape((1, 2 * lines, HEAD_DIM))],
        [HBM] * len(sources),
        *sources,
        scratch=[
            (pltpu.SMEM if source.dtype == jnp.int32 else pltpu.VMEM)(source.shape, source.dtype)
            for source in sources
        ]
        + [
            pltpu.VMEM((2, rows, feats), jnp.bfloat16),
            pltpu.SemaphoreType.DMA((len(sources),)),
        ],
    )
    half = lax.axis_size("blk") // 2
    own_moved = swap(sent[owners], "blk", half)
    got, own_moved = lax.optimization_barrier((exchange(sent[:owners], steps_in(owners), "ulysses"), own_moved))
    pairs, rest, asks, gives = call(
        sort_kernel,
        [
            shape((owners, 2 * lines, HEAD_DIM)),
            shape((owners - 1, 2 * lines, HEAD_DIM)),
            shape((owners // 2 + 1, lines, HEAD_DIM)),
            shape((owners // 2 - 1, lines, HEAD_DIM)),
        ],
        [VMEM] * owners,
        *got,
    )
    hint = call(
        hint_kernel,
        shape((owners, rows // owners, feats), jnp.float32),
        [SMEM] + [VMEM] * (2 + owners),
        layer_index,
        hint_weight,
        hint_gain,
        *got,
        flops=2 * rows * width * feats,
        nbytes=2 * width * feats,
    )
    moved = swap(rest, "blk", half)
    held = gather([own_moved], half // 2, "blk")
    taken = swap(gives, "blk", 1)
    moved, held, taken, hint = lax.optimization_barrier((moved, held, taken, hint))
    moved = gather([moved], half // 2, "blk")
    early = held + gather([pairs], half // 2, "blk") + moved[: len(moved) // 2]
    late = moved[len(moved) // 2 :]
    heads, many = lines // rows, owners * rows
    state = call(
        functools.partial(early_kernel, rows),
        [
            shape((heads, many, HEAD_DIM), jnp.float32),
        ]
        * 3,
        [VMEM] * (2 + len(early)),
        asks,
        taken,
        *early,
        flops=2 * many * sum(array.size for array in early),
        nbytes=2 * sum(array.size for array in early),
    )
    mixed = call(
        functools.partial(late_kernel, rows),
        [shape((lines, HEAD_DIM)), shape((lines, HEAD_DIM), jnp.float32)]
        + [shape((2 * lines, HEAD_DIM))] * (owners // 2 - 1),
        [VMEM] * (5 + len(late)),
        *state,
        asks,
        taken,
        *late,
        flops=2 * many * sum(array.size for array in late),
        nbytes=2 * sum(array.size for array in late),
    )
    kept = [swap_far(array, step) for array, step in zip(mixed[2:], step_pairs(owners))]
    near = swap(mixed[1], "ulysses", 1)
    far = [array for one in kept for array in (one, swap(one, "blk", 1))]
    return call(
        functools.partial(finish_kernel, owners),
        shape((rows, feats)),
        [VMEM] * (3 + len(far)),
        hint.reshape(rows, feats),
        mixed[0],
        near,
        *far,
    )


def solution(mesh):
    split = P(("groups", "blk", "ulysses"), None)
    return jax.shard_map(
        shards,
        mesh=mesh,
        in_specs=(
            split,
            split,
            split,
            P(),
            P(),
            split,
            P(),
            P(),
            split,
            P(("groups", "blk", "ulysses")),
        ),
        out_specs=split,
        check_vma=False,
    )
```
